32 devices in a mesh: tok: 2 (over core), row: 4 (over y, x), col: 4 (over z).
Axes of the slice: x: 2, y: 2, z: 4, core: 2. Of those that a mesh axis runs over, the one named last changes fastest.
Arguments:
- hidden: bfloat16 [1024, 5120], P('tok', ('row', 'col')), may hold values from -6 to 6
- gains: float32 [2, 5120], P('tok', ('row', 'col')), may hold values from 0.25 to 1.75
- weights: bfloat16 [2, 5120, 2048], P('tok', 'row', 'col'), may hold values from -6 to 6
- lengths: int32 [2], replicated, may hold values from 1 to 512, 768 in all
Outputs:
- merged: float32 [5120, 2048], P(('row', 'tok'), 'col')
The draws below stay inside these ranges and needn't reach their ends.
Inputs may be any that keep to these rules, and one draw needn't show every extreme that they name: The largest entry of lengths is exactly 512.
All inputs are finite; a program needn't handle non-finite values.
Results may differ from the reference program's by a relative error of at most 0.0054.
Values may be sent and summed in bfloat16 or wider, within the bound.
No kernel may reach another device: no remote copies, remote signals or barrier semaphores. Data moves between devices by JAX's collectives and lax.ppermute only.
A program may use at most 64 MiB of HBM per device.

```python
import math
import jax
import jax.numpy as jnp
import numpy as np
from jax import lax

D = 5120
OUT = 2048
CAP = 512
ITERS = 4
MODELS = 2
TOKENS = 1024


def block_levels(stream_key, dims, shards, smallest, top_value):
    level, own = 1.0, jax.random.fold_in(stream_key, 6)
    for position, blocks in shards:
        heights = jnp.exp(jax.random.uniform(jax.random.fold_in(own, position), (blocks,), jnp.float32, smallest / len(shards), top_value / len(shards)))
        level = level * jnp.repeat(heights, dims[position] // blocks).reshape([-1 if axis == position else 1 for axis in range(len(dims))])
    return level


def split_up(count, total, limit, lean):
    weights = [(1 << 20) // math.isqrt(rank ** lean) + 1 for rank in range(2, count + 1)]
    rest, given = total - limit - (count - 1), [1] * (count - 1)
    while rest > 0:
        movable = [i for i in range(count - 1) if given[i] < limit]
        mass, left = sum([weights[i] for i in movable]), rest
        for i in movable:
            more = min(limit - given[i], max(1, left * weights[i] // mass), rest)
            given[i] = given[i] + more
            rest = rest - more
    return np.array([limit] + given)


def ragged_sizes(stream_key, count, total, bound, skew):
    if count == 2:
        one = jax.random.randint(stream_key, (), max(1, total - bound), min(bound, total - 1) + 1)
        return jnp.stack([one, total - one])
    sizes = jnp.asarray(split_up(count, total, bound, skew), jnp.int32)
    twos = (count - 1) // 2
    source_of, sink = sizes[1:1 + 2 * twos:2], sizes[2:2 + 2 * twos:2]
    margin = jnp.minimum(source_of - 1, bound - sink)
    shifted = jax.random.randint(jax.random.fold_in(stream_key, 1), (twos,), 0, 1 << 20) % (margin + 1)
    sizes = sizes.at[1:1 + 2 * twos:2].set(source_of - shifted).at[2:2 + 2 * twos:2].set(sink + shifted)
    return sizes[jax.random.permutation(jax.random.fold_in(stream_key, 2), count)]


def centred(key, extent, spread, most, split=(), held_as=jnp.bfloat16):
    drawn = spread * jax.random.normal(key, extent, jnp.float32)
    if split:
        drawn = drawn * block_levels(key, extent, split, -0.22, 0.18)
    return jnp.clip(drawn, -most, most).astype(held_as)


def setup_inputs(seed: int = 0) -> dict:
    key_of = jax.random.split(jax.random.key(seed), 5)
    return {
        "hidden": centred(key_of[0], (TOKENS, D), 1.0, 6.0, ((0, 2), (1, 16))),
        "gains": jnp.clip(1.0 + 0.15 * jax.random.normal(key_of[1], (MODELS, D), jnp.float32), 0.25, 1.75),
        "weights": centred(key_of[2], (MODELS, D, OUT), 1.0, 6.0, ((0, 2), (1, 4), (2, 4))),
        "lengths": ragged_sizes(key_of[3], MODELS, (MODELS + 1) * CAP // 2, CAP, 2).astype(jnp.int32),
    }


MIXING = 0.9
EPSILON = 1e-06

def reference(hidden, gains, weights, lengths):
    positions = jnp.arange(CAP, dtype=jnp.int32)
    tokens_all = hidden.astype(jnp.float32).reshape(MODELS, CAP, D)
    inverse_rms = lax.rsqrt(lax.optimization_barrier(jnp.sum(tokens_all * tokens_all, axis=2)) / D + EPSILON)
    live_mask = (positions[None, :] < lengths[:, None]).astype(jnp.float32)
    normed = (tokens_all * (inverse_rms * live_mask)[:, :, None] * gains[:, None, :]).astype(jnp.bfloat16)
    gram = jnp.zeros((D, D), jnp.float32)
    right = jnp.zeros((D, OUT), jnp.float32)
    for model in range(MODELS):
        block_model = normed[model]
        gram = gram + jnp.dot(block_model.T, block_model, preferred_element_type=jnp.float32)
        outputs = jnp.dot(block_model, weights[model], preferred_element_type=jnp.float32).astype(jnp.bfloat16)
        squared = lax.optimization_barrier(jnp.sum(jnp.square(block_model.astype(jnp.float32)), axis=0))
        cross_term = jnp.dot(block_model.T, outputs, preferred_element_type=jnp.float32)
        right = right + (MIXING * cross_term + (1.0 - MIXING) * squared[:, None] * weights[model].astype(jnp.float32))
    diagonal = jnp.diagonal(gram)

    def operate(direction):
        product = jnp.dot(gram, direction, precision=lax.Precision.HIGHEST)
        return MIXING * product + (1.0 - MIXING) * diagonal[:, None] * direction
    merged = jnp.zeros((D, OUT), jnp.float32)
    residual = right
    direction = right
    norm_now = lax.optimization_barrier(jnp.sum(residual * residual, axis=0))
    for step in range(ITERS):
        image = operate(direction)
        step_size = norm_now / lax.optimization_barrier(jnp.sum(direction * image, axis=0))
        merged = merged + step_size[None, :] * direction
        residual = residual - step_size[None, :] * image
        norm_next = lax.optimization_barrier(jnp.sum(residual * residual, axis=0))
        direction = residual + (norm_next / norm_now)[None, :] * direction
        norm_now = norm_next
    return merged
```

```python
import functools

import jax
import jax.numpy as jnp
from jax import lax
from jax.experimental import pallas as pl
from jax.experimental.pallas import tpu as pltpu
from jax.sharding import PartitionSpec as P

ITERS = 4

MIXING = 0.9
EPSILON = 1e-06

LANES = 128
CHUNK = 512
MOST_TOKENS = 1024
TABLE_OUT = 0


def two_terms(value):
    high = value.astype(jnp.bfloat16).astype(jnp.float32)
    return jnp.concatenate([high, value - high], axis=0).astype(jnp.bfloat16)


def over_features(left, tokens, found):
    slots = tokens.shape[1]
    if slots <= MOST_TOKENS:
        found[...] = jnp.dot(left[...], tokens[...], preferred_element_type=jnp.float32)
        return

    def some(step, carry):
        lanes = pl.ds(pl.multiple_of(step * CHUNK, CHUNK), CHUNK)
        found[:, lanes] = jnp.dot(left[...], tokens[:, lanes], preferred_element_type=jnp.float32)
        return carry

    lax.fori_loop(0, slots // CHUNK, some, 0)


def over_tokens(left, tokens, part):
    slots = tokens.shape[1]
    product = functools.partial(
        lax.dot_general, dimension_numbers=(((1,), (1,)), ((), ())), preferred_element_type=jnp.float32
    )
    if slots <= MOST_TOKENS:
        return product(left[...], tokens[part, :])

    def some(step, total):
        lanes = pl.ds(pl.multiple_of(step * CHUNK, CHUNK), CHUNK)
        return total + product(left[:, lanes], tokens[part, lanes])

    return lax.fori_loop(0, slots // CHUNK, some, jnp.zeros((left.shape[0], CHUNK), jnp.float32))


def solve_kernel(owners, models, block, copies, places, table_ref, live_ref, owner_ref, squares_ref, gains_ref, *refs):
    pieces = refs[:len(copies)]
    weight_pieces = refs[len(copies):len(copies) + len(places)]
    out_refs = refs[len(copies) + len(places):-12]
    tokens, weights, squared, diagonal, residual, direction, merged, terms, values, outputs, seen, sems = refs[-12:]
    width, slots = tokens.shape
    columns = residual.shape[0]
    started = []
    for piece, parts in zip(pieces, copies):
        for source, entry, part, lanes in parts:
            start = pl.multiple_of(table_ref[entry] * block, 16)
            lane = pl.multiple_of(table_ref[part] * lanes, LANES)
            copy = pltpu.make_async_copy(
                piece.at[source],
                tokens.at[pl.ds(start, block), pl.ds(lane, lanes)],
                sems.at[0],
            )
            copy.start()
            started.append(copy)
    for piece, (entry, part) in zip(weight_pieces, places):
        held, row_width = piece.shape
        lane = pl.multiple_of(table_ref[entry] * row_width, LANES)
        row = pl.multiple_of(table_ref[part] * held, held)
        copy = pltpu.make_async_copy(
            piece, weights.at[pl.ds(row, held), pl.ds(lane, row_width)], sems.at[1]
        )
        copy.start()
        started.append(copy)
    for copy in started:
        copy.wait()

    inverse_rms = lax.rsqrt(squares_ref[...] / width + EPSILON) * live_ref[...]

    def norm_rows(step, carry):
        start = pl.multiple_of(step * LANES, LANES)
        gains = gains_ref[pl.ds(start, LANES), :]
        sums = [jnp.zeros((LANES, LANES), jnp.float32) for _ in range(models)]
        for tile, owner in enumerate(owners):
            lanes = slice(tile * LANES, (tile + 1) * LANES)
            value = tokens[pl.ds(start, LANES), lanes].astype(jnp.float32)
            if owner < 0:
                gain = jnp.where(owner_ref[:, lanes] > 0, gains[:, 1:2], gains[:, 0:1])
            else:
                gain = gains[:, owner:owner + 1]
            normed = (value * inverse_rms[:, lanes] * gain).astype(jnp.bfloat16)
            tokens[pl.ds(start, LANES), lanes] = normed
            value = normed.astype(jnp.float32)
            value = value * value
            if owner < 0:
                theirs = value * owner_ref[:, lanes]
                sums[0] = sums[0] + (value - theirs)
                sums[1] = sums[1] + theirs
            else:
                sums[owner] = sums[owner] + value
        sums = [jnp.sum(part.T, axis=0, keepdims=True) for part in sums]
        for model in range(models):
            squared[model:model + 1, pl.ds(start, LANES)] = sums[model]
        diagonal[:, pl.ds(start, LANES)] = functools.reduce(jnp.add, sums)
        return carry

    lax.fori_loop(0, width // LANES, norm_rows, 0)

    over_features(weights, tokens, values)
    picked = []
    for tile, owner in enumerate(owners):
        lanes = slice(tile * LANES, (tile + 1) * LANES)
        if owner < 0:
            picked.append(jnp.where(owner_ref[:, lanes] > 0, values[columns:2 * columns, lanes], values[:columns, lanes]))
        else:
            picked.append(values[owner * columns:(owner + 1) * columns, lanes])
    outputs[...] = jnp.concatenate(picked, axis=1).astype(jnp.bfloat16)

    norm_now = jnp.zeros((columns, 1), jnp.float32)
    for start in range(0, width, CHUNK):
        part = slice(start, start + CHUNK)
        weighted = jnp.zeros((columns, CHUNK), jnp.float32)
        for model in range(models):
            rows = weights[model * columns:(model + 1) * columns, part].astype(jnp.float32)
            weighted = weighted + squared[model:model + 1, part] * rows
        right = MIXING * over_tokens(outputs, tokens, part) + (1.0 - MIXING) * weighted
        residual[:, part] = right
        direction[:, part] = jnp.zeros_like(right)
        merged[:, part] = jnp.zeros_like(right)
        norm_now = norm_now + jnp.sum(right * right, axis=1, keepdims=True)

    def step_of(scale, norm_now):
        weighted = jnp.zeros((columns, 1), jnp.float32)
        for start in range(0, width, CHUNK):
            part = slice(start, start + CHUNK)
            value = residual[:, part] + scale * direction[:, part]
            direction[:, part] = value
            terms[:, part] = two_terms(value)
            weighted = weighted + jnp.sum(diagonal[:, part] * value * value, axis=1, keepdims=True)
        both = values.at[:2 * columns]
        over_features(terms, tokens, both)
        both = both[:columns] + both[columns:]
        seen[...] = two_terms(both)
        curvature = MIXING * jnp.sum(both * both, axis=1, keepdims=True) + (1.0 - MIXING) * weighted
        return norm_now / curvature

    def iterate(_, carry):
        scale, norm_now = carry
        step_size = step_of(scale, norm_now)
        norm_next = jnp.zeros((columns, 1), jnp.float32)
        for start in range(0, width, CHUNK):
            part = slice(start, start + CHUNK)
            both = over_tokens(seen, tokens, part)
            along = direction[:, part]
            image = MIXING * (both[:columns] + both[columns:]) + (1.0 - MIXING) * diagonal[:, part] * along
            merged[:, part] = merged[:, part] + step_size * along
            value = residual[:, part] - step_size * image
            residual[:, part] = value
            norm_next = norm_next + jnp.sum(value * value, axis=1, keepdims=True)
        return norm_next / norm_now, norm_next

    scale, norm_now = lax.fori_loop(0, ITERS - 1, iterate, (jnp.zeros((columns, 1), jnp.float32), norm_now))
    step_size = step_of(scale, norm_now)
    merged[...] = merged[...] + step_size * direction[...]
    for number, out_ref in enumerate(out_refs):
        sub_rows = out_ref.shape[1]
        if len(out_refs) > 1:
            start = pl.multiple_of(table_ref[TABLE_OUT + number] * sub_rows, LANES)
            out_ref[...] = merged[:, pl.ds(start, sub_rows)].astype(out_ref.dtype)
        else:
            out_ref[...] = merged[...].astype(out_ref.dtype)


def place_kernel(table_ref, *refs):
    pieces, out_ref, sem = refs[:-2], refs[-2], refs[-1]
    started = []
    for number, piece in enumerate(pieces):
        copy = pltpu.make_async_copy(piece, out_ref.at[table_ref[number]], sem.at[0])
        copy.start()
        started.append(copy)
    for copy in started:
        copy.wait()


def pick_kernel(table_ref, whole_ref, *refs):
    sem = refs[-1]
    started = []
    for number, out_ref in enumerate(refs[:-1]):
        copy = pltpu.make_async_copy(whole_ref.at[table_ref[number]], out_ref, sem.at[0])
        copy.start()
        started.append(copy)
    for copy in started:
        copy.wait()


def body(hidden, gains, weights, lengths):
    rows = lax.axis_size("row")
    cols = lax.axis_size("col")
    toks = lax.axis_size("tok")
    row, col, tok = lax.axis_index("row"), lax.axis_index("col"), lax.axis_index("tok")
    slots, block = hidden.shape
    width = block * rows * cols
    models = toks * gains.shape[0]
    row_width, col_width = weights.shape[1:]
    columns = col_width // (rows * toks)
    sub_rows = row_width // toks
    features = hidden.T
    positions = jnp.arange(slots, dtype=jnp.int32)
    paired = toks == 2 and rows == 4
    any_space = pl.BlockSpec(memory_space=pl.ANY)
    scalars = pl.BlockSpec(memory_space=pltpu.SMEM)
    in_vmem = pl.BlockSpec(memory_space=pltpu.VMEM)
    dma = [pltpu.SemaphoreType.DMA((1,))]

    def swap(value, flip):
        pairs = [
            (t * rows + r, (t ^ flip % 2) * rows + (r ^ flip // 2)) for t in range(toks) for r in range(rows)
        ]
        return lax.ppermute(value, ("tok", "row"), pairs)

    sent = weights[0].T.reshape(rows * toks, columns, row_width)
    if paired:
        near_first = (0, 2, 4, 6, 3, 5, 7, 1)
        partners = jnp.stack([(row * toks + tok) ^ flip for flip in near_first]).astype(jnp.int32)
        picked = pl.pallas_call(
            pick_kernel,
            out_shape=[jax.ShapeDtypeStruct((columns, row_width), jnp.bfloat16)] * len(near_first),
            in_specs=[scalars, any_space],
            out_specs=[any_space] * len(near_first),
            scratch_shapes=dma,
        )(partners, sent)
        weight_pieces = [picked[0]] + [swap(x, flip) for x, flip in zip(picked[1:], near_first[1:])]

        half, quarter = slots // 2, slots // 4
        held = half + quarter
        lower, upper = features[:, half:held], features[:, held:]
        given = swap(upper, 1)
        mirror = jnp.eye(quarter, dtype=jnp.bfloat16)[::-1]
        turned = jnp.dot(jnp.where(tok == 0, given, lower), mirror, preferred_element_type=jnp.float32)
        place = jnp.arange(half, dtype=jnp.int32)
        of_second = place >= lengths[0] - half
        ours = lax.dynamic_slice(of_second, (tok * quarter,), (quarter,))
        mixed = jnp.where(ours[None, :], turned.astype(jnp.bfloat16), jnp.where(tok == 0, lower, given))
        piece = jnp.concatenate([features[:, :half], mixed], axis=1)
        line = [piece]
        for shift in range(1, cols):
            line.append(lax.ppermute(piece, "col", [(i, (i + shift) % cols) for i in range(cols)]))
        table = list(partners) + [tok, 1 - tok, row] + [row ^ 1, row ^ 2, row ^ 3]
        origin = {}
        mine, homes = [], []
        for back in range(cols):
            by_near, by_far = swap(line[back], 2), swap(line[back], 4)
            across = swap(by_far, 2) if back % 2 == 0 else swap(by_near, 4)
            for flip, value in enumerate((line[back], by_near, by_far, across)):
                mine.append(value)
                homes.append(len(table))
                table.append((row ^ flip) * cols + (col - back + cols) % cols)
        theirs = [swap(value, 1) for value in mine]
        pieces = [value[None] for value in mine + theirs]
        base = len(partners)
        copies = [[(0, home, base, held)] for home in homes] + [[(0, home, base + 1, held)] for home in homes]
        places = []
        for flip in near_first:
            places.append((base + 2 + flip // 2, base + flip % 2))
        owners = (0, 0, -1, 1, 1, -1)
        late = jnp.where(of_second, slots - 1 - place < lengths[1], half + place < lengths[0])
        live = jnp.concatenate([
            positions[:half] < lengths[0], late[:quarter], positions[:half] < lengths[1], late[quarter:]
        ])
        lane_owner = jnp.concatenate([
            jnp.zeros(half, bool), of_second[:quarter], jnp.ones(half, bool), of_second[quarter:]
        ])
    else:
        own_weights = lax.all_to_all(sent, ("row", "tok"), 0, 0, tiled=True)
        own_weights = own_weights.reshape(rows, models * columns, row_width)
        weight_pieces = [own_weights.transpose(1, 0, 2).reshape(models * columns, width)]
        places = [(0, 0)]
        piece, held = features, slots
        everything = lax.all_gather(features, ("row", "col"), axis=0, tiled=False)
        pieces = [lax.all_gather(everything, "tok", axis=0, tiled=True)]
        tiles = slots // LANES
        owners = tuple(m for m in range(models) for _ in range(tiles))
        table = list(range(max(models, rows * cols)))
        copies = [[
            (m * rows * cols + b, b, m, slots) for m in range(models) for b in range(rows * cols)
        ]]
        live = (positions[None, :] < lengths[:, None]).reshape(-1)
        lane_owner = jnp.zeros(models * slots, bool)
    slots_held = toks * held

    floats = piece.astype(jnp.float32)
    squares = jnp.sum(floats * floats, axis=0)
    spread = lax.dynamic_update_slice(
        jnp.zeros((rows * cols, block), jnp.float32), gains, (row * cols + col, 0)
    ).reshape(width)
    shared = lax.dynamic_update_slice(
        jnp.zeros((toks, held + width), jnp.float32), jnp.concatenate([squares, spread])[None], (tok, 0)
    )
    shared = lax.psum(shared, ("tok", "row", "col"))
    every_gain = shared[:, held:].T
    squares = shared[:, :held].reshape(1, slots_held)

    if paired:
        out_shape = [jax.ShapeDtypeStruct((columns, sub_rows), jnp.bfloat16)] * (rows * toks)
    else:
        out_shape = [jax.ShapeDtypeStruct((columns, width), jnp.bfloat16)]
    found = pl.pallas_call(
        functools.partial(solve_kernel, owners, models, block, copies, places),
        out_shape=out_shape,
        in_specs=[scalars] + [in_vmem] * 4 + [any_space] * (len(pieces) + len(weight_pieces)),
        out_specs=[in_vmem] * len(out_shape),
        scratch_shapes=[
            pltpu.VMEM((width, slots_held), jnp.bfloat16),
            pltpu.VMEM((models * columns, width), jnp.bfloat16),
            pltpu.VMEM((models, width), jnp.float32),
            pltpu.VMEM((1, width), jnp.float32),
            pltpu.VMEM((columns, width), jnp.float32),
            pltpu.VMEM((columns, width), jnp.float32),
            pltpu.VMEM((columns, width), jnp.float32),
            pltpu.VMEM((2 * columns, width), jnp.bfloat16),
            pltpu.VMEM((max(models, 2) * columns, slots_held), jnp.float32),
            pltpu.VMEM((columns, slots_held), jnp.bfloat16),
            pltpu.VMEM((2 * columns, slots_held), jnp.bfloat16),
            pltpu.SemaphoreType.DMA((2,)),
        ],
        compiler_params=pltpu.CompilerParams(vmem_limit_bytes=width * slots_held * 2 + (18 << 20)),
    )(
        jnp.stack([jnp.asarray(x, jnp.int32) for x in table]),
        live.astype(jnp.float32)[None, :],
        lane_owner.astype(jnp.float32)[None, :],
        squares,
        every_gain,
        *pieces,
        *weight_pieces,
    )
    if paired:
        arrived = [found[0]] + [swap(x, flip) for x, flip in zip(found[1:], near_first[1:])]
        back = pl.pallas_call(
            place_kernel,
            out_shape=jax.ShapeDtypeStruct((rows * toks, columns, sub_rows), jnp.bfloat16),
            in_specs=[scalars] + [any_space] * len(arrived),
            out_specs=any_space,
            scratch_shapes=dma,
        )(partners, *arrived)
    else:
        found = found[0].reshape(columns, rows * toks, sub_rows).transpose(1, 0, 2)
        back = lax.all_to_all(found, ("row", "tok"), 0, 0, tiled=True)
    return back.reshape(col_width, sub_rows).T.astype(jnp.float32)


def solution(mesh):
    return jax.shard_map(
        body,
        mesh=mesh,
        in_specs=(P("tok", ("row", "col")), P("tok", ("row", "col")), P("tok", "row", "col"), P()),
        out_specs=P(("row", "tok"), "col"),
        check_vma=False,
    )
```

```python
import functools

import jax
import jax.numpy as jnp
from jax import lax
from jax.experimental import pallas as pl
from jax.experimental.pallas import tpu as pltpu
from jax.sharding import PartitionSpec as P

ITERS = 4

MIXING = 0.9
EPSILON = 1e-06

LANES = 128
CHUNK = 512
MOST_TOKENS = 1024
NEAR_FIRST = (0, 2, 4, 6, 3, 5, 7, 1)


def two_terms(value):
    high = value.astype(jnp.bfloat16).astype(jnp.float32)
    return jnp.concatenate([high, value - high], axis=0).astype(jnp.bfloat16)


def over_features(left, tokens, found):
    slots = tokens.shape[1]
    if slots <= MOST_TOKENS:
        found[...] = jnp.dot(left[...], tokens[...], preferred_element_type=jnp.float32)
        return

    def some(step, carry):
        lanes = pl.ds(pl.multiple_of(step * CHUNK, CHUNK), CHUNK)
        found[:, lanes] = jnp.dot(left[...], tokens[:, lanes], preferred_element_type=jnp.float32)
        return carry

    lax.fori_loop(0, slots // CHUNK, some, 0)


def over_tokens(left, tokens, part):
    slots = tokens.shape[1]
    product = functools.partial(
        lax.dot_general, dimension_numbers=(((1,), (1,)), ((), ())), preferred_element_type=jnp.float32
    )
    if slots <= MOST_TOKENS:
        return product(left[...], tokens[part, :])

    def some(step, total):
        lanes = pl.ds(pl.multiple_of(step * CHUNK, CHUNK), CHUNK)
        return total + product(left[:, lanes], tokens[part, lanes])

    return lax.fori_loop(0, slots // CHUNK, some, jnp.zeros((left.shape[0], CHUNK), jnp.float32))


def in_pair_order(lengths_ref, width):
    half, quarter = width // 3, width // 6
    lane = lax.broadcasted_iota(jnp.int32, (1, width), 1)
    part = jnp.where(lane >= width // 2, 1, 0)
    spot = lane - part * (width // 2)
    place = spot - half + part * quarter
    late = spot >= half
    second = jnp.where(late, jnp.where(place >= lengths_ref[0] - half, 1, 0), part)
    position = jnp.where(late, jnp.where(second == 1, 2 * half - 1 - place, half + place), spot)
    length = jnp.where(second == 1, lengths_ref[1], lengths_ref[0])
    return jnp.where(position < length, 1.0, 0.0), second.astype(jnp.float32)


def solve_kernel(owners, models, block, copies, places, lengths_ref, *refs):
    riding = len(copies) > 1
    if not riding:
        live_ref, squares_ref, gains_ref, refs = refs[0], refs[1], refs[2], refs[3:]
    pieces = refs[:len(copies)]
    weight_pieces = refs[len(copies):len(copies) + len(places)]
    out_refs = refs[len(copies) + len(places):-14]
    (tokens, weights, squared, diagonal, residual, direction, merged, terms, values, outputs, seen, extras, gains_held,
     sems) = refs[-14:]
    width, slots = tokens.shape
    columns = residual.shape[0]
    blocks = width // block
    started = []
    if riding:
        row, col, tok = lax.axis_index("row"), lax.axis_index("col"), lax.axis_index("tok")
        cols = lax.axis_size("col")
        row_devices = lax.axis_size("row")
    for piece, parts in zip(pieces, copies):
        for source, entry, part, lanes, first, held in parts:
            if riding:
                flip, back = entry
                entry = (row ^ flip) * cols + lax.rem(col - back + cols, cols)
                part = tok ^ part
            start = pl.multiple_of(entry * block + first, 16)
            lane = pl.multiple_of(part * lanes, LANES)
            copy = pltpu.make_async_copy(
                piece.at[source, pl.ds(0, held)],
                tokens.at[pl.ds(start, held), pl.ds(lane, lanes)],
                sems.at[0],
            )
            copy.start()
            started.append(copy)
            if piece.shape[1] > held:
                copy = pltpu.make_async_copy(
                    piece.at[source, pl.ds(held, 16)],
                    extras.at[part * blocks + entry],
                    sems.at[0],
                )
                copy.start()
                started.append(copy)
    for piece, place in zip(weight_pieces, places):
        moves = [(piece, weights)]
        if riding:
            row_width = piece.shape[1]
            lane = pl.multiple_of((row ^ place) * row_width, LANES)
            moves = [
                (
                    piece.at[pl.ds(part * columns, columns)],
                    weights.at[pl.ds(pl.multiple_of((tok ^ part) * columns, columns), columns), pl.ds(lane, row_width)],
                )
                for part in range(2)
            ]
        for source, target in moves:
            copy = pltpu.make_async_copy(source, target, sems.at[1])
            copy.start()
            started.append(copy)
    for copy in started:
        copy.wait()

    if riding:
        every = extras[...].astype(jnp.float32)
        sums = [jnp.sum(every[part * blocks:(part + 1) * blocks], axis=0) for part in range(models)]
        squares = jnp.concatenate([x[0:1] + x[1:2] + x[2:3] for x in sums], axis=1)
        turned = (every[:, 3] + every[:, 4] + every[:, 5]).T[:block]
        lane = lax.broadcasted_iota(jnp.int32, turned.shape, 1)
        side = lax.broadcasted_iota(jnp.int32, (block, LANES), 1)

        def hold_gains(step, carry):
            gain = [
                jnp.sum(jnp.where(lane == part * blocks + step, turned, 0.0), axis=1, keepdims=True)
                for part in range(models)
            ]
            gains_held[pl.ds(pl.multiple_of(step * block, block), block), :] = jnp.where(side == 0, gain[0], gain[1])
            return carry

        lax.fori_loop(0, blocks, hold_gains, 0)
        gains_ref = gains_held
        live, second = in_pair_order(lengths_ref, slots)
    else:
        squares, live = squares_ref[...], live_ref[...]
    inverse_rms = lax.rsqrt(squares / width + EPSILON) * live

    def norm_rows(step, carry):
        start = pl.multiple_of(step * LANES, LANES)
        gains = gains_ref[pl.ds(start, LANES), :]
        sums = [jnp.zeros((LANES, LANES), jnp.float32) for _ in range(models)]
        for tile, owner in enumerate(owners):
            lanes = slice(tile * LANES, (tile + 1) * LANES)
            value = tokens[pl.ds(start, LANES), lanes].astype(jnp.float32)
            if owner < 0:
                gain = jnp.where(second[:, lanes] > 0, gains[:, 1:2], gains[:, 0:1])
            else:
                gain = gains[:, owner:owner + 1]
            normed = (value * inverse_rms[:, lanes] * gain).astype(jnp.bfloat16)
            tokens[pl.ds(start, LANES), lanes] = normed
            value = normed.astype(jnp.float32)
            value = value * value
            if owner < 0:
                theirs = value * second[:, lanes]
                sums[0] = sums[0] + (value - theirs)
                sums[1] = sums[1] + theirs
            else:
                sums[owner] = sums[owner] + value
        sums = [jnp.sum(part.T, axis=0, keepdims=True) for part in sums]
        for model in range(models):
            squared[model:model + 1, pl.ds(start, LANES)] = sums[model]
        diagonal[:, pl.ds(start, LANES)] = functools.reduce(jnp.add, sums)
        return carry

    lax.fori_loop(0, width // LANES, norm_rows, 0, unroll=4 if riding else 1)

    over_features(weights, tokens, values)
    picked = []
    for tile, owner in enumerate(owners):
        lanes = slice(tile * LANES, (tile + 1) * LANES)
        if owner < 0:
            picked.append(jnp.where(second[:, lanes] > 0, values[columns:2 * columns, lanes], values[:columns, lanes]))
        else:
            picked.append(values[owner * columns:(owner + 1) * columns, lanes])
    outputs[...] = jnp.concatenate(picked, axis=1).astype(jnp.bfloat16)

    norm_now = jnp.zeros((columns, 1), jnp.float32)
    for start in range(0, width, CHUNK):
        part = slice(start, start + CHUNK)
        weighted = jnp.zeros((columns, CHUNK), jnp.float32)
        for model in range(models):
            rows = weights[model * columns:(model + 1) * columns, part].astype(jnp.float32)
            weighted = weighted + squared[model:model + 1, part] * rows
        right = MIXING * over_tokens(outputs, tokens, part) + (1.0 - MIXING) * weighted
        residual[:, part] = right
        direction[:, part] = jnp.zeros_like(right)
        merged[:, part] = jnp.zeros_like(right)
        norm_now = norm_now + jnp.sum(right * right, axis=1, keepdims=True)

    def step_of(scale, norm_now):
        weighted = jnp.zeros((columns, 1), jnp.float32)
        for start in range(0, width, CHUNK):
            part = slice(start, start + CHUNK)
            value = residual[:, part] + scale * direction[:, part]
            direction[:, part] = value
            terms[:, part] = two_terms(value)
            weighted = weighted + jnp.sum(diagonal[:, part] * value * value, axis=1, keepdims=True)
        both = values.at[:2 * columns]
        over_features(terms, tokens, both)
        both = both[:columns] + both[columns:]
        seen[...] = two_terms(both)
        curvature = MIXING * jnp.sum(both * both, axis=1, keepdims=True) + (1.0 - MIXING) * weighted
        return norm_now / curvature

    def iterate(_, carry):
        scale, norm_now = carry
        step_size = step_of(scale, norm_now)
        norm_next = jnp.zeros((columns, 1), jnp.float32)
        for start in range(0, width, CHUNK):
            part = slice(start, start + CHUNK)
            both = over_tokens(seen, tokens, part)
            along = direction[:, part]
            image = MIXING * (both[:columns] + both[columns:]) + (1.0 - MIXING) * diagonal[:, part] * along
            merged[:, part] = merged[:, part] + step_size * along
            value = residual[:, part] - step_size * image
            residual[:, part] = value
            norm_next = norm_next + jnp.sum(value * value, axis=1, keepdims=True)
        return norm_next / norm_now, norm_next

    scale, norm_now = lax.fori_loop(0, ITERS - 1, iterate, (jnp.zeros((columns, 1), jnp.float32), norm_now))
    step_size = step_of(scale, norm_now)
    merged[...] = merged[...] + step_size * direction[...]
    for number, out_ref in enumerate(out_refs):
        sub_rows = out_ref.shape[1]
        if len(out_refs) > 1:
            flip = NEAR_FIRST[number]
            sub_block = (row ^ flip // 2) * 2 + (tok ^ flip % 2)
            start = pl.multiple_of(sub_block * sub_rows, LANES)
            out_ref[...] = merged[:, pl.ds(start, sub_rows)].astype(out_ref.dtype)
        else:
            out_ref[...] = merged[...].astype(out_ref.dtype)


def three_terms(value):
    high = value.astype(jnp.bfloat16).astype(jnp.float32)
    rest = value - high
    middle = rest.astype(jnp.bfloat16).astype(jnp.float32)
    return [high, middle, rest - middle]


def piece_kernel(lengths_ref, features_ref, given_ref, gains_ref, upper_ref, lower_ref, extra):
    block, slots = features_ref.shape
    half, quarter = slots // 2, slots // 4
    tok = lax.axis_index("tok")
    first = tok == 0
    lower = features_ref[:, half:half + quarter].astype(jnp.float32)
    given = given_ref[...].astype(jnp.float32)
    row = lax.broadcasted_iota(jnp.int32, (quarter, quarter), 0)
    lane = lax.broadcasted_iota(jnp.int32, (quarter, quarter), 1)
    mirror = jnp.where(row + lane == quarter - 1, 1.0, 0.0).astype(jnp.bfloat16)
    turned = jnp.dot(
        jnp.where(first, given, lower).astype(jnp.bfloat16), mirror, preferred_element_type=jnp.float32
    )
    place = lax.broadcasted_iota(jnp.int32, (block, quarter), 1) + tok * quarter
    mixed = jnp.where(place >= lengths_ref[0] - half, turned, jnp.where(first, lower, given))
    kept = features_ref[:, :half]
    cut = lower_ref.shape[0]
    upper_ref[:cut, :half] = kept[:cut]
    upper_ref[:cut, half:] = mixed[:cut].astype(jnp.bfloat16)
    lower_ref[:, :half] = kept[cut:]
    lower_ref[:, half:] = mixed[cut:].astype(jnp.bfloat16)
    kept = kept.astype(jnp.float32)
    extra[...] = jnp.zeros_like(extra)
    for number, value in enumerate(three_terms(jnp.sum(kept * kept, axis=0, keepdims=True))):
        extra[number:number + 1, :half] = value
    for number, value in enumerate(three_terms(jnp.sum(mixed * mixed, axis=0, keepdims=True))):
        extra[number:number + 1, half:] = value
    for number, value in enumerate(three_terms(gains_ref[...])):
        extra[3 + number:4 + number, :block] = value
    upper_ref[cut:, :] = extra[...].astype(jnp.bfloat16)


def send_kernel(weights_ref, own_ref, other_ref, turned):
    row, tok = lax.axis_index("row"), lax.axis_index("tok")
    for start in range(0, weights_ref.shape[1], LANES):
        value = weights_ref[:, start:start + LANES].astype(jnp.float32)
        turned[start:start + LANES, :] = value.T.astype(jnp.bfloat16)
    rows, held, _ = own_ref.shape
    for flip in range(rows):
        for out_ref, core in ((own_ref, tok), (other_ref, 1 - tok)):
            start = pl.multiple_of(((row ^ flip) * 2 + core) * held, held)
            out_ref[flip] = turned[pl.ds(start, held), :]


def join_kernel(own_ref, given_ref, *refs):
    for flip, out_ref in enumerate(refs):
        held = own_ref.shape[1]
        out_ref[:held] = own_ref[flip]
        out_ref[held:] = given_ref[flip]


def gather_kernel(*refs):
    out_ref, ordered = refs[-2:]
    row, tok = lax.axis_index("row"), lax.axis_index("tok")
    for flip, piece in zip(NEAR_FIRST, refs[:-2]):
        held = piece.shape[0]
        start = pl.multiple_of(((row ^ flip // 2) * 2 + (tok ^ flip % 2)) * held, held)
        ordered[pl.ds(start, held), :] = piece[...].astype(jnp.float32)
    for start in range(0, out_ref.shape[1], LANES):
        out_ref[:, start:start + LANES] = ordered[start:start + LANES, :].T


def body(hidden, gains, weights, lengths):
    rows = lax.axis_size("row")
    cols = lax.axis_size("col")
    toks = lax.axis_size("tok")
    slots, block = hidden.shape
    width = block * rows * cols
    models = toks * gains.shape[0]
    row_width, col_width = weights.shape[1:]
    columns = col_width // (rows * toks)
    sub_rows = row_width // toks
    features = hidden.T
    paired = toks == 2 and rows == 4
    any_space = pl.BlockSpec(memory_space=pl.ANY)
    small = pltpu.CompilerParams(vmem_limit_bytes=10 << 20)
    scalars = pl.BlockSpec(memory_space=pltpu.SMEM)
    in_vmem = pl.BlockSpec(memory_space=pltpu.VMEM)

    def swap(value, flip):
        pairs = [
            (t * rows + r, (t ^ flip % 2) * rows + (r ^ flip // 2)) for t in range(toks) for r in range(rows)
        ]
        return lax.ppermute(value, ("tok", "row"), pairs)

    if paired:
        half, quarter = slots // 2, slots // 4
        held = half + quarter
        given = swap(features[:, held:], 1)
        own, other = pl.pallas_call(
            send_kernel,
            out_shape=[jax.ShapeDtypeStruct((rows, columns, row_width), jnp.bfloat16)] * 2,
            in_specs=[in_vmem],
            out_specs=[in_vmem] * 2,
            scratch_shapes=[pltpu.VMEM((col_width, row_width), jnp.bfloat16)],
            compiler_params=small,
        )(weights[0])
        joined = pl.pallas_call(
            join_kernel,
            out_shape=[jax.ShapeDtypeStruct((toks * columns, row_width), jnp.bfloat16)] * rows,
            in_specs=[in_vmem] * 2,
            out_specs=[in_vmem] * rows,
            compiler_params=small,
        )(own, swap(other, 1))
        weight_pieces = [swap(value, 2 * flip) if flip else value for flip, value in enumerate(joined)]
        places = list(range(rows))
        cut = block // 2
        upper, lower = pl.pallas_call(
            piece_kernel,
            out_shape=[
                jax.ShapeDtypeStruct((cut + 16, held), jnp.bfloat16), jax.ShapeDtypeStruct((cut, held), jnp.bfloat16)
            ],
            in_specs=[scalars, in_vmem, in_vmem, in_vmem],
            out_specs=[in_vmem] * 2,
            scratch_shapes=[pltpu.VMEM((16, held), jnp.float32)],
            compiler_params=small,
        )(lengths, features, given, gains)
        up = [(i, (i + 1) % cols) for i in range(cols)]
        lines = [[upper], [lower]]
        for _ in range(cols - 1):
            for line in lines:
                line.append(lax.ppermute(line[-1], "col", up))
        lines, weight_pieces = lax.optimization_barrier((lines, weight_pieces))
        pieces, copies = [], []
        for first, line in ((0, lines[0]), (cut, lines[1])):
            value = jnp.stack(line)
            by_near, by_far = swap(value, 2), swap(value, 4)
            across = swap(by_near, 4) if first else swap(by_far, 2)
            for flip, found in enumerate((value, by_near, by_far, across)):
                for part, arrived in enumerate((found, swap(found, 1))):
                    pieces.append(arrived)
                    copies.append([(i, (flip, i), part, held, first, cut) for i in range(cols)])
        owners = (0, 0, -1, 1, 1, -1)
        small_inputs = []
    else:
        sent = weights[0].T.reshape(rows * toks, columns, row_width)
        own_weights = lax.all_to_all(sent, ("row", "tok"), 0, 0, tiled=True)
        own_weights = own_weights.reshape(rows, models * columns, row_width)
        weight_pieces = [own_weights.transpose(1, 0, 2).reshape(models * columns, width)]
        places = [(0, 0)]
        held = slots
        everything = lax.all_gather(features, ("row", "col"), axis=0, tiled=False)
        pieces = [lax.all_gather(everything, "tok", axis=0, tiled=True)]
        tiles = slots // LANES
        owners = tuple(m for m in range(models) for _ in range(tiles))
        copies = [[
            (m * rows * cols + b, b, m, slots, 0, block) for m in range(models) for b in range(rows * cols)
        ]]
        live = jnp.arange(slots, dtype=jnp.int32)[None, :] < lengths[:, None]
        floats = features.astype(jnp.float32)
        squares = lax.psum(jnp.sum(floats * floats, axis=0), ("row", "col"))
        every_gain = lax.all_gather(gains[0], ("row", "col"), axis=0, tiled=True)
        small_inputs = [
            live.reshape(1, -1).astype(jnp.float32),
            lax.all_gather(squares, "tok", axis=0, tiled=True)[None, :],
            lax.all_gather(every_gain, "tok", axis=0, tiled=False).T,
        ]
    slots_held = toks * held

    if paired:
        out_shape = [jax.ShapeDtypeStruct((columns, sub_rows), jnp.bfloat16)] * (rows * toks)
    else:
        out_shape = [jax.ShapeDtypeStruct((columns, width), jnp.bfloat16)]
    found = pl.pallas_call(
        functools.partial(solve_kernel, owners, models, block, copies, places),
        out_shape=out_shape,
        in_specs=[scalars] + [in_vmem] * len(small_inputs) + [any_space] * (len(pieces) + len(weight_pieces)),
        out_specs=[in_vmem] * len(out_shape),
        scratch_shapes=[
            pltpu.VMEM((width, slots_held), jnp.bfloat16),
            pltpu.VMEM((models * columns, width), jnp.bfloat16),
            pltpu.VMEM((models, width), jnp.float32),
            pltpu.VMEM((1, width), jnp.float32),
            pltpu.VMEM((columns, width), jnp.float32),
            pltpu.VMEM((columns, width), jnp.float32),
            pltpu.VMEM((columns, width), jnp.float32),
            pltpu.VMEM((2 * columns, width), jnp.bfloat16),
            pltpu.VMEM((max(models, 2) * columns, slots_held), jnp.float32),
            pltpu.VMEM((columns, slots_held), jnp.bfloat16),
            pltpu.VMEM((2 * columns, slots_held), jnp.bfloat16),
            pltpu.VMEM((models * rows * cols, 16, slots_held // models) if paired else (8, 16, LANES), jnp.bfloat16),
            pltpu.VMEM((width if paired else 8, LANES), jnp.float32),
            pltpu.SemaphoreType.DMA((2,)),
        ],
        compiler_params=pltpu.CompilerParams(vmem_limit_bytes=width * slots_held * 2 + (18 << 20)),
    )(
        lengths,
        *small_inputs,
        *pieces,
        *weight_pieces,
    )
    if paired:
        arrived = [found[0]] + [swap(x, flip) for x, flip in zip(found[1:], NEAR_FIRST[1:])]
        return pl.pallas_call(
            gather_kernel,
            out_shape=jax.ShapeDtypeStruct((sub_rows, col_width), jnp.float32),
            in_specs=[in_vmem] * len(arrived),
            out_specs=in_vmem,
            scratch_shapes=[pltpu.VMEM((col_width, sub_rows), jnp.float32)],
            compiler_params=small,
        )(*arrived)
    found = found[0].reshape(columns, rows * toks, sub_rows).transpose(1, 0, 2)
    back = lax.all_to_all(found, ("row", "tok"), 0, 0, tiled=True)
    return back.reshape(col_width, sub_rows).T.astype(jnp.float32)


def solution(mesh):
    return jax.shard_map(
        body,
        mesh=mesh,
        in_specs=(P("tok", ("row", "col")), P("tok", ("row", "col")), P("tok", "row", "col"), P()),
        out_specs=P(("row", "tok"), "col"),
        check_vma=False,
    )
```

```python
import functools

import jax
import jax.numpy as jnp
from jax import lax
from jax.experimental import pallas as pl
from jax.experimental.pallas import tpu as pltpu
from jax.sharding import PartitionSpec as P

ITERS = 4

MIXING = 0.9
EPSILON = 1e-06

LANES = 128
CHUNK = 512
MOST_TOKENS = 1024
NEAR_FIRST = (0, 2, 4, 6, 3, 5, 7, 1)


def two_terms(value):
    high = value.astype(jnp.bfloat16).astype(jnp.float32)
    return jnp.concatenate([high, value - high], axis=0).astype(jnp.bfloat16)


def over_features(left, tokens, found):
    slots = tokens.shape[1]
    if slots <= MOST_TOKENS:
        found[...] = jnp.dot(left[...], tokens[...], preferred_element_type=jnp.float32)
        return

    def some(step, carry):
        lanes = pl.ds(pl.multiple_of(step * CHUNK, CHUNK), CHUNK)
        found[:, lanes] = jnp.dot(left[...], tokens[:, lanes], preferred_element_type=jnp.float32)
        return carry

    lax.fori_loop(0, slots // CHUNK, some, 0)


def over_tokens(left, tokens, part):
    slots = tokens.shape[1]
    product = functools.partial(
        lax.dot_general, dimension_numbers=(((1,), (1,)), ((), ())), preferred_element_type=jnp.float32
    )
    if slots <= MOST_TOKENS:
        return product(left[...], tokens[part, :])

    def some(step, total):
        lanes = pl.ds(pl.multiple_of(step * CHUNK, CHUNK), CHUNK)
        return total + product(left[:, lanes], tokens[part, lanes])

    return lax.fori_loop(0, slots // CHUNK, some, jnp.zeros((left.shape[0], CHUNK), jnp.float32))


def in_pair_order(lengths_ref, tok, width):
    half, quarter = width // 3, width // 6
    lane = lax.broadcasted_iota(jnp.int32, (1, width), 1)
    low = lane < width // 2
    part = jnp.where(low, tok, 1 - tok)
    spot = jnp.where(low, lane, lane - width // 2)
    place = spot - half + part * quarter
    late = spot >= half
    second = jnp.where(late, jnp.where(place >= lengths_ref[0] - half, 1, 0), part)
    position = jnp.where(late, jnp.where(second == 1, 2 * half - 1 - place, half + place), spot)
    length = jnp.where(second == 1, lengths_ref[1], lengths_ref[0])
    return jnp.where(position < length, 1.0, 0.0), second.astype(jnp.float32)


def norm_pieces(block, copies, pieces, lengths_ref, tokens, squared, diagonal, gains, sums, extras):
    width, slots = tokens.shape
    row, col, tok = lax.axis_index("row"), lax.axis_index("col"), lax.axis_index("tok")
    cols = lax.axis_size("col")
    held = slots // 2
    live, second = in_pair_order(lengths_ref, tok, slots)

    def start_of(flip, back):
        return ((row ^ flip) * cols + lax.rem(col - back + cols, cols)) * block

    extras[...] = jnp.zeros_like(extras)
    squares = [jnp.zeros((1, held), jnp.float32) for _ in range(2)]
    riders = []
    for number, (by_flip, flip, back, first, high) in enumerate(copies):
        if pieces[2 * number].shape[1] > high:
            for index in range(cols):
                for part in range(2):
                    rows = pieces[2 * number + part][index, high:high + 16, :].astype(jnp.float32)
                    squares[part] = squares[part] + (rows[0:1] + rows[1:2] + rows[2:3])
                    spot = 2 * len(riders) + part
                    extras[spot:spot + 1, :] = rows[3:4] + rows[4:5] + rows[5:6]
                riders.append((flip, back + index))
    scale = lax.rsqrt(jnp.concatenate(squares, axis=1) / width + EPSILON) * live
    turned = extras[...].T[:block]
    side = lax.broadcasted_iota(jnp.int32, (block, LANES), 1)
    for spot, (flip, back) in enumerate(riders):
        gains[pl.ds(pl.multiple_of(start_of(flip, back), 64), block), :] = jnp.where(
            side == 0, turned[:, 2 * spot:2 * spot + 1], turned[:, 2 * spot + 1:2 * spot + 2]
        )

    for number, (by_flip, flip, back, first, high) in enumerate(copies):
        both = pieces[2 * number:2 * number + 2]

        def norm_block(index, carry, both=both, by_flip=by_flip, flip=flip, back=back, first=first, high=high):
            place = start_of(index, back) if by_flip else start_of(flip, back + index)
            low = 0
            while low < high:
                size = min(80 if high % 80 == 0 else 64, high - low)
                start = pl.multiple_of(place + first + low, 16)
                gain = gains[pl.ds(start, size), :]
                own, other = gain[:, 0:1], gain[:, 1:2]
                gain_first = jnp.where(tok == 0, own, other)
                gain_second = jnp.where(tok == 0, other, own)
                sums_part = [jnp.zeros((size, LANES), jnp.float32) for _ in range(2)]
                sums_model = [jnp.zeros((size, LANES), jnp.float32) for _ in range(2)]
                for part in range(2):
                    for tile in range(held // LANES):
                        lanes = slice(part * held + tile * LANES, part * held + (tile + 1) * LANES)
                        value = both[part][index, low:low + size, tile * LANES:(tile + 1) * LANES].astype(jnp.float32)
                        mixed = tile == held // LANES - 1
                        if mixed:
                            factor = jnp.where(second[:, lanes] > 0, gain_second, gain_first)
                        else:
                            factor = (own, other)[part]
                        normed = (value * scale[:, lanes] * factor).astype(jnp.bfloat16)
                        tokens[pl.ds(start, size), lanes] = normed
                        value = normed.astype(jnp.float32)
                        value = value * value
                        if mixed:
                            theirs = value * second[:, lanes]
                            sums_model[0] = sums_model[0] + (value - theirs)
                            sums_model[1] = sums_model[1] + theirs
                        else:
                            sums_part[part] = sums_part[part] + value
                total = [
                    jnp.sum(sums_model[model] + jnp.where(tok == model, sums_part[0], sums_part[1]), axis=1, keepdims=True)
                    for model in range(2)
                ]
                lane = lax.broadcasted_iota(jnp.int32, (size, LANES), 1)
                sums[pl.ds(start, size), :] = jnp.where(lane == 0, total[0], total[1])
                low += size
            return carry

        lax.fori_loop(0, cols, norm_block, 0)

    def turn(step, carry):
        start = pl.multiple_of(step * LANES, LANES)
        rows = sums[pl.ds(start, LANES), :].T
        squared[:, pl.ds(start, LANES)] = rows[0:2]
        diagonal[:, pl.ds(start, LANES)] = rows[0:1] + rows[1:2]
        return carry

    lax.fori_loop(0, width // LANES, turn, 0, unroll=4)
    return second


def solve_kernel(owners, models, block, copies, places, lengths_ref, *refs):
    riding = len(copies) > 1
    if not riding:
        live_ref, squares_ref, gains_ref, refs = refs[0], refs[1], refs[2], refs[3:]
    count = 2 * len(copies) if riding else len(copies)
    pieces = refs[:count]
    weight_pieces = refs[count:count + len(places)]
    out_refs = refs[count + len(places):-15]
    (tokens, weights, squared, diagonal, residual, direction, merged, terms, values, outputs, seen, extras, gains_held,
     sums_held, sems) = refs[-15:]
    width, slots = tokens.shape
    columns = residual.shape[0]
    started = []
    if riding:
        row, tok = lax.axis_index("row"), lax.axis_index("tok")
    for piece, place in zip(weight_pieces, places):
        moves = [(piece, weights)]
        if riding:
            row_width = piece.shape[1]
            lane = pl.multiple_of((row ^ place) * row_width, LANES)
            moves = [
                (
                    piece.at[pl.ds(part * columns, columns)],
                    weights.at[pl.ds(pl.multiple_of((tok ^ part) * columns, columns), columns), pl.ds(lane, row_width)],
                )
                for part in range(2)
            ]
        for source, target in moves:
            copy = pltpu.make_async_copy(source, target, sems.at[1])
            copy.start()
            started.append(copy)
    if not riding:
        for piece, parts in zip(pieces, copies):
            for source, entry, part, lanes in parts:
                copy = pltpu.make_async_copy(
                    piece.at[source],
                    tokens.at[pl.ds(entry * block, block), pl.ds(part * lanes, lanes)],
                    sems.at[0],
                )
                copy.start()
                started.append(copy)

    def norm_rows(step, carry):
        start = pl.multiple_of(step * LANES, LANES)
        gains = gains_ref[pl.ds(start, LANES), :]
        sums = [jnp.zeros((LANES, LANES), jnp.float32) for _ in range(models)]
        for tile, owner in enumerate(owners):
            lanes = slice(tile * LANES, (tile + 1) * LANES)
            value = tokens[pl.ds(start, LANES), lanes].astype(jnp.float32)
            normed = (value * inverse_rms[:, lanes] * gains[:, owner:owner + 1]).astype(jnp.bfloat16)
            tokens[pl.ds(start, LANES), lanes] = normed
            value = normed.astype(jnp.float32)
            sums[owner] = sums[owner] + value * value
        sums = [jnp.sum(part.T, axis=0, keepdims=True) for part in sums]
        for model in range(models):
            squared[model:model + 1, pl.ds(start, LANES)] = sums[model]
        diagonal[:, pl.ds(start, LANES)] = functools.reduce(jnp.add, sums)
        return carry

    if riding:
        second = norm_pieces(
            block, copies, pieces, lengths_ref, tokens, squared, diagonal, gains_held, sums_held, extras
        )
    for copy in started:
        copy.wait()
    if not riding:
        inverse_rms = lax.rsqrt(squares_ref[...] / width + EPSILON) * live_ref[...]
        lax.fori_loop(0, width // LANES, norm_rows, 0)

    over_features(weights, tokens, values)
    if riding:
        outputs[...] = jnp.where(second > 0, values[columns:2 * columns, :], values[:columns, :]).astype(jnp.bfloat16)
    else:
        for tile, owner in enumerate(owners):
            lanes = slice(tile * LANES, (tile + 1) * LANES)
            outputs[:, lanes] = values[owner * columns:(owner + 1) * columns, lanes].astype(jnp.bfloat16)

    norm_now = jnp.zeros((columns, 1), jnp.float32)
    for start in range(0, width, CHUNK):
        part = slice(start, start + CHUNK)
        weighted = jnp.zeros((columns, CHUNK), jnp.float32)
        for model in range(models):
            rows = weights[model * columns:(model + 1) * columns, part].astype(jnp.float32)
            weighted = weighted + squared[model:model + 1, part] * rows
        right = MIXING * over_tokens(outputs, tokens, part) + (1.0 - MIXING) * weighted
        residual[:, part] = right
        direction[:, part] = jnp.zeros_like(right)
        merged[:, part] = jnp.zeros_like(right)
        norm_now = norm_now + jnp.sum(right * right, axis=1, keepdims=True)

    def step_of(scale, norm_now):
        weighted = jnp.zeros((columns, 1), jnp.float32)
        for start in range(0, width, CHUNK):
            part = slice(start, start + CHUNK)
            value = residual[:, part] + scale * direction[:, part]
            direction[:, part] = value
            terms[:, part] = two_terms(value)
            weighted = weighted + jnp.sum(diagonal[:, part] * value * value, axis=1, keepdims=True)
        both = values.at[:2 * columns]
        over_features(terms, tokens, both)
        both = both[:columns] + both[columns:]
        seen[...] = two_terms(both)
        curvature = MIXING * jnp.sum(both * both, axis=1, keepdims=True) + (1.0 - MIXING) * weighted
        return norm_now / curvature

    def iterate(_, carry):
        scale, norm_now = carry
        step_size = step_of(scale, norm_now)
        norm_next = jnp.zeros((columns, 1), jnp.float32)
        for start in range(0, width, CHUNK):
            part = slice(start, start + CHUNK)
            both = over_tokens(seen, tokens, part)
            along = direction[:, part]
            image = MIXING * (both[:columns] + both[columns:]) + (1.0 - MIXING) * diagonal[:, part] * along
            merged[:, part] = merged[:, part] + step_size * along
            value = residual[:, part] - step_size * image
            residual[:, part] = value
            norm_next = norm_next + jnp.sum(value * value, axis=1, keepdims=True)
        return norm_next / norm_now, norm_next

    scale, norm_now = lax.fori_loop(0, ITERS - 1, iterate, (jnp.zeros((columns, 1), jnp.float32), norm_now))
    step_size = step_of(scale, norm_now)
    merged[...] = merged[...] + step_size * direction[...]
    for number, out_ref in enumerate(out_refs):
        sub_rows = out_ref.shape[1]
        if len(out_refs) > 1:
            flip = NEAR_FIRST[number]
            sub_block = (row ^ flip // 2) * 2 + (tok ^ flip % 2)
            start = pl.multiple_of(sub_block * sub_rows, LANES)
            out_ref[...] = merged[:, pl.ds(start, sub_rows)].astype(out_ref.dtype)
        else:
            out_ref[...] = merged[...].astype(out_ref.dtype)


def three_terms(value):
    high = value.astype(jnp.bfloat16).astype(jnp.float32)
    rest = value - high
    middle = rest.astype(jnp.bfloat16).astype(jnp.float32)
    return [high, middle, rest - middle]


def piece_kernel(lengths_ref, features_ref, given_ref, gains_ref, upper_ref, lower_ref, extra):
    block, slots = features_ref.shape
    half, quarter = slots // 2, slots // 4
    tok = lax.axis_index("tok")
    first = tok == 0
    lower = features_ref[:, half:half + quarter].astype(jnp.float32)
    given = given_ref[...].astype(jnp.float32)
    row = lax.broadcasted_iota(jnp.int32, (quarter, quarter), 0)
    lane = lax.broadcasted_iota(jnp.int32, (quarter, quarter), 1)
    mirror = jnp.where(row + lane == quarter - 1, 1.0, 0.0).astype(jnp.bfloat16)
    turned = jnp.dot(
        jnp.where(first, given, lower).astype(jnp.bfloat16), mirror, preferred_element_type=jnp.float32
    )
    place = lax.broadcasted_iota(jnp.int32, (block, quarter), 1) + tok * quarter
    mixed = jnp.where(place >= lengths_ref[0] - half, turned, jnp.where(first, lower, given))
    kept = features_ref[:, :half]
    cut = block - lower_ref.shape[0]
    upper_ref[:cut, :half] = kept[:cut]
    upper_ref[:cut, half:] = mixed[:cut].astype(jnp.bfloat16)
    lower_ref[:, :half] = kept[cut:]
    lower_ref[:, half:] = mixed[cut:].astype(jnp.bfloat16)
    kept = kept.astype(jnp.float32)
    extra[...] = jnp.zeros_like(extra)
    for number, value in enumerate(three_terms(jnp.sum(kept * kept, axis=0, keepdims=True))):
        extra[number:number + 1, :half] = value
    for number, value in enumerate(three_terms(jnp.sum(mixed * mixed, axis=0, keepdims=True))):
        extra[number:number + 1, half:] = value
    for number, value in enumerate(three_terms(gains_ref[...])):
        extra[3 + number:4 + number, :block] = value
    upper_ref[cut:, :] = extra[...].astype(jnp.bfloat16)


def send_kernel(weights_ref, own_ref, other_ref, turned):
    row, tok = lax.axis_index("row"), lax.axis_index("tok")
    for start in range(0, weights_ref.shape[1], LANES):
        value = weights_ref[:, start:start + LANES].astype(jnp.float32)
        turned[start:start + LANES, :] = value.T.astype(jnp.bfloat16)
    rows, held, _ = own_ref.shape
    for flip in range(rows):
        for out_ref, core in ((own_ref, tok), (other_ref, 1 - tok)):
            start = pl.multiple_of(((row ^ flip) * 2 + core) * held, held)
            out_ref[flip] = turned[pl.ds(start, held), :]


def join_kernel(own_ref, given_ref, *refs):
    for flip, out_ref in enumerate(refs):
        held = own_ref.shape[1]
        out_ref[:held] = own_ref[flip]
        out_ref[held:] = given_ref[flip]


def gather_kernel(*refs):
    out_ref, ordered = refs[-2:]
    row, tok = lax.axis_index("row"), lax.axis_index("tok")
    for flip, piece in zip(NEAR_FIRST, refs[:-2]):
        held = piece.shape[0]
        start = pl.multiple_of(((row ^ flip // 2) * 2 + (tok ^ flip % 2)) * held, held)
        ordered[pl.ds(start, held), :] = piece[...].astype(jnp.float32)
    for start in range(0, out_ref.shape[1], LANES):
        out_ref[:, start:start + LANES] = ordered[start:start + LANES, :].T


def body(hidden, gains, weights, lengths):
    rows = lax.axis_size("row")
    cols = lax.axis_size("col")
    toks = lax.axis_size("tok")
    slots, block = hidden.shape
    width = block * rows * cols
    models = toks * gains.shape[0]
    row_width, col_width = weights.shape[1:]
    columns = col_width // (rows * toks)
    sub_rows = row_width // toks
    features = hidden.T
    paired = toks == 2 and rows == 4
    any_space = pl.BlockSpec(memory_space=pl.ANY)
    small = pltpu.CompilerParams(vmem_limit_bytes=10 << 20)
    scalars = pl.BlockSpec(memory_space=pltpu.SMEM)
    in_vmem = pl.BlockSpec(memory_space=pltpu.VMEM)

    def swap(value, flip):
        pairs = [
            (t * rows + r, (t ^ flip % 2) * rows + (r ^ flip // 2)) for t in range(toks) for r in range(rows)
        ]
        return lax.ppermute(value, ("tok", "row"), pairs)

    if paired:
        half, quarter = slots // 2, slots // 4
        held = half + quarter
        given = swap(features[:, held:], 1)
        own, other = pl.pallas_call(
            send_kernel,
            out_shape=[jax.ShapeDtypeStruct((rows, columns, row_width), jnp.bfloat16)] * 2,
            in_specs=[in_vmem],
            out_specs=[in_vmem] * 2,
            scratch_shapes=[pltpu.VMEM((col_width, row_width), jnp.bfloat16)],
            compiler_params=small,
        )(weights[0])
        joined = pl.pallas_call(
            join_kernel,
            out_shape=[jax.ShapeDtypeStruct((toks * columns, row_width), jnp.bfloat16)] * rows,
            in_specs=[in_vmem] * 2,
            out_specs=[in_vmem] * rows,
            compiler_params=small,
        )(own, swap(other, 1))
        cut = block * 3 // 4
        upper, lower = pl.pallas_call(
            piece_kernel,
            out_shape=[
                jax.ShapeDtypeStruct((cut + 16, held), jnp.bfloat16),
                jax.ShapeDtypeStruct((block - cut, held), jnp.bfloat16),
            ],
            in_specs=[scalars, in_vmem, in_vmem, in_vmem],
            out_specs=[in_vmem] * 2,
            scratch_shapes=[pltpu.VMEM((16, held), jnp.float32)],
            compiler_params=small,
        )(lengths, features, given, gains)
        up = [(i, (i + 1) % cols) for i in range(cols)]
        line = [upper]
        for _ in range(cols - 1):
            line.append(lax.ppermute(line[-1], "col", up))
        by_near, by_far = swap(lower, 2), swap(lower, 4)
        (by_near, by_far), joined = lax.optimization_barrier(((by_near, by_far), joined))
        plane = [lower, by_near, by_far, swap(by_far, 2)]
        weight_pieces = [swap(value, 2 * flip) if flip else value for flip, value in enumerate(joined)]
        places = list(range(rows))
        line, plane, weight_pieces = lax.optimization_barrier((line, plane, weight_pieces))
        value = jnp.stack(line)
        by_near, by_far = swap(value, 2), swap(value, 4)
        middle = (cut + 16) // 2
        crossed = [
            (0, 0, value), (1, 0, by_near), (2, 0, by_far),
            (3, 0, swap(by_far[:, :middle], 2)), (3, middle, swap(by_near[:, middle:], 4)),
        ]
        rounds = [jnp.stack(plane)]
        for _ in range(cols - 1):
            rounds.append(lax.ppermute(rounds[-1], "col", up))
        pieces, copies = [], []
        for flip, first, found in crossed:
            pieces += [found, swap(found, 1)]
            copies.append((False, flip, 0, first, min(first + found.shape[1], cut) - first))
        for back, found in enumerate(rounds):
            pieces += [found, swap(found, 1)]
            copies.append((True, 0, back, cut, block - cut))
        owners = ()
        small_inputs = []
    else:
        sent = weights[0].T.reshape(rows * toks, columns, row_width)
        own_weights = lax.all_to_all(sent, ("row", "tok"), 0, 0, tiled=True)
        own_weights = own_weights.reshape(rows, models * columns, row_width)
        weight_pieces = [own_weights.transpose(1, 0, 2).reshape(models * columns, width)]
        places = [(0, 0)]
        held = slots
        everything = lax.all_gather(features, ("row", "col"), axis=0, tiled=False)
        pieces = [lax.all_gather(everything, "tok", axis=0, tiled=True)]
        tiles = slots // LANES
        owners = tuple(m for m in range(models) for _ in range(tiles))
        copies = [[
            (m * rows * cols + b, b, m, slots) for m in range(models) for b in range(rows * cols)
        ]]
        live = jnp.arange(slots, dtype=jnp.int32)[None, :] < lengths[:, None]
        floats = features.astype(jnp.float32)
        squares = lax.psum(jnp.sum(floats * floats, axis=0), ("row", "col"))
        every_gain = lax.all_gather(gains[0], ("row", "col"), axis=0, tiled=True)
        small_inputs = [
            live.reshape(1, -1).astype(jnp.float32),
            lax.all_gather(squares, "tok", axis=0, tiled=True)[None, :],
            lax.all_gather(every_gain, "tok", axis=0, tiled=False).T,
        ]
    slots_held = toks * held

    if paired:
        out_shape = [jax.ShapeDtypeStruct((columns, sub_rows), jnp.bfloat16)] * (rows * toks)
    else:
        out_shape = [jax.ShapeDtypeStruct((columns, width), jnp.bfloat16)]
    found = pl.pallas_call(
        functools.partial(solve_kernel, owners, models, block, copies, places),
        out_shape=out_shape,
        in_specs=[scalars] + [in_vmem] * len(small_inputs) + [in_vmem if paired else any_space] * len(pieces)
        + [any_space] * len(weight_pieces),
        out_specs=[in_vmem] * len(out_shape),
        scratch_shapes=[
            pltpu.VMEM((width, slots_held), jnp.bfloat16),
            pltpu.VMEM((models * columns, width), jnp.bfloat16),
            pltpu.VMEM((models, width), jnp.float32),
            pltpu.VMEM((1, width), jnp.float32),
            pltpu.VMEM((columns, width), jnp.float32),
            pltpu.VMEM((columns, width), jnp.float32),
            pltpu.VMEM((columns, width), jnp.float32),
            pltpu.VMEM((2 * columns, width), jnp.bfloat16),
            pltpu.VMEM((max(models, 2) * columns, slots_held), jnp.float32),
            pltpu.VMEM((columns, slots_held), jnp.bfloat16),
            pltpu.VMEM((2 * columns, slots_held), jnp.bfloat16),
            pltpu.VMEM((LANES, held if paired else LANES), jnp.float32),
            pltpu.VMEM((width if paired else 8, LANES), jnp.float32),
            pltpu.VMEM((width if paired else 8, LANES), jnp.float32),
            pltpu.SemaphoreType.DMA((2,)),
        ],
        compiler_params=pltpu.CompilerParams(vmem_limit_bytes=width * slots_held * 2 + (18 << 20)),
    )(
        lengths,
        *small_inputs,
        *pieces,
        *weight_pieces,
    )
    if paired:
        arrived = [found[0]] + [swap(x, flip) for x, flip in zip(found[1:], NEAR_FIRST[1:])]
        return pl.pallas_call(
            gather_kernel,
            out_shape=jax.ShapeDtypeStruct((sub_rows, col_width), jnp.float32),
            in_specs=[in_vmem] * len(arrived),
            out_specs=in_vmem,
            scratch_shapes=[pltpu.VMEM((col_width, sub_rows), jnp.float32)],
            compiler_params=small,
        )(*arrived)
    found = found[0].reshape(columns, rows * toks, sub_rows).transpose(1, 0, 2)
    back = lax.all_to_all(found, ("row", "tok"), 0, 0, tiled=True)
    return back.reshape(col_width, sub_rows).T.astype(jnp.float32)


def solution(mesh):
    return jax.shard_map(
        body,
        mesh=mesh,
        in_specs=(P("tok", ("row", "col")), P("tok", ("row", "col")), P("tok", "row", "col"), P()),
        out_specs=P(("row", "tok"), "col"),
        check_vma=False,
    )
```

```python
import functools

import jax
import jax.numpy as jnp
from jax import lax
from jax.experimental import pallas as pl
from jax.experimental.pallas import tpu as pltpu
from jax.sharding import PartitionSpec as P

ITERS = 4

MIXING = 0.9
EPSILON = 1e-06

LANES = 128
CHUNK = 512
MOST_TOKENS = 1024
NEAR_FIRST = (0, 2, 4, 6, 3, 5, 7, 1)


def two_terms(value):
    high = value.astype(jnp.bfloat16).astype(jnp.float32)
    return jnp.concatenate([high, value - high], axis=0).astype(jnp.bfloat16)


def over_features(left, tokens, found):
    slots = tokens.shape[1]
    if slots <= MOST_TOKENS:
        found[...] = jnp.dot(left[...], tokens[...], preferred_element_type=jnp.float32)
        return

    def some(step, carry):
        lanes = pl.ds(pl.multiple_of(step * CHUNK, CHUNK), CHUNK)
        found[:, lanes] = jnp.dot(left[...], tokens[:, lanes], preferred_element_type=jnp.float32)
        return carry

    lax.fori_loop(0, slots // CHUNK, some, 0)


def over_tokens(left, tokens, part):
    slots = tokens.shape[1]
    product = functools.partial(
        lax.dot_general, dimension_numbers=(((1,), (1,)), ((), ())), preferred_element_type=jnp.float32
    )
    if slots <= MOST_TOKENS:
        return product(left[...], tokens[part, :])

    def some(step, total):
        lanes = pl.ds(pl.multiple_of(step * CHUNK, CHUNK), CHUNK)
        return total + product(left[:, lanes], tokens[part, lanes])

    return lax.fori_loop(0, slots // CHUNK, some, jnp.zeros((left.shape[0], CHUNK), jnp.float32))


def in_pair_order(lengths_ref, width):
    half, quarter = width // 3, width // 6
    lane = lax.broadcasted_iota(jnp.int32, (1, width), 1)
    part = jnp.where(lane >= width // 2, 1, 0)
    spot = lane - part * (width // 2)
    place = spot - half + part * quarter
    late = spot >= half
    second = jnp.where(late, jnp.where(place >= lengths_ref[0] - half, 1, 0), part)
    position = jnp.where(late, jnp.where(second == 1, 2 * half - 1 - place, half + place), spot)
    length = jnp.where(second == 1, lengths_ref[1], lengths_ref[0])
    return jnp.where(position < length, 1.0, 0.0), second.astype(jnp.float32)


def solve_kernel(owners, models, block, copies, places, lengths_ref, *refs):
    riding = len(copies) > 1
    if not riding:
        live_ref, squares_ref, gains_ref, refs = refs[0], refs[1], refs[2], refs[3:]
    pieces = refs[:len(copies)]
    weight_pieces = refs[len(copies):len(copies) + len(places)]
    out_refs = refs[len(copies) + len(places):-14]
    (tokens, weights, squared, diagonal, residual, direction, merged, terms, values, outputs, seen, extras, gains_held,
     sems) = refs[-14:]
    width, slots = tokens.shape
    columns = residual.shape[0]
    blocks = width // block
    started = []
    if riding:
        row, col, tok = lax.axis_index("row"), lax.axis_index("col"), lax.axis_index("tok")
        cols = lax.axis_size("col")
        row_devices = lax.axis_size("row")
    for piece, parts in zip(pieces, copies):
        for source, entry, part, lanes, first, held in parts:
            if riding:
                flip, back = entry
                entry = (row ^ flip) * cols + lax.rem(col - back + cols, cols)
                part = tok ^ part
            start = pl.multiple_of(entry * block + first, 16)
            lane = pl.multiple_of(part * lanes, LANES)
            copy = pltpu.make_async_copy(
                piece.at[source, pl.ds(0, held)],
                tokens.at[pl.ds(start, held), pl.ds(lane, lanes)],
                sems.at[0],
            )
            copy.start()
            started.append(copy)
            if piece.shape[1] > held:
                copy = pltpu.make_async_copy(
                    piece.at[source, pl.ds(held, 16)],
                    extras.at[part * blocks + entry],
                    sems.at[0],
                )
                copy.start()
                started.append(copy)
    for piece, place in zip(weight_pieces, places):
        moves = [(piece, weights)]
        if riding:
            row_width = piece.shape[1]
            lane = pl.multiple_of((row ^ place) * row_width, LANES)
            moves = [
                (
                    piece.at[pl.ds(part * columns, columns)],
                    weights.at[pl.ds(pl.multiple_of((tok ^ part) * columns, columns), columns), pl.ds(lane, row_width)],
                )
                for part in range(2)
            ]
        for source, target in moves:
            copy = pltpu.make_async_copy(source, target, sems.at[1])
            copy.start()
            started.append(copy)
    for copy in started:
        copy.wait()

    if riding:
        every = extras[...].astype(jnp.float32)
        sums = [jnp.sum(every[part * blocks:(part + 1) * blocks], axis=0) for part in range(models)]
        squares = jnp.concatenate([x[0:1] + x[1:2] + x[2:3] for x in sums], axis=1)
        turned = (every[:, 3] + every[:, 4] + every[:, 5]).T[:block]
        lane = lax.broadcasted_iota(jnp.int32, turned.shape, 1)
        side = lax.broadcasted_iota(jnp.int32, (block, LANES), 1)

        def hold_gains(step, carry):
            gain = [
                jnp.sum(jnp.where(lane == part * blocks + step, turned, 0.0), axis=1, keepdims=True)
                for part in range(models)
            ]
            gains_held[pl.ds(pl.multiple_of(step * block, block), block), :] = jnp.where(side == 0, gain[0], gain[1])
            return carry

        lax.fori_loop(0, blocks, hold_gains, 0)
        gains_ref = gains_held
        live, second = in_pair_order(lengths_ref, slots)
    else:
        squares, live = squares_ref[...], live_ref[...]
    inverse_rms = lax.rsqrt(squares / width + EPSILON) * live

    def norm_rows(step, carry):
        start = pl.multiple_of(step * LANES, LANES)
        gains = gains_ref[pl.ds(start, LANES), :]
        sums = [jnp.zeros((LANES, LANES), jnp.float32) for _ in range(models)]
        for tile, owner in enumerate(owners):
            lanes = slice(tile * LANES, (tile + 1) * LANES)
            value = tokens[pl.ds(start, LANES), lanes].astype(jnp.float32)
            if owner < 0:
                gain = jnp.where(second[:, lanes] > 0, gains[:, 1:2], gains[:, 0:1])
            else:
                gain = gains[:, owner:owner + 1]
            normed = (value * inverse_rms[:, lanes] * gain).astype(jnp.bfloat16)
            tokens[pl.ds(start, LANES), lanes] = normed
            value = normed.astype(jnp.float32)
            value = value * value
            if owner < 0:
                theirs = value * second[:, lanes]
                sums[0] = sums[0] + (value - theirs)
                sums[1] = sums[1] + theirs
            else:
                sums[owner] = sums[owner] + value
        sums = [jnp.sum(part.T, axis=0, keepdims=True) for part in sums]
        for model in range(models):
            squared[model:model + 1, pl.ds(start, LANES)] = sums[model]
        diagonal[:, pl.ds(start, LANES)] = functools.reduce(jnp.add, sums)
        return carry

    lax.fori_loop(0, width // LANES, norm_rows, 0, unroll=4 if riding else 1)

    over_features(weights, tokens, values)
    picked = []
    for tile, owner in enumerate(owners):
        lanes = slice(tile * LANES, (tile + 1) * LANES)
        if owner < 0:
            picked.append(jnp.where(second[:, lanes] > 0, values[columns:2 * columns, lanes], values[:columns, lanes]))
        else:
            picked.append(values[owner * columns:(owner + 1) * columns, lanes])
    outputs[...] = jnp.concatenate(picked, axis=1).astype(jnp.bfloat16)

    norm_now = jnp.zeros((columns, 1), jnp.float32)
    for start in range(0, width, CHUNK):
        part = slice(start, start + CHUNK)
        weighted = jnp.zeros((columns, CHUNK), jnp.float32)
        for model in range(models):
            rows = weights[model * columns:(model + 1) * columns, part].astype(jnp.float32)
            weighted = weighted + squared[model:model + 1, part] * rows
        right = MIXING * over_tokens(outputs, tokens, part) + (1.0 - MIXING) * weighted
        residual[:, part] = right
        direction[:, part] = jnp.zeros_like(right)
        merged[:, part] = jnp.zeros_like(right)
        norm_now = norm_now + jnp.sum(right * right, axis=1, keepdims=True)

    def step_of(scale, norm_now):
        weighted = jnp.zeros((columns, 1), jnp.float32)
        for start in range(0, width, CHUNK):
            part = slice(start, start + CHUNK)
            value = residual[:, part] + scale * direction[:, part]
            direction[:, part] = value
            terms[:, part] = two_terms(value)
            weighted = weighted + jnp.sum(diagonal[:, part] * value * value, axis=1, keepdims=True)
        both = values.at[:2 * columns]
        over_features(terms, tokens, both)
        both = both[:columns] + both[columns:]
        seen[...] = two_terms(both)
        curvature = MIXING * jnp.sum(both * both, axis=1, keepdims=True) + (1.0 - MIXING) * weighted
        return norm_now / curvature

    def iterate(_, carry):
        scale, norm_now = carry
        step_size = step_of(scale, norm_now)
        norm_next = jnp.zeros((columns, 1), jnp.float32)
        for start in range(0, width, CHUNK):
            part = slice(start, start + CHUNK)
            both = over_tokens(seen, tokens, part)
            along = direction[:, part]
            image = MIXING * (both[:columns] + both[columns:]) + (1.0 - MIXING) * diagonal[:, part] * along
            merged[:, part] = merged[:, part] + step_size * along
            value = residual[:, part] - step_size * image
            residual[:, part] = value
            norm_next = norm_next + jnp.sum(value * value, axis=1, keepdims=True)
        return norm_next / norm_now, norm_next

    scale, norm_now = lax.fori_loop(0, ITERS - 1, iterate, (jnp.zeros((columns, 1), jnp.float32), norm_now))
    step_size = step_of(scale, norm_now)
    merged[...] = merged[...] + step_size * direction[...]
    for number, out_ref in enumerate(out_refs):
        sub_rows = out_ref.shape[1]
        if len(out_refs) > 1:
            flip = NEAR_FIRST[number]
            sub_block = (row ^ flip // 2) * 2 + (tok ^ flip % 2)
            start = pl.multiple_of(sub_block * sub_rows, LANES)
            out_ref[...] = merged[:, pl.ds(start, sub_rows)].astype(out_ref.dtype)
        else:
            out_ref[...] = merged[...].astype(out_ref.dtype)


def three_terms(value):
    high = value.astype(jnp.bfloat16).astype(jnp.float32)
    rest = value - high
    middle = rest.astype(jnp.bfloat16).astype(jnp.float32)
    return [high, middle, rest - middle]


def piece_kernel(lengths_ref, features_ref, given_ref, gains_ref, upper_ref, lower_ref, extra):
    block, slots = features_ref.shape
    half, quarter = slots // 2, slots // 4
    tok = lax.axis_index("tok")
    first = tok == 0
    lower = features_ref[:, half:half + quarter].astype(jnp.float32)
    given = given_ref[...].astype(jnp.float32)
    row = lax.broadcasted_iota(jnp.int32, (quarter, quarter), 0)
    lane = lax.broadcasted_iota(jnp.int32, (quarter, quarter), 1)
    mirror = jnp.where(row + lane == quarter - 1, 1.0, 0.0).astype(jnp.bfloat16)
    turned = jnp.dot(
        jnp.where(first, given, lower).astype(jnp.bfloat16), mirror, preferred_element_type=jnp.float32
    )
    place = lax.broadcasted_iota(jnp.int32, (block, quarter), 1) + tok * quarter
    mixed = jnp.where(place >= lengths_ref[0] - half, turned, jnp.where(first, lower, given))
    kept = features_ref[:, :half]
    cut = block - lower_ref.shape[0]
    upper_ref[:cut, :half] = kept[:cut]
    upper_ref[:cut, half:] = mixed[:cut].astype(jnp.bfloat16)
    lower_ref[:, :half] = kept[cut:]
    lower_ref[:, half:] = mixed[cut:].astype(jnp.bfloat16)
    kept = kept.astype(jnp.float32)
    extra[...] = jnp.zeros_like(extra)
    for number, value in enumerate(three_terms(jnp.sum(kept * kept, axis=0, keepdims=True))):
        extra[number:number + 1, :half] = value
    for number, value in enumerate(three_terms(jnp.sum(mixed * mixed, axis=0, keepdims=True))):
        extra[number:number + 1, half:] = value
    for number, value in enumerate(three_terms(gains_ref[...])):
        extra[3 + number:4 + number, :block] = value
    upper_ref[cut:, :] = extra[...].astype(jnp.bfloat16)


def send_kernel(weights_ref, own_ref, other_ref, turned):
    row, tok = lax.axis_index("row"), lax.axis_index("tok")
    for start in range(0, weights_ref.shape[1], LANES):
        value = weights_ref[:, start:start + LANES].astype(jnp.float32)
        turned[start:start + LANES, :] = value.T.astype(jnp.bfloat16)
    rows, held, _ = own_ref.shape
    for flip in range(rows):
        for out_ref, core in ((own_ref, tok), (other_ref, 1 - tok)):
            start = pl.multiple_of(((row ^ flip) * 2 + core) * held, held)
            out_ref[flip] = turned[pl.ds(start, held), :]


def packed_rows(lower, width):
    return -(-lower.shape[0] // (width // lower.shape[1]) // 16) * 16


def join_kernel(own_ref, given_ref, lower_ref, *refs):
    _, held, width = own_ref.shape
    rows, lanes = lower_ref.shape
    high = packed_rows(lower_ref, width)
    for flip, out_ref in enumerate(refs):
        out_ref[:held] = own_ref[flip]
        out_ref[held:2 * held] = given_ref[flip]
        if flip:
            out_ref[2 * held:] = jnp.zeros((high, width), out_ref.dtype)
            for number, start in enumerate(range(0, rows, high)):
                size = min(high, rows - start)
                out_ref[2 * held:2 * held + size, number * lanes:(number + 1) * lanes] = lower_ref[start:start + size]


def plane_kernel(lower_ref, *refs):
    out_ref = refs[-1]
    rows, lanes = lower_ref.shape
    out_ref[0] = lower_ref[...]
    for flip, found in enumerate(refs[:-1]):
        high = packed_rows(lower_ref, found.shape[1])
        base = found.shape[0] - high
        for number, start in enumerate(range(0, rows, high)):
            size = min(high, rows - start)
            out_ref[flip + 1, start:start + size] = found[base:base + size, number * lanes:(number + 1) * lanes]


def gather_kernel(*refs):
    out_ref, ordered = refs[-2:]
    row, tok = lax.axis_index("row"), lax.axis_index("tok")
    for flip, piece in zip(NEAR_FIRST, refs[:-2]):
        held = piece.shape[0]
        start = pl.multiple_of(((row ^ flip // 2) * 2 + (tok ^ flip % 2)) * held, held)
        ordered[pl.ds(start, held), :] = piece[...].astype(jnp.float32)
    for start in range(0, out_ref.shape[1], LANES):
        out_ref[:, start:start + LANES] = ordered[start:start + LANES, :].T


def body(hidden, gains, weights, lengths):
    rows = lax.axis_size("row")
    cols = lax.axis_size("col")
    toks = lax.axis_size("tok")
    slots, block = hidden.shape
    width = block * rows * cols
    models = toks * gains.shape[0]
    row_width, col_width = weights.shape[1:]
    columns = col_width // (rows * toks)
    sub_rows = row_width // toks
    features = hidden.T
    paired = toks == 2 and rows == 4
    any_space = pl.BlockSpec(memory_space=pl.ANY)
    small = pltpu.CompilerParams(vmem_limit_bytes=10 << 20)
    scalars = pl.BlockSpec(memory_space=pltpu.SMEM)
    in_vmem = pl.BlockSpec(memory_space=pltpu.VMEM)

    def swap(value, flip):
        pairs = [
            (t * rows + r, (t ^ flip % 2) * rows + (r ^ flip // 2)) for t in range(toks) for r in range(rows)
        ]
        return lax.ppermute(value, ("tok", "row"), pairs)

    if paired:
        half, quarter = slots // 2, slots // 4
        held = half + quarter
        given = swap(features[:, held:], 1)
        own, other = pl.pallas_call(
            send_kernel,
            out_shape=[jax.ShapeDtypeStruct((rows, columns, row_width), jnp.bfloat16)] * 2,
            in_specs=[in_vmem],
            out_specs=[in_vmem] * 2,
            scratch_shapes=[pltpu.VMEM((col_width, row_width), jnp.bfloat16)],
            compiler_params=small,
        )(weights[0])
        cut = block * 3 // 4
        upper, lower = pl.pallas_call(
            piece_kernel,
            out_shape=[
                jax.ShapeDtypeStruct((cut + 16, held), jnp.bfloat16),
                jax.ShapeDtypeStruct((block - cut, held), jnp.bfloat16),
            ],
            in_specs=[scalars, in_vmem, in_vmem, in_vmem],
            out_specs=[in_vmem] * 2,
            scratch_shapes=[pltpu.VMEM((16, held), jnp.float32)],
            compiler_params=small,
        )(lengths, features, given, gains)
        packed = packed_rows(lower, row_width)
        joined = pl.pallas_call(
            join_kernel,
            out_shape=[
                jax.ShapeDtypeStruct((toks * columns + (packed if flip else 0), row_width), jnp.bfloat16)
                for flip in range(rows)
            ],
            in_specs=[in_vmem] * 3,
            out_specs=[in_vmem] * rows,
            compiler_params=small,
        )(own, swap(other, 1), lower)
        line = [upper] + [
            lax.ppermute(upper, "col", [(i, (i + shift) % cols) for i in range(cols)]) for shift in range(1, cols)
        ]
        weight_pieces = [swap(value, 2 * flip) if flip else value for flip, value in enumerate(joined)]
        places = list(range(rows))
        line, weight_pieces = lax.optimization_barrier((line, weight_pieces))
        plane = pl.pallas_call(
            plane_kernel,
            out_shape=jax.ShapeDtypeStruct((rows,) + lower.shape, jnp.bfloat16),
            in_specs=[in_vmem] * rows,
            out_specs=in_vmem,
            compiler_params=small,
        )(lower, *weight_pieces[1:])
        up = [(i, (i + 1) % cols) for i in range(cols)]
        value = jnp.stack(line)
        by_near, by_far = swap(value, 2), swap(value, 4)
        middle = (cut + 16) // 2
        crossed = [
            (0, 0, value), (1, 0, by_near), (2, 0, by_far),
            (3, 0, swap(by_far[:, :middle], 2)), (3, middle, swap(by_near[:, middle:], 4)),
        ]
        rounds = [plane]
        for _ in range(cols - 1):
            rounds.append(lax.ppermute(rounds[-1], "col", up))
        pieces, copies = [], []
        for flip, first, found in crossed:
            high = min(first + found.shape[1], cut) - first
            for part, arrived in enumerate((found, swap(found, 1))):
                pieces.append(arrived)
                copies.append([(i, (flip, i), part, held, first, high) for i in range(cols)])
        for back, found in enumerate(rounds):
            for part, arrived in enumerate((found, swap(found, 1))):
                pieces.append(arrived)
                copies.append([(flip, (flip, back), part, held, cut, block - cut) for flip in range(rows)])
        owners = (0, 0, -1, 1, 1, -1)
        small_inputs = []
    else:
        sent = weights[0].T.reshape(rows * toks, columns, row_width)
        own_weights = lax.all_to_all(sent, ("row", "tok"), 0, 0, tiled=True)
        own_weights = own_weights.reshape(rows, models * columns, row_width)
        weight_pieces = [own_weights.transpose(1, 0, 2).reshape(models * columns, width)]
        places = [(0, 0)]
        held = slots
        everything = lax.all_gather(features, ("row", "col"), axis=0, tiled=False)
        pieces = [lax.all_gather(everything, "tok", axis=0, tiled=True)]
        tiles = slots // LANES
        owners = tuple(m for m in range(models) for _ in range(tiles))
        copies = [[
            (m * rows * cols + b, b, m, slots, 0, block) for m in range(models) for b in range(rows * cols)
        ]]
        live = jnp.arange(slots, dtype=jnp.int32)[None, :] < lengths[:, None]
        floats = features.astype(jnp.float32)
        squares = lax.psum(jnp.sum(floats * floats, axis=0), ("row", "col"))
        every_gain = lax.all_gather(gains[0], ("row", "col"), axis=0, tiled=True)
        small_inputs = [
            live.reshape(1, -1).astype(jnp.float32),
            lax.all_gather(squares, "tok", axis=0, tiled=True)[None, :],
            lax.all_gather(every_gain, "tok", axis=0, tiled=False).T,
        ]
    slots_held = toks * held

    if paired:
        out_shape = [jax.ShapeDtypeStruct((columns, sub_rows), jnp.bfloat16)] * (rows * toks)
    else:
        out_shape = [jax.ShapeDtypeStruct((columns, width), jnp.bfloat16)]
    found = pl.pallas_call(
        functools.partial(solve_kernel, owners, models, block, copies, places),
        out_shape=out_shape,
        in_specs=[scalars] + [in_vmem] * len(small_inputs) + [any_space] * (len(pieces) + len(weight_pieces)),
        out_specs=[in_vmem] * len(out_shape),
        scratch_shapes=[
            pltpu.VMEM((width, slots_held), jnp.bfloat16),
            pltpu.VMEM((models * columns, width), jnp.bfloat16),
            pltpu.VMEM((models, width), jnp.float32),
            pltpu.VMEM((1, width), jnp.float32),
            pltpu.VMEM((columns, width), jnp.float32),
            pltpu.VMEM((columns, width), jnp.float32),
            pltpu.VMEM((columns, width), jnp.float32),
            pltpu.VMEM((2 * columns, width), jnp.bfloat16),
            pltpu.VMEM((max(models, 2) * columns, slots_held), jnp.float32),
            pltpu.VMEM((columns, slots_held), jnp.bfloat16),
            pltpu.VMEM((2 * columns, slots_held), jnp.bfloat16),
            pltpu.VMEM((models * rows * cols, 16, slots_held // models) if paired else (8, 16, LANES), jnp.bfloat16),
            pltpu.VMEM((width if paired else 8, LANES), jnp.float32),
            pltpu.SemaphoreType.DMA((2,)),
        ],
        compiler_params=pltpu.CompilerParams(vmem_limit_bytes=width * slots_held * 2 + (18 << 20)),
    )(
        lengths,
        *small_inputs,
        *pieces,
        *weight_pieces,
    )
    if paired:
        arrived = [found[0]] + [swap(x, flip) for x, flip in zip(found[1:], NEAR_FIRST[1:])]
        return pl.pallas_call(
            gather_kernel,
            out_shape=jax.ShapeDtypeStruct((sub_rows, col_width), jnp.float32),
            in_specs=[in_vmem] * len(arrived),
            out_specs=in_vmem,
            scratch_shapes=[pltpu.VMEM((col_width, sub_rows), jnp.float32)],
            compiler_params=small,
        )(*arrived)
    found = found[0].reshape(columns, rows * toks, sub_rows).transpose(1, 0, 2)
    back = lax.all_to_all(found, ("row", "tok"), 0, 0, tiled=True)
    return back.reshape(col_width, sub_rows).T.astype(jnp.float32)


def solution(mesh):
    return jax.shard_map(
        body,
        mesh=mesh,
        in_specs=(P("tok", ("row", "col")), P("tok", ("row", "col")), P("tok", "row", "col"), P()),
        out_specs=P(("row", "tok"), "col"),
        check_vma=False,
    )
```

```python
import functools

import jax
import jax.numpy as jnp
from jax import lax
from jax.experimental import pallas as pl
from jax.experimental.pallas import tpu as pltpu
from jax.sharding import PartitionSpec as P

ITERS = 4

MIXING = 0.9
EPSILON = 1e-06

LANES = 128
CHUNK = 1024
MOST_TOKENS = 1024
NEAR_FIRST = (0, 2, 4, 6, 3, 5, 7, 1)


def two_terms(value):
    high = value.astype(jnp.bfloat16).astype(jnp.float32)
    return jnp.concatenate([high, value - high], axis=0).astype(jnp.bfloat16)


def over_features(left, tokens, found):
    slots = tokens.shape[1]
    if slots <= MOST_TOKENS:
        found[...] = jnp.dot(left[...], tokens[...], preferred_element_type=jnp.float32)
        return

    def some(step, carry):
        lanes = pl.ds(pl.multiple_of(step * CHUNK, CHUNK), CHUNK)
        found[:, lanes] = jnp.dot(left[...], tokens[:, lanes], preferred_element_type=jnp.float32)
        return carry

    lax.fori_loop(0, slots // CHUNK, some, 0)


def over_tokens(left, tokens, part):
    slots = tokens.shape[1]
    product = functools.partial(
        lax.dot_general, dimension_numbers=(((1,), (1,)), ((), ())), preferred_element_type=jnp.float32
    )
    if slots <= MOST_TOKENS:
        return product(left[...], tokens[part, :])

    def some(step, total):
        lanes = pl.ds(pl.multiple_of(step * CHUNK, CHUNK), CHUNK)
        return total + product(left[:, lanes], tokens[part, lanes])

    return lax.fori_loop(0, slots // CHUNK, some, jnp.zeros((left.shape[0], CHUNK), jnp.float32))


def in_pair_order(lengths_ref, width):
    half, quarter = width // 3, width // 6
    lane = lax.broadcasted_iota(jnp.int32, (1, width), 1)
    part = jnp.where(lane >= width // 2, 1, 0)
    spot = lane - part * (width // 2)
    place = spot - half + part * quarter
    late = spot >= half
    second = jnp.where(late, jnp.where(place >= lengths_ref[0] - half, 1, 0), part)
    position = jnp.where(late, jnp.where(second == 1, 2 * half - 1 - place, half + place), spot)
    length = jnp.where(second == 1, lengths_ref[1], lengths_ref[0])
    return jnp.where(position < length, 1.0, 0.0), second.astype(jnp.float32)


def solve_kernel(owners, models, block, copies, places, lengths_ref, *refs):
    riding = len(copies) > 1
    if not riding:
        live_ref, squares_ref, gains_ref, refs = refs[0], refs[1], refs[2], refs[3:]
    pieces = refs[:len(copies)]
    weight_pieces = refs[len(copies):len(copies) + len(places)]
    out_refs = refs[len(copies) + len(places):-14]
    (tokens, weights, squared, diagonal, residual, direction, merged, terms, values, outputs, seen, extras, gains_held,
     sems) = refs[-14:]
    width, slots = tokens.shape
    columns = residual.shape[0]
    blocks = width // block
    started = [[], [], []]

    def begin(source, target, kind):
        copy = pltpu.make_async_copy(source, target, sems.at[kind])
        copy.start()
        started[kind].append(copy)

    def finish(kind):
        for copy in started[kind]:
            copy.wait()

    if riding:
        row, col, tok = lax.axis_index("row"), lax.axis_index("col"), lax.axis_index("tok")
        cols = lax.axis_size("col")
    moves = []
    for piece, parts in zip(pieces, copies):
        for source, entry, part, lanes, first, held in parts:
            if riding:
                flip, back = entry
                entry = (row ^ flip) * cols + lax.rem(col - back + cols, cols)
                part = tok ^ part
            moves.append((piece, source, entry, part, lanes, first, held))
    for piece, source, entry, part, lanes, first, held in moves:
        if piece.shape[1] > held:
            begin(piece.at[source, pl.ds(held, 16)], extras.at[part * blocks + entry], 0)
    for piece, source, entry, part, lanes, first, held in moves:
        start = pl.multiple_of(entry * block + first, 16)
        lane = pl.multiple_of(part * lanes, LANES)
        begin(piece.at[source, pl.ds(0, held)], tokens.at[pl.ds(start, held), pl.ds(lane, lanes)], 1)
    for piece, place in zip(weight_pieces, places):
        if riding:
            row_width = piece.shape[1]
            lane = pl.multiple_of((row ^ place) * row_width, LANES)
            for part in range(2):
                high = pl.multiple_of((tok ^ part) * columns, columns)
                begin(
                    piece.at[pl.ds(part * columns, columns)],
                    weights.at[pl.ds(high, columns), pl.ds(lane, row_width)],
                    2,
                )
        else:
            begin(piece, weights, 2)
    finish(0)

    if riding:
        every = extras[...].astype(jnp.float32)
        sums = [jnp.sum(every[part * blocks:(part + 1) * blocks], axis=0) for part in range(models)]
        squares = jnp.concatenate([x[0:1] + x[1:2] + x[2:3] for x in sums], axis=1)
        turned = (every[:, 3] + every[:, 4] + every[:, 5]).T[:block]
        lane = lax.broadcasted_iota(jnp.int32, turned.shape, 1)
        side = lax.broadcasted_iota(jnp.int32, (block, LANES), 1)

        def hold_gains(step, carry):
            gain = [
                jnp.sum(jnp.where(lane == part * blocks + step, turned, 0.0), axis=1, keepdims=True)
                for part in range(models)
            ]
            gains_held[pl.ds(pl.multiple_of(step * block, block), block), :] = jnp.where(side == 0, gain[0], gain[1])
            return carry

        lax.fori_loop(0, blocks, hold_gains, 0)
        gains_ref = gains_held
        live, second = in_pair_order(lengths_ref, slots)
    else:
        squares, live = squares_ref[...], live_ref[...]
    inverse_rms = lax.rsqrt(squares / width + EPSILON) * live
    finish(1)

    def norm_rows(step, carry):
        start = pl.multiple_of(step * LANES, LANES)
        gains = gains_ref[pl.ds(start, LANES), :]
        sums = [jnp.zeros((LANES, LANES), jnp.float32) for _ in range(models)]
        for tile, owner in enumerate(owners):
            lanes = slice(tile * LANES, (tile + 1) * LANES)
            value = tokens[pl.ds(start, LANES), lanes].astype(jnp.float32)
            if owner < 0:
                gain = jnp.where(second[:, lanes] > 0, gains[:, 1:2], gains[:, 0:1])
            else:
                gain = gains[:, owner:owner + 1]
            normed = (value * inverse_rms[:, lanes] * gain).astype(jnp.bfloat16)
            tokens[pl.ds(start, LANES), lanes] = normed
            value = normed.astype(jnp.float32)
            value = value * value
            if owner < 0:
                theirs = value * second[:, lanes]
                sums[0] = sums[0] + (value - theirs)
                sums[1] = sums[1] + theirs
            else:
                sums[owner] = sums[owner] + value
        sums = [jnp.sum(part.T, axis=0, keepdims=True) for part in sums]
        for model in range(models):
            squared[model:model + 1, pl.ds(start, LANES)] = sums[model]
        diagonal[:, pl.ds(start, LANES)] = functools.reduce(jnp.add, sums)
        return carry

    lax.fori_loop(0, width // LANES, norm_rows, 0, unroll=4 if riding else 1)

    finish(2)
    over_features(weights, tokens, values)
    picked = []
    for tile, owner in enumerate(owners):
        lanes = slice(tile * LANES, (tile + 1) * LANES)
        if owner < 0:
            picked.append(jnp.where(second[:, lanes] > 0, values[columns:2 * columns, lanes], values[:columns, lanes]))
        else:
            picked.append(values[owner * columns:(owner + 1) * columns, lanes])
    outputs[...] = jnp.concatenate(picked, axis=1).astype(jnp.bfloat16)

    norm_now = jnp.zeros((columns, 1), jnp.float32)
    for start in range(0, width, CHUNK):
        part = slice(start, start + CHUNK)
        weighted = jnp.zeros((columns, CHUNK), jnp.float32)
        for model in range(models):
            rows = weights[model * columns:(model + 1) * columns, part].astype(jnp.float32)
            weighted = weighted + squared[model:model + 1, part] * rows
        right = MIXING * over_tokens(outputs, tokens, part) + (1.0 - MIXING) * weighted
        residual[:, part] = right
        direction[:, part] = jnp.zeros_like(right)
        merged[:, part] = jnp.zeros_like(right)
        norm_now = norm_now + jnp.sum(right * right, axis=1, keepdims=True)

    def step_of(scale, norm_now):
        weighted = jnp.zeros((columns, 1), jnp.float32)
        for start in range(0, width, CHUNK):
            part = slice(start, start + CHUNK)
            value = residual[:, part] + scale * direction[:, part]
            direction[:, part] = value
            terms[:, part] = two_terms(value)
            weighted = weighted + jnp.sum(diagonal[:, part] * value * value, axis=1, keepdims=True)
        both = values.at[:2 * columns]
        over_features(terms, tokens, both)
        both = both[:columns] + both[columns:]
        seen[...] = two_terms(both)
        curvature = MIXING * jnp.sum(both * both, axis=1, keepdims=True) + (1.0 - MIXING) * weighted
        return norm_now / curvature

    def iterate(_, carry):
        scale, norm_now = carry
        step_size = step_of(scale, norm_now)
        norm_next = jnp.zeros((columns, 1), jnp.float32)
        for start in range(0, width, CHUNK):
            part = slice(start, start + CHUNK)
            both = over_tokens(seen, tokens, part)
            along = direction[:, part]
            image = MIXING * (both[:columns] + both[columns:]) + (1.0 - MIXING) * diagonal[:, part] * along
            merged[:, part] = merged[:, part] + step_size * along
            value = residual[:, part] - step_size * image
            residual[:, part] = value
            norm_next = norm_next + jnp.sum(value * value, axis=1, keepdims=True)
        return norm_next / norm_now, norm_next

    scale, norm_now = lax.fori_loop(0, ITERS - 1, iterate, (jnp.zeros((columns, 1), jnp.float32), norm_now))
    step_size = step_of(scale, norm_now)
    merged[...] = merged[...] + step_size * direction[...]
    for number, out_ref in enumerate(out_refs):
        sub_rows = out_ref.shape[1]
        if len(out_refs) > 1:
            flip = NEAR_FIRST[number]
            sub_block = (row ^ flip // 2) * 2 + (tok ^ flip % 2)
            start = pl.multiple_of(sub_block * sub_rows, LANES)
            out_ref[...] = merged[:, pl.ds(start, sub_rows)].astype(out_ref.dtype)
        else:
            out_ref[...] = merged[...].astype(out_ref.dtype)


def three_terms(value):
    high = value.astype(jnp.bfloat16).astype(jnp.float32)
    rest = value - high
    middle = rest.astype(jnp.bfloat16).astype(jnp.float32)
    return [high, middle, rest - middle]


def piece_kernel(lengths_ref, features_ref, given_ref, gains_ref, upper_ref, lower_ref, extra):
    block, slots = features_ref.shape
    half, quarter = slots // 2, slots // 4
    tok = lax.axis_index("tok")
    first = tok == 0
    lower = features_ref[:, half:half + quarter].astype(jnp.float32)
    given = given_ref[...].astype(jnp.float32)
    row = lax.broadcasted_iota(jnp.int32, (quarter, quarter), 0)
    lane = lax.broadcasted_iota(jnp.int32, (quarter, quarter), 1)
    mirror = jnp.where(row + lane == quarter - 1, 1.0, 0.0).astype(jnp.bfloat16)
    turned = jnp.dot(
        jnp.where(first, given, lower).astype(jnp.bfloat16), mirror, preferred_element_type=jnp.float32
    )
    place = lax.broadcasted_iota(jnp.int32, (block, quarter), 1) + tok * quarter
    mixed = jnp.where(place >= lengths_ref[0] - half, turned, jnp.where(first, lower, given))
    kept = features_ref[:, :half]
    cut = block - lower_ref.shape[0]
    upper_ref[:cut, :half] = kept[:cut]
    upper_ref[:cut, half:] = mixed[:cut].astype(jnp.bfloat16)
    lower_ref[:, :half] = kept[cut:]
    lower_ref[:, half:] = mixed[cut:].astype(jnp.bfloat16)
    kept = kept.astype(jnp.float32)
    extra[...] = jnp.zeros_like(extra)
    for number, value in enumerate(three_terms(jnp.sum(kept * kept, axis=0, keepdims=True))):
        extra[number:number + 1, :half] = value
    for number, value in enumerate(three_terms(jnp.sum(mixed * mixed, axis=0, keepdims=True))):
        extra[number:number + 1, half:] = value
    for number, value in enumerate(three_terms(gains_ref[...])):
        extra[3 + number:4 + number, :block] = value
    upper_ref[cut:, :] = extra[...].astype(jnp.bfloat16)


def send_kernel(weights_ref, own_ref, other_ref, turned):
    row, tok = lax.axis_index("row"), lax.axis_index("tok")
    for start in range(0, weights_ref.shape[1], LANES):
        value = weights_ref[:, start:start + LANES].astype(jnp.float32)
        turned[start:start + LANES, :] = value.T.astype(jnp.bfloat16)
    rows, held, _ = own_ref.shape
    for flip in range(rows):
        for out_ref, core in ((own_ref, tok), (other_ref, 1 - tok)):
            start = pl.multiple_of(((row ^ flip) * 2 + core) * held, held)
            out_ref[flip] = turned[pl.ds(start, held), :]


def packed_rows(lower, width):
    return -(-lower.shape[0] // (width // lower.shape[1]) // 16) * 16


def join_kernel(own_ref, given_ref, lower_ref, *refs):
    _, held, width = own_ref.shape
    rows, lanes = lower_ref.shape
    high = packed_rows(lower_ref, width)
    for flip, out_ref in enumerate(refs):
        out_ref[:held] = own_ref[flip]
        out_ref[held:2 * held] = given_ref[flip]
        if flip:
            out_ref[2 * held:] = jnp.zeros((high, width), out_ref.dtype)
            for number, start in enumerate(range(0, rows, high)):
                size = min(high, rows - start)
                out_ref[2 * held:2 * held + size, number * lanes:(number + 1) * lanes] = lower_ref[start:start + size]


def plane_kernel(lower_ref, *refs):
    out_ref = refs[-1]
    rows, lanes = lower_ref.shape
    out_ref[0] = lower_ref[...]
    for flip, found in enumerate(refs[:-1]):
        high = packed_rows(lower_ref, found.shape[1])
        base = found.shape[0] - high
        for number, start in enumerate(range(0, rows, high)):
            size = min(high, rows - start)
            out_ref[flip + 1, start:start + size] = found[base:base + size, number * lanes:(number + 1) * lanes]


def gather_kernel(*refs):
    out_ref, ordered = refs[-2:]
    row, tok = lax.axis_index("row"), lax.axis_index("tok")
    for flip, piece in zip(NEAR_FIRST, refs[:-2]):
        held = piece.shape[0]
        start = pl.multiple_of(((row ^ flip // 2) * 2 + (tok ^ flip % 2)) * held, held)
        ordered[pl.ds(start, held), :] = piece[...].astype(jnp.float32)
    for start in range(0, out_ref.shape[1], LANES):
        out_ref[:, start:start + LANES] = ordered[start:start + LANES, :].T


def body(hidden, gains, weights, lengths):
    rows = lax.axis_size("row")
    cols = lax.axis_size("col")
    toks = lax.axis_size("tok")
    slots, block = hidden.shape
    width = block * rows * cols
    models = toks * gains.shape[0]
    row_width, col_width = weights.shape[1:]
    columns = col_width // (rows * toks)
    sub_rows = row_width // toks
    features = hidden.T
    paired = toks == 2 and rows == 4
    any_space = pl.BlockSpec(memory_space=pl.ANY)
    small = pltpu.CompilerParams(vmem_limit_bytes=10 << 20)
    scalars = pl.BlockSpec(memory_space=pltpu.SMEM)
    in_vmem = pl.BlockSpec(memory_space=pltpu.VMEM)

    def swap(value, flip):
        pairs = [
            (t * rows + r, (t ^ flip % 2) * rows + (r ^ flip // 2)) for t in range(toks) for r in range(rows)
        ]
        return lax.ppermute(value, ("tok", "row"), pairs)

    if paired:
        half, quarter = slots // 2, slots // 4
        held = half + quarter
        given = swap(features[:, held:], 1)
        own, other = pl.pallas_call(
            send_kernel,
            out_shape=[jax.ShapeDtypeStruct((rows, columns, row_width), jnp.bfloat16)] * 2,
            in_specs=[in_vmem],
            out_specs=[in_vmem] * 2,
            scratch_shapes=[pltpu.VMEM((col_width, row_width), jnp.bfloat16)],
            compiler_params=small,
        )(weights[0])
        cut = block * 7 // 10
        upper, lower = pl.pallas_call(
            piece_kernel,
            out_shape=[
                jax.ShapeDtypeStruct((cut + 16, held), jnp.bfloat16),
                jax.ShapeDtypeStruct((block - cut, held), jnp.bfloat16),
            ],
            in_specs=[scalars, in_vmem, in_vmem, in_vmem],
            out_specs=[in_vmem] * 2,
            scratch_shapes=[pltpu.VMEM((16, held), jnp.float32)],
            compiler_params=small,
        )(lengths, features, given, gains)
        packed = packed_rows(lower, row_width)
        joined = pl.pallas_call(
            join_kernel,
            out_shape=[
                jax.ShapeDtypeStruct((toks * columns + (packed if flip else 0), row_width), jnp.bfloat16)
                for flip in range(rows)
            ],
            in_specs=[in_vmem] * 3,
            out_specs=[in_vmem] * rows,
            compiler_params=small,
        )(own, swap(other, 1), lower)
        line = [upper] + [
            lax.ppermute(upper, "col", [(i, (i + shift) % cols) for i in range(cols)]) for shift in range(1, cols)
        ]
        weight_pieces = [swap(value, 2 * flip) if flip else value for flip, value in enumerate(joined)]
        places = list(range(rows))
        line, weight_pieces = lax.optimization_barrier((line, weight_pieces))
        plane = pl.pallas_call(
            plane_kernel,
            out_shape=jax.ShapeDtypeStruct((rows,) + lower.shape, jnp.bfloat16),
            in_specs=[in_vmem] * rows,
            out_specs=in_vmem,
            compiler_params=small,
        )(lower, *weight_pieces[1:])
        up = [(i, (i + 1) % cols) for i in range(cols)]
        value = jnp.stack(line)
        by_near, by_far = swap(value, 2), swap(value, 4)
        middle = cut // 2
        crossed = [
            (0, 0, value), (1, 0, by_near), (2, 0, by_far),
            (3, 0, swap(by_far[:, :middle], 2)), (3, middle, swap(by_near[:, middle:], 4)),
        ]
        rounds = [plane]
        for _ in range(cols - 1):
            rounds.append(lax.ppermute(rounds[-1], "col", up))
        pieces, copies = [], []
        for flip, first, found in crossed:
            high = min(first + found.shape[1], cut) - first
            for part, arrived in enumerate((found, swap(found, 1))):
                pieces.append(arrived)
                copies.append([(i, (flip, i), part, held, first, high) for i in range(cols)])
        for back, found in enumerate(rounds):
            for part, arrived in enumerate((found, swap(found, 1))):
                pieces.append(arrived)
                copies.append([(flip, (flip, back), part, held, cut, block - cut) for flip in range(rows)])
        owners = (0, 0, -1, 1, 1, -1)
        small_inputs = []
    else:
        sent = weights[0].T.reshape(rows * toks, columns, row_width)
        own_weights = lax.all_to_all(sent, ("row", "tok"), 0, 0, tiled=True)
        own_weights = own_weights.reshape(rows, models * columns, row_width)
        weight_pieces = [own_weights.transpose(1, 0, 2).reshape(models * columns, width)]
        places = [(0, 0)]
        held = slots
        everything = lax.all_gather(features, ("row", "col"), axis=0, tiled=False)
        pieces = [lax.all_gather(everything, "tok", axis=0, tiled=True)]
        tiles = slots // LANES
        owners = tuple(m for m in range(models) for _ in range(tiles))
        copies = [[
            (m * rows * cols + b, b, m, slots, 0, block) for m in range(models) for b in range(rows * cols)
        ]]
        live = jnp.arange(slots, dtype=jnp.int32)[None, :] < lengths[:, None]
        floats = features.astype(jnp.float32)
        squares = lax.psum(jnp.sum(floats * floats, axis=0), ("row", "col"))
        every_gain = lax.all_gather(gains[0], ("row", "col"), axis=0, tiled=True)
        small_inputs = [
            live.reshape(1, -1).astype(jnp.float32),
            lax.all_gather(squares, "tok", axis=0, tiled=True)[None, :],
            lax.all_gather(every_gain, "tok", axis=0, tiled=False).T,
        ]
    slots_held = toks * held

    if paired:
        out_shape = [jax.ShapeDtypeStruct((columns, sub_rows), jnp.bfloat16)] * (rows * toks)
    else:
        out_shape = [jax.ShapeDtypeStruct((columns, width), jnp.bfloat16)]
    found = pl.pallas_call(
        functools.partial(solve_kernel, owners, models, block, copies, places),
        out_shape=out_shape,
        in_specs=[scalars] + [in_vmem] * len(small_inputs) + [any_space] * (len(pieces) + len(weight_pieces)),
        out_specs=[in_vmem] * len(out_shape),
        scratch_shapes=[
            pltpu.VMEM((width, slots_held), jnp.bfloat16),
            pltpu.VMEM((models * columns, width), jnp.bfloat16),
            pltpu.VMEM((models, width), jnp.float32),
            pltpu.VMEM((1, width), jnp.float32),
            pltpu.VMEM((columns, width), jnp.float32),
            pltpu.VMEM((columns, width), jnp.float32),
            pltpu.VMEM((columns, width), jnp.float32),
            pltpu.VMEM((2 * columns, width), jnp.bfloat16),
            pltpu.VMEM((max(models, 2) * columns, slots_held), jnp.float32),
            pltpu.VMEM((columns, slots_held), jnp.bfloat16),
            pltpu.VMEM((2 * columns, slots_held), jnp.bfloat16),
            pltpu.VMEM((models * rows * cols, 16, slots_held // models) if paired else (8, 16, LANES), jnp.bfloat16),
            pltpu.VMEM((width if paired else 8, LANES), jnp.float32),
            pltpu.SemaphoreType.DMA((3,)),
        ],
        compiler_params=pltpu.CompilerParams(vmem_limit_bytes=width * slots_held * 2 + (18 << 20)),
    )(
        lengths,
        *small_inputs,
        *pieces,
        *weight_pieces,
    )
    if paired:
        arrived = [found[0]] + [swap(x, flip) for x, flip in zip(found[1:], NEAR_FIRST[1:])]
        return pl.pallas_call(
            gather_kernel,
            out_shape=jax.ShapeDtypeStruct((sub_rows, col_width), jnp.float32),
            in_specs=[in_vmem] * len(arrived),
            out_specs=in_vmem,
            scratch_shapes=[pltpu.VMEM((col_width, sub_rows), jnp.float32)],
            compiler_params=small,
        )(*arrived)
    found = found[0].reshape(columns, rows * toks, sub_rows).transpose(1, 0, 2)
    back = lax.all_to_all(found, ("row", "tok"), 0, 0, tiled=True)
    return back.reshape(col_width, sub_rows).T.astype(jnp.float32)


def solution(mesh):
    return jax.shard_map(
        body,
        mesh=mesh,
        in_specs=(P("tok", ("row", "col")), P("tok", ("row", "col")), P("tok", "row", "col"), P()),
        out_specs=P(("row", "tok"), "col"),
        check_vma=False,
    )
```

```python
import functools

import jax
import jax.numpy as jnp
from jax import lax
from jax.experimental import pallas as pl
from jax.experimental.pallas import tpu as pltpu
from jax.sharding import PartitionSpec as P

ITERS = 4

MIXING = 0.9
EPSILON = 1e-06

LANES = 128
CHUNK = 1024
MOST_TOKENS = 1024
NEAR_FIRST = (0, 2, 4, 6, 3, 5, 7, 1)


def two_terms(value):
    high = value.astype(jnp.bfloat16).astype(jnp.float32)
    return jnp.concatenate([high, value - high], axis=0).astype(jnp.bfloat16)


def over_features(left, tokens, found):
    slots = tokens.shape[1]
    if slots <= MOST_TOKENS:
        found[...] = jnp.dot(left[...], tokens[...], preferred_element_type=jnp.float32)
        return

    def some(step, carry):
        lanes = pl.ds(pl.multiple_of(step * CHUNK, CHUNK), CHUNK)
        found[:, lanes] = jnp.dot(left[...], tokens[:, lanes], preferred_element_type=jnp.float32)
        return carry

    lax.fori_loop(0, slots // CHUNK, some, 0)


def add_over_features(left, tokens, part, found):
    slots = tokens.shape[1]
    if slots <= MOST_TOKENS:
        found[...] += jnp.dot(left, tokens[part, :], preferred_element_type=jnp.float32)
        return

    def some(step, carry):
        lanes = pl.ds(pl.multiple_of(step * CHUNK, CHUNK), CHUNK)
        found[:, lanes] += jnp.dot(left, tokens[part, lanes], preferred_element_type=jnp.float32)
        return carry

    lax.fori_loop(0, slots // CHUNK, some, 0)


def over_tokens(left, tokens, part):
    slots = tokens.shape[1]
    product = functools.partial(
        lax.dot_general, dimension_numbers=(((1,), (1,)), ((), ())), preferred_element_type=jnp.float32
    )
    if slots <= MOST_TOKENS:
        return product(left[...], tokens[part, :])

    def some(step, total):
        lanes = pl.ds(pl.multiple_of(step * CHUNK, CHUNK), CHUNK)
        return total + product(left[:, lanes], tokens[part, lanes])

    return lax.fori_loop(0, slots // CHUNK, some, jnp.zeros((left.shape[0], CHUNK), jnp.float32))


def in_pair_order(lengths_ref, width):
    half, quarter = width // 3, width // 6
    lane = lax.broadcasted_iota(jnp.int32, (1, width), 1)
    part = jnp.where(lane >= width // 2, 1, 0)
    spot = lane - part * (width // 2)
    place = spot - half + part * quarter
    late = spot >= half
    second = jnp.where(late, jnp.where(place >= lengths_ref[0] - half, 1, 0), part)
    position = jnp.where(late, jnp.where(second == 1, 2 * half - 1 - place, half + place), spot)
    length = jnp.where(second == 1, lengths_ref[1], lengths_ref[0])
    return jnp.where(position < length, 1.0, 0.0), second.astype(jnp.float32)


def solve_kernel(owners, models, block, copies, places, lengths_ref, *refs):
    riding = len(copies) > 1
    if not riding:
        live_ref, squares_ref, gains_ref, refs = refs[0], refs[1], refs[2], refs[3:]
    pieces = refs[:len(copies)]
    weight_pieces = refs[len(copies):len(copies) + len(places)]
    out_refs = refs[len(copies) + len(places):-14]
    (tokens, weights, squared, diagonal, residual, direction, merged, kept, values, outputs, seen, extras, gains_held,
     sems) = refs[-14:]
    width, slots = tokens.shape
    columns = residual.shape[0]
    blocks = width // block
    started = [[], [], []]

    def begin(source, target, kind):
        copy = pltpu.make_async_copy(source, target, sems.at[kind])
        copy.start()
        started[kind].append(copy)

    def finish(kind):
        for copy in started[kind]:
            copy.wait()

    if riding:
        row, col, tok = lax.axis_index("row"), lax.axis_index("col"), lax.axis_index("tok")
        cols = lax.axis_size("col")
    moves = []
    for piece, parts in zip(pieces, copies):
        for source, entry, part, lanes, first, held in parts:
            if riding:
                flip, back = entry
                entry = (row ^ flip) * cols + lax.rem(col - back + cols, cols)
                part = tok ^ part
            moves.append((piece, source, entry, part, lanes, first, held))
    for piece, source, entry, part, lanes, first, held in moves:
        if piece.shape[1] > held:
            begin(piece.at[source, pl.ds(held, 16)], extras.at[part * blocks + entry], 0)
    for piece, source, entry, part, lanes, first, held in moves:
        start = pl.multiple_of(entry * block + first, 16)
        lane = pl.multiple_of(part * lanes, LANES)
        begin(piece.at[source, pl.ds(0, held)], tokens.at[pl.ds(start, held), pl.ds(lane, lanes)], 1)
    for piece, place in zip(weight_pieces, places):
        if riding:
            row_width = piece.shape[1]
            lane = pl.multiple_of((row ^ place) * row_width, LANES)
            for part in range(2):
                high = pl.multiple_of((tok ^ part) * columns, columns)
                begin(
                    piece.at[pl.ds(part * columns, columns)],
                    weights.at[pl.ds(high, columns), pl.ds(lane, row_width)],
                    2,
                )
        else:
            begin(piece, weights, 2)
    finish(0)

    if riding:
        every = extras[...].astype(jnp.float32)
        sums = [jnp.sum(every[part * blocks:(part + 1) * blocks], axis=0) for part in range(models)]
        squares = jnp.concatenate([x[0:1] + x[1:2] + x[2:3] for x in sums], axis=1)
        turned = (every[:, 3] + every[:, 4] + every[:, 5]).T[:block]
        lane = lax.broadcasted_iota(jnp.int32, turned.shape, 1)
        side = lax.broadcasted_iota(jnp.int32, (block, LANES), 1)

        def hold_gains(step, carry):
            gain = [
                jnp.sum(jnp.where(lane == part * blocks + step, turned, 0.0), axis=1, keepdims=True)
                for part in range(models)
            ]
            gains_held[pl.ds(pl.multiple_of(step * block, block), block), :] = jnp.where(side == 0, gain[0], gain[1])
            return carry

        lax.fori_loop(0, blocks, hold_gains, 0)
        gains_ref = gains_held
        live, second = in_pair_order(lengths_ref, slots)
    else:
        squares, live = squares_ref[...], live_ref[...]
    inverse_rms = lax.rsqrt(squares / width + EPSILON) * live
    finish(1)

    def norm_rows(step, carry):
        start = pl.multiple_of(step * LANES, LANES)
        gains = gains_ref[pl.ds(start, LANES), :]
        sums = [jnp.zeros((LANES, LANES), jnp.float32) for _ in range(models)]
        for tile, owner in enumerate(owners):
            lanes = slice(tile * LANES, (tile + 1) * LANES)
            value = tokens[pl.ds(start, LANES), lanes].astype(jnp.float32)
            if owner < 0:
                gain = jnp.where(second[:, lanes] > 0, gains[:, 1:2], gains[:, 0:1])
            else:
                gain = gains[:, owner:owner + 1]
            normed = (value * inverse_rms[:, lanes] * gain).astype(jnp.bfloat16)
            tokens[pl.ds(start, LANES), lanes] = normed
            value = normed.astype(jnp.float32)
            value = value * value
            if owner < 0:
                theirs = value * second[:, lanes]
                sums[0] = sums[0] + (value - theirs)
                sums[1] = sums[1] + theirs
            else:
                sums[owner] = sums[owner] + value
        sums = [jnp.sum(part.T, axis=0, keepdims=True) for part in sums]
        for model in range(models):
            squared[model:model + 1, pl.ds(start, LANES)] = sums[model]
        diagonal[:, pl.ds(start, LANES)] = functools.reduce(jnp.add, sums)
        return carry

    lax.fori_loop(0, width // LANES, norm_rows, 0, unroll=4 if riding else 1)

    finish(2)
    over_features(weights, tokens, values)
    picked = []
    for tile, owner in enumerate(owners):
        lanes = slice(tile * LANES, (tile + 1) * LANES)
        if owner < 0:
            picked.append(jnp.where(second[:, lanes] > 0, values[columns:2 * columns, lanes], values[:columns, lanes]))
        else:
            picked.append(values[owner * columns:(owner + 1) * columns, lanes])
    outputs[...] = jnp.concatenate(picked, axis=1).astype(jnp.bfloat16)

    nothing = jnp.zeros((columns, 1), jnp.float32)
    both = values.at[:2 * columns]

    def total(value):
        return jnp.sum(value, axis=1, keepdims=True)

    norm_now, weighted = nothing, nothing
    both[...] = jnp.zeros(both.shape, jnp.float32)
    for start in range(0, width, CHUNK):
        part = slice(start, start + CHUNK)
        diagonal_part = jnp.zeros((columns, CHUNK), jnp.float32)
        for model in range(models):
            rows = weights[model * columns:(model + 1) * columns, part].astype(jnp.float32)
            diagonal_part = diagonal_part + squared[model:model + 1, part] * rows
        right = MIXING * over_tokens(outputs, tokens, part) + (1.0 - MIXING) * diagonal_part
        residual[:, part] = right
        direction[:, part] = jnp.zeros_like(right)
        merged[:, part] = jnp.zeros_like(right)
        norm_now = norm_now + total(right * right)
        weighted = weighted + total(diagonal[:, part] * right * right)
        add_over_features(two_terms(right), tokens, part, both)
    kept[...] = both[:columns] + both[columns:]

    def step_of(norm_now, weighted):
        curvature = MIXING * total(kept[...] * kept[...]) + (1.0 - MIXING) * weighted
        return norm_now / curvature

    def iterate(_, carry):
        scale, norm_now, weighted = carry
        step_size = step_of(norm_now, weighted)
        seen[...] = two_terms(kept[...])
        both[...] = jnp.zeros(both.shape, jnp.float32)
        norm_next, by_residual, by_both = nothing, nothing, nothing
        for start in range(0, width, CHUNK):
            part = slice(start, start + CHUNK)
            product = over_tokens(seen, tokens, part)
            along = residual[:, part] + scale * direction[:, part]
            direction[:, part] = along
            image = MIXING * (product[:columns] + product[columns:]) + (1.0 - MIXING) * diagonal[:, part] * along
            merged[:, part] = merged[:, part] + step_size * along
            value = residual[:, part] - step_size * image
            residual[:, part] = value
            norm_next = norm_next + total(value * value)
            scaled = diagonal[:, part] * value
            by_residual = by_residual + total(scaled * value)
            by_both = by_both + total(scaled * along)
            add_over_features(two_terms(value), tokens, part, both)
        scale = norm_next / norm_now
        kept[...] = both[:columns] + both[columns:] + scale * kept[...]
        weighted = by_residual + 2.0 * scale * by_both + scale * scale * weighted
        return scale, norm_next, weighted

    scale, norm_now, weighted = lax.fori_loop(0, ITERS - 1, iterate, (nothing, norm_now, weighted))
    step_size = step_of(norm_now, weighted)
    for start in range(0, width, CHUNK):
        part = slice(start, start + CHUNK)
        along = residual[:, part] + scale * direction[:, part]
        merged[:, part] = merged[:, part] + step_size * along
    for number, out_ref in enumerate(out_refs):
        sub_rows = out_ref.shape[1]
        if len(out_refs) > 1:
            flip = NEAR_FIRST[number]
            sub_block = (row ^ flip // 2) * 2 + (tok ^ flip % 2)
            start = pl.multiple_of(sub_block * sub_rows, LANES)
            out_ref[...] = merged[:, pl.ds(start, sub_rows)].astype(out_ref.dtype)
        else:
            out_ref[...] = merged[...].astype(out_ref.dtype)


def three_terms(value):
    high = value.astype(jnp.bfloat16).astype(jnp.float32)
    rest = value - high
    middle = rest.astype(jnp.bfloat16).astype(jnp.float32)
    return [high, middle, rest - middle]


def piece_kernel(lengths_ref, features_ref, given_ref, gains_ref, upper_ref, lower_ref, extra):
    block, slots = features_ref.shape
    half, quarter = slots // 2, slots // 4
    tok = lax.axis_index("tok")
    first = tok == 0
    lower = features_ref[:, half:half + quarter].astype(jnp.float32)
    given = given_ref[...].astype(jnp.float32)
    row = lax.broadcasted_iota(jnp.int32, (quarter, quarter), 0)
    lane = lax.broadcasted_iota(jnp.int32, (quarter, quarter), 1)
    mirror = jnp.where(row + lane == quarter - 1, 1.0, 0.0).astype(jnp.bfloat16)
    turned = jnp.dot(
        jnp.where(first, given, lower).astype(jnp.bfloat16), mirror, preferred_element_type=jnp.float32
    )
    place = lax.broadcasted_iota(jnp.int32, (block, quarter), 1) + tok * quarter
    mixed = jnp.where(place >= lengths_ref[0] - half, turned, jnp.where(first, lower, given))
    kept = features_ref[:, :half]
    cut = block - lower_ref.shape[0]
    upper_ref[:cut, :half] = kept[:cut]
    upper_ref[:cut, half:] = mixed[:cut].astype(jnp.bfloat16)
    lower_ref[:, :half] = kept[cut:]
    lower_ref[:, half:] = mixed[cut:].astype(jnp.bfloat16)
    kept = kept.astype(jnp.float32)
    extra[...] = jnp.zeros_like(extra)
    for number, value in enumerate(three_terms(jnp.sum(kept * kept, axis=0, keepdims=True))):
        extra[number:number + 1, :half] = value
    for number, value in enumerate(three_terms(jnp.sum(mixed * mixed, axis=0, keepdims=True))):
        extra[number:number + 1, half:] = value
    for number, value in enumerate(three_terms(gains_ref[...])):
        extra[3 + number:4 + number, :block] = value
    upper_ref[cut:, :] = extra[...].astype(jnp.bfloat16)


def send_kernel(weights_ref, own_ref, other_ref, turned):
    row, tok = lax.axis_index("row"), lax.axis_index("tok")
    for start in range(0, weights_ref.shape[1], LANES):
        value = weights_ref[:, start:start + LANES].astype(jnp.float32)
        turned[start:start + LANES, :] = value.T.astype(jnp.bfloat16)
    rows, held, _ = own_ref.shape
    for flip in range(rows):
        for out_ref, core in ((own_ref, tok), (other_ref, 1 - tok)):
            start = pl.multiple_of(((row ^ flip) * 2 + core) * held, held)
            out_ref[flip] = turned[pl.ds(start, held), :]


def packed_rows(lower, width):
    return -(-lower.shape[0] // (width // lower.shape[1]) // 16) * 16


def join_kernel(own_ref, given_ref, lower_ref, *refs):
    _, held, width = own_ref.shape
    rows, lanes = lower_ref.shape
    high = packed_rows(lower_ref, width)
    for flip, out_ref in enumerate(refs):
        out_ref[:held] = own_ref[flip]
        out_ref[held:2 * held] = given_ref[flip]
        if flip:
            out_ref[2 * held:] = jnp.zeros((high, width), out_ref.dtype)
            for number, start in enumerate(range(0, rows, high)):
                size = min(high, rows - start)
                out_ref[2 * held:2 * held + size, number * lanes:(number + 1) * lanes] = lower_ref[start:start + size]


def plane_kernel(lower_ref, *refs):
    out_ref = refs[-1]
    rows, lanes = lower_ref.shape
    out_ref[0] = lower_ref[...]
    for flip, found in enumerate(refs[:-1]):
        high = packed_rows(lower_ref, found.shape[1])
        base = found.shape[0] - high
        for number, start in enumerate(range(0, rows, high)):
            size = min(high, rows - start)
            out_ref[flip + 1, start:start + size] = found[base:base + size, number * lanes:(number + 1) * lanes]


def gather_kernel(*refs):
    out_ref, ordered = refs[-2:]
    row, tok = lax.axis_index("row"), lax.axis_index("tok")
    for flip, piece in zip(NEAR_FIRST, refs[:-2]):
        held = piece.shape[0]
        start = pl.multiple_of(((row ^ flip // 2) * 2 + (tok ^ flip % 2)) * held, held)
        ordered[pl.ds(start, held), :] = piece[...].astype(jnp.float32)
    for start in range(0, out_ref.shape[1], LANES):
        out_ref[:, start:start + LANES] = ordered[start:start + LANES, :].T


def body(hidden, gains, weights, lengths):
    rows = lax.axis_size("row")
    cols = lax.axis_size("col")
    toks = lax.axis_size("tok")
    slots, block = hidden.shape
    width = block * rows * cols
    models = toks * gains.shape[0]
    row_width, col_width = weights.shape[1:]
    columns = col_width // (rows * toks)
    sub_rows = row_width // toks
    features = hidden.T
    paired = toks == 2 and rows == 4
    any_space = pl.BlockSpec(memory_space=pl.ANY)
    small = pltpu.CompilerParams(vmem_limit_bytes=10 << 20)
    scalars = pl.BlockSpec(memory_space=pltpu.SMEM)
    in_vmem = pl.BlockSpec(memory_space=pltpu.VMEM)

    def swap(value, flip):
        pairs = [
            (t * rows + r, (t ^ flip % 2) * rows + (r ^ flip // 2)) for t in range(toks) for r in range(rows)
        ]
        return lax.ppermute(value, ("tok", "row"), pairs)

    if paired:
        half, quarter = slots // 2, slots // 4
        held = half + quarter
        given = swap(features[:, held:], 1)
        own, other = pl.pallas_call(
            send_kernel,
            out_shape=[jax.ShapeDtypeStruct((rows, columns, row_width), jnp.bfloat16)] * 2,
            in_specs=[in_vmem],
            out_specs=[in_vmem] * 2,
            scratch_shapes=[pltpu.VMEM((col_width, row_width), jnp.bfloat16)],
            compiler_params=small,
        )(weights[0])
        cut = block * 7 // 10
        upper, lower = pl.pallas_call(
            piece_kernel,
            out_shape=[
                jax.ShapeDtypeStruct((cut + 16, held), jnp.bfloat16),
                jax.ShapeDtypeStruct((block - cut, held), jnp.bfloat16),
            ],
            in_specs=[scalars, in_vmem, in_vmem, in_vmem],
            out_specs=[in_vmem] * 2,
            scratch_shapes=[pltpu.VMEM((16, held), jnp.float32)],
            compiler_params=small,
        )(lengths, features, given, gains)
        packed = packed_rows(lower, row_width)
        joined = pl.pallas_call(
            join_kernel,
            out_shape=[
                jax.ShapeDtypeStruct((toks * columns + (packed if flip else 0), row_width), jnp.bfloat16)
                for flip in range(rows)
            ],
            in_specs=[in_vmem] * 3,
            out_specs=[in_vmem] * rows,
            compiler_params=small,
        )(own, swap(other, 1), lower)
        line = [upper] + [
            lax.ppermute(upper, "col", [(i, (i + shift) % cols) for i in range(cols)]) for shift in range(1, cols)
        ]
        weight_pieces = [swap(value, 2 * flip) if flip else value for flip, value in enumerate(joined)]
        places = list(range(rows))
        line, weight_pieces = lax.optimization_barrier((line, weight_pieces))
        plane = pl.pallas_call(
            plane_kernel,
            out_shape=jax.ShapeDtypeStruct((rows,) + lower.shape, jnp.bfloat16),
            in_specs=[in_vmem] * rows,
            out_specs=in_vmem,
            compiler_params=small,
        )(lower, *weight_pieces[1:])
        up = [(i, (i + 1) % cols) for i in range(cols)]
        value = jnp.stack(line)
        by_near, by_far = swap(value, 2), swap(value, 4)
        middle = cut // 2
        crossed = [
            (0, 0, value), (1, 0, by_near), (2, 0, by_far),
            (3, 0, swap(by_far[:, :middle], 2)), (3, middle, swap(by_near[:, middle:], 4)),
        ]
        middle = plane.shape[1] // 2
        rounds = [plane]
        halves = [plane[:, :middle], plane[:, middle:]]
        for _ in range(cols - 1):
            halves = [lax.ppermute(value, "col", up) for value in halves]
            rounds.append(jnp.concatenate(halves, axis=1))
        pieces, copies = [], []
        for flip, first, found in crossed:
            high = min(first + found.shape[1], cut) - first
            for part, arrived in enumerate((found, swap(found, 1))):
                pieces.append(arrived)
                copies.append([(i, (flip, i), part, held, first, high) for i in range(cols)])
        for back, found in enumerate(rounds):
            for part, arrived in enumerate((found, swap(found, 1))):
                pieces.append(arrived)
                copies.append([(flip, (flip, back), part, held, cut, block - cut) for flip in range(rows)])
        owners = (0, 0, -1, 1, 1, -1)
        small_inputs = []
    else:
        sent = weights[0].T.reshape(rows * toks, columns, row_width)
        own_weights = lax.all_to_all(sent, ("row", "tok"), 0, 0, tiled=True)
        own_weights = own_weights.reshape(rows, models * columns, row_width)
        weight_pieces = [own_weights.transpose(1, 0, 2).reshape(models * columns, width)]
        places = [(0, 0)]
        held = slots
        everything = lax.all_gather(features, ("row", "col"), axis=0, tiled=False)
        pieces = [lax.all_gather(everything, "tok", axis=0, tiled=True)]
        tiles = slots // LANES
        owners = tuple(m for m in range(models) for _ in range(tiles))
        copies = [[
            (m * rows * cols + b, b, m, slots, 0, block) for m in range(models) for b in range(rows * cols)
        ]]
        live = jnp.arange(slots, dtype=jnp.int32)[None, :] < lengths[:, None]
        floats = features.astype(jnp.float32)
        squares = lax.psum(jnp.sum(floats * floats, axis=0), ("row", "col"))
        every_gain = lax.all_gather(gains[0], ("row", "col"), axis=0, tiled=True)
        small_inputs = [
            live.reshape(1, -1).astype(jnp.float32),
            lax.all_gather(squares, "tok", axis=0, tiled=True)[None, :],
            lax.all_gather(every_gain, "tok", axis=0, tiled=False).T,
        ]
    slots_held = toks * held

    if paired:
        out_shape = [jax.ShapeDtypeStruct((columns, sub_rows), jnp.bfloat16)] * (rows * toks)
    else:
        out_shape = [jax.ShapeDtypeStruct((columns, width), jnp.bfloat16)]
    found = pl.pallas_call(
        functools.partial(solve_kernel, owners, models, block, copies, places),
        out_shape=out_shape,
        in_specs=[scalars] + [in_vmem] * len(small_inputs) + [any_space] * (len(pieces) + len(weight_pieces)),
        out_specs=[in_vmem] * len(out_shape),
        scratch_shapes=[
            pltpu.VMEM((width, slots_held), jnp.bfloat16),
            pltpu.VMEM((models * columns, width), jnp.bfloat16),
            pltpu.VMEM((models, width), jnp.float32),
            pltpu.VMEM((1, width), jnp.float32),
            pltpu.VMEM((columns, width), jnp.float32),
            pltpu.VMEM((columns, width), jnp.float32),
            pltpu.VMEM((columns, width), jnp.float32),
            pltpu.VMEM((columns, slots_held), jnp.float32),
            pltpu.VMEM((max(models, 2) * columns, slots_held), jnp.float32),
            pltpu.VMEM((columns, slots_held), jnp.bfloat16),
            pltpu.VMEM((2 * columns, slots_held), jnp.bfloat16),
            pltpu.VMEM((models * rows * cols, 16, slots_held // models) if paired else (8, 16, LANES), jnp.bfloat16),
            pltpu.VMEM((width if paired else 8, LANES), jnp.float32),
            pltpu.SemaphoreType.DMA((3,)),
        ],
        compiler_params=pltpu.CompilerParams(vmem_limit_bytes=width * slots_held * 2 + (18 << 20)),
    )(
        lengths,
        *small_inputs,
        *pieces,
        *weight_pieces,
    )
    if paired:
        arrived = [found[0]] + [swap(x, flip) for x, flip in zip(found[1:], NEAR_FIRST[1:])]
        return pl.pallas_call(
            gather_kernel,
            out_shape=jax.ShapeDtypeStruct((sub_rows, col_width), jnp.float32),
            in_specs=[in_vmem] * len(arrived),
            out_specs=in_vmem,
            scratch_shapes=[pltpu.VMEM((col_width, sub_rows), jnp.float32)],
            compiler_params=small,
        )(*arrived)
    found = found[0].reshape(columns, rows * toks, sub_rows).transpose(1, 0, 2)
    back = lax.all_to_all(found, ("row", "tok"), 0, 0, tiled=True)
    return back.reshape(col_width, sub_rows).T.astype(jnp.float32)


def solution(mesh):
    return jax.shard_map(
        body,
        mesh=mesh,
        in_specs=(P("tok", ("row", "col")), P("tok", ("row", "col")), P("tok", "row", "col"), P()),
        out_specs=P(("row", "tok"), "col"),
        check_vma=False,
    )
```

```python
import functools

import jax
import jax.numpy as jnp
from jax import lax
from jax.experimental import pallas as pl
from jax.experimental.pallas import tpu as pltpu
from jax.sharding import PartitionSpec as P

ITERS = 4

MIXING = 0.9
EPSILON = 1e-06

LANES = 128
CHUNK = 1024
MOST_TOKENS = 1024
NEAR_FIRST = (0, 2, 4, 6, 3, 5, 7, 1)


def two_terms(value):
    high = value.astype(jnp.bfloat16).astype(jnp.float32)
    return jnp.concatenate([high, value - high], axis=0).astype(jnp.bfloat16)


def over_features(left, tokens, found):
    slots = tokens.shape[1]
    if slots <= MOST_TOKENS:
        found[...] = jnp.dot(left[...], tokens[...], preferred_element_type=jnp.float32)
        return

    def some(step, carry):
        lanes = pl.ds(pl.multiple_of(step * CHUNK, CHUNK), CHUNK)
        found[:, lanes] = jnp.dot(left[...], tokens[:, lanes], preferred_element_type=jnp.float32)
        return carry

    lax.fori_loop(0, slots // CHUNK, some, 0)


def over_tokens(left, tokens, part):
    slots = tokens.shape[1]
    product = functools.partial(
        lax.dot_general, dimension_numbers=(((1,), (1,)), ((), ())), preferred_element_type=jnp.float32
    )
    if slots <= MOST_TOKENS:
        return product(left[...], tokens[part, :])

    def some(step, total):
        lanes = pl.ds(pl.multiple_of(step * CHUNK, CHUNK), CHUNK)
        return total + product(left[:, lanes], tokens[part, lanes])

    return lax.fori_loop(0, slots // CHUNK, some, jnp.zeros((left.shape[0], CHUNK), jnp.float32))


def in_pair_order(lengths_ref, width):
    half, quarter = width // 3, width // 6
    lane = lax.broadcasted_iota(jnp.int32, (1, width), 1)
    part = jnp.where(lane >= width // 2, 1, 0)
    spot = lane - part * (width // 2)
    place = spot - half + part * quarter
    late = spot >= half
    second = jnp.where(late, jnp.where(place >= lengths_ref[0] - half, 1, 0), part)
    position = jnp.where(late, jnp.where(second == 1, 2 * half - 1 - place, half + place), spot)
    length = jnp.where(second == 1, lengths_ref[1], lengths_ref[0])
    return jnp.where(position < length, 1.0, 0.0), second.astype(jnp.float32)


def solve_kernel(owners, models, block, copies, places, lengths_ref, *refs):
    riding = len(copies) > 1
    if not riding:
        live_ref, squares_ref, gains_ref, refs = refs[0], refs[1], refs[2], refs[3:]
    pieces = refs[:len(copies)]
    weight_pieces = refs[len(copies):len(copies) + len(places)]
    out_refs = refs[len(copies) + len(places):-14]
    (tokens, weights, squared, diagonal, residual, direction, merged, terms, values, outputs, seen, extras, gains_held,
     sems) = refs[-14:]
    width, slots = tokens.shape
    columns = residual.shape[0]
    blocks = width // block
    started = [[], [], []]

    def begin(source, target, kind):
        copy = pltpu.make_async_copy(source, target, sems.at[kind])
        copy.start()
        started[kind].append(copy)

    def finish(kind):
        for copy in started[kind]:
            copy.wait()

    if riding:
        row, tok = lax.axis_index("row"), lax.axis_index("tok")
        cols = lax.axis_size("col")
    moves = []
    for piece, parts in zip(pieces, copies):
        for source, entry, part, lanes, first, held in parts:
            if riding:
                flip, back = entry
                entry = (row ^ flip) * cols + back
                part = tok ^ part
            moves.append((piece, source, entry, part, lanes, first, held))
    for piece, source, entry, part, lanes, first, held in moves:
        if piece.shape[1] > held:
            begin(piece.at[source, pl.ds(held, 16)], extras.at[part * blocks + entry], 0)
    for piece, source, entry, part, lanes, first, held in moves:
        start = pl.multiple_of(entry * block + first, 16)
        lane = pl.multiple_of(part * lanes, LANES)
        begin(piece.at[source, pl.ds(0, held)], tokens.at[pl.ds(start, held), pl.ds(lane, lanes)], 1)
    for piece, place in zip(weight_pieces, places):
        if riding:
            row_width = piece.shape[1]
            lane = pl.multiple_of((row ^ place) * row_width, LANES)
            for part in range(2):
                high = pl.multiple_of((tok ^ part) * columns, columns)
                begin(
                    piece.at[pl.ds(part * columns, columns)],
                    weights.at[pl.ds(high, columns), pl.ds(lane, row_width)],
                    2,
                )
        else:
            begin(piece, weights, 2)
    finish(0)

    if riding:
        every = extras[...].astype(jnp.float32)
        sums = [jnp.sum(every[part * blocks:(part + 1) * blocks], axis=0) for part in range(models)]
        squares = jnp.concatenate([x[0:1] + x[1:2] + x[2:3] for x in sums], axis=1)
        turned = (every[:, 3] + every[:, 4] + every[:, 5]).T[:block]
        lane = lax.broadcasted_iota(jnp.int32, turned.shape, 1)
        side = lax.broadcasted_iota(jnp.int32, (block, LANES), 1)

        def hold_gains(step, carry):
            gain = [
                jnp.sum(jnp.where(lane == part * blocks + step, turned, 0.0), axis=1, keepdims=True)
                for part in range(models)
            ]
            gains_held[pl.ds(pl.multiple_of(step * block, block), block), :] = jnp.where(side == 0, gain[0], gain[1])
            return carry

        lax.fori_loop(0, blocks, hold_gains, 0)
        gains_ref = gains_held
        live, second = in_pair_order(lengths_ref, slots)
    else:
        squares, live = squares_ref[...], live_ref[...]
    inverse_rms = lax.rsqrt(squares / width + EPSILON) * live
    finish(1)

    def norm_rows(step, carry):
        start = pl.multiple_of(step * LANES, LANES)
        gains = gains_ref[pl.ds(start, LANES), :]
        sums = [jnp.zeros((LANES, LANES), jnp.float32) for _ in range(models)]
        for tile, owner in enumerate(owners):
            lanes = slice(tile * LANES, (tile + 1) * LANES)
            value = tokens[pl.ds(start, LANES), lanes].astype(jnp.float32)
            if owner < 0:
                gain = jnp.where(second[:, lanes] > 0, gains[:, 1:2], gains[:, 0:1])
            else:
                gain = gains[:, owner:owner + 1]
            normed = (value * inverse_rms[:, lanes] * gain).astype(jnp.bfloat16)
            tokens[pl.ds(start, LANES), lanes] = normed
            value = normed.astype(jnp.float32)
            value = value * value
            if owner < 0:
                theirs = value * second[:, lanes]
                sums[0] = sums[0] + (value - theirs)
                sums[1] = sums[1] + theirs
            else:
                sums[owner] = sums[owner] + value
        sums = [jnp.sum(part.T, axis=0, keepdims=True) for part in sums]
        for model in range(models):
            squared[model:model + 1, pl.ds(start, LANES)] = sums[model]
        diagonal[:, pl.ds(start, LANES)] = functools.reduce(jnp.add, sums)
        return carry

    lax.fori_loop(0, width // LANES, norm_rows, 0, unroll=4 if riding else 1)

    finish(2)
    over_features(weights, tokens, values)
    picked = []
    for tile, owner in enumerate(owners):
        lanes = slice(tile * LANES, (tile + 1) * LANES)
        if owner < 0:
            picked.append(jnp.where(second[:, lanes] > 0, values[columns:2 * columns, lanes], values[:columns, lanes]))
        else:
            picked.append(values[owner * columns:(owner + 1) * columns, lanes])
    outputs[...] = jnp.concatenate(picked, axis=1).astype(jnp.bfloat16)

    norm_now = jnp.zeros((columns, 1), jnp.float32)
    for start in range(0, width, CHUNK):
        part = slice(start, start + CHUNK)
        weighted = jnp.zeros((columns, CHUNK), jnp.float32)
        for model in range(models):
            rows = weights[model * columns:(model + 1) * columns, part].astype(jnp.float32)
            weighted = weighted + squared[model:model + 1, part] * rows
        right = MIXING * over_tokens(outputs, tokens, part) + (1.0 - MIXING) * weighted
        residual[:, part] = right
        direction[:, part] = jnp.zeros_like(right)
        merged[:, part] = jnp.zeros_like(right)
        norm_now = norm_now + jnp.sum(right * right, axis=1, keepdims=True)

    def step_of(scale, norm_now):
        weighted = jnp.zeros((columns, 1), jnp.float32)
        for start in range(0, width, CHUNK):
            part = slice(start, start + CHUNK)
            value = residual[:, part] + scale * direction[:, part]
            direction[:, part] = value
            terms[:, part] = two_terms(value)
            weighted = weighted + jnp.sum(diagonal[:, part] * value * value, axis=1, keepdims=True)
        both = values.at[:2 * columns]
        over_features(terms, tokens, both)
        both = both[:columns] + both[columns:]
        seen[...] = two_terms(both)
        curvature = MIXING * jnp.sum(both * both, axis=1, keepdims=True) + (1.0 - MIXING) * weighted
        return norm_now / curvature

    def iterate(_, carry):
        scale, norm_now = carry
        step_size = step_of(scale, norm_now)
        norm_next = jnp.zeros((columns, 1), jnp.float32)
        for start in range(0, width, CHUNK):
            part = slice(start, start + CHUNK)
            both = over_tokens(seen, tokens, part)
            along = direction[:, part]
            image = MIXING * (both[:columns] + both[columns:]) + (1.0 - MIXING) * diagonal[:, part] * along
            merged[:, part] = merged[:, part] + step_size * along
            value = residual[:, part] - step_size * image
            residual[:, part] = value
            norm_next = norm_next + jnp.sum(value * value, axis=1, keepdims=True)
        return norm_next / norm_now, norm_next

    scale, norm_now = lax.fori_loop(0, ITERS - 1, iterate, (jnp.zeros((columns, 1), jnp.float32), norm_now))
    step_size = step_of(scale, norm_now)
    merged[...] = merged[...] + step_size * direction[...]
    for number, out_ref in enumerate(out_refs):
        sub_rows = out_ref.shape[1]
        if len(out_refs) > 1:
            flip = NEAR_FIRST[number]
            sub_block = (row ^ flip // 2) * 2 + (tok ^ flip % 2)
            start = pl.multiple_of(sub_block * sub_rows, LANES)
            out_ref[...] = merged[:, pl.ds(start, sub_rows)].astype(out_ref.dtype)
        else:
            out_ref[...] = merged[...].astype(out_ref.dtype)


def three_terms(value):
    high = value.astype(jnp.bfloat16).astype(jnp.float32)
    rest = value - high
    middle = rest.astype(jnp.bfloat16).astype(jnp.float32)
    return [high, middle, rest - middle]


def piece_kernel(lengths_ref, features_ref, given_ref, gains_ref, upper_ref, lower_ref, extra):
    block, slots = features_ref.shape
    half, quarter = slots // 2, slots // 4
    tok = lax.axis_index("tok")
    first = tok == 0
    lower = features_ref[:, half:half + quarter].astype(jnp.float32)
    given = given_ref[...].astype(jnp.float32)
    row = lax.broadcasted_iota(jnp.int32, (quarter, quarter), 0)
    lane = lax.broadcasted_iota(jnp.int32, (quarter, quarter), 1)
    mirror = jnp.where(row + lane == quarter - 1, 1.0, 0.0).astype(jnp.bfloat16)
    turned = jnp.dot(
        jnp.where(first, given, lower).astype(jnp.bfloat16), mirror, preferred_element_type=jnp.float32
    )
    place = lax.broadcasted_iota(jnp.int32, (block, quarter), 1) + tok * quarter
    mixed = jnp.where(place >= lengths_ref[0] - half, turned, jnp.where(first, lower, given))
    kept = features_ref[:, :half]
    cut = block - lower_ref.shape[0]
    upper_ref[:cut, :half] = kept[:cut]
    upper_ref[:cut, half:] = mixed[:cut].astype(jnp.bfloat16)
    lower_ref[:, :half] = kept[cut:]
    lower_ref[:, half:] = mixed[cut:].astype(jnp.bfloat16)
    kept = kept.astype(jnp.float32)
    extra[...] = jnp.zeros_like(extra)
    for number, value in enumerate(three_terms(jnp.sum(kept * kept, axis=0, keepdims=True))):
        extra[number:number + 1, :half] = value
    for number, value in enumerate(three_terms(jnp.sum(mixed * mixed, axis=0, keepdims=True))):
        extra[number:number + 1, half:] = value
    for number, value in enumerate(three_terms(gains_ref[...])):
        extra[3 + number:4 + number, :block] = value
    upper_ref[cut:, :] = extra[...].astype(jnp.bfloat16)


def send_kernel(weights_ref, own_ref, other_ref, turned):
    row, tok = lax.axis_index("row"), lax.axis_index("tok")
    for start in range(0, weights_ref.shape[1], LANES):
        value = weights_ref[:, start:start + LANES].astype(jnp.float32)
        turned[start:start + LANES, :] = value.T.astype(jnp.bfloat16)
    rows, held, _ = own_ref.shape
    for flip in range(rows):
        for out_ref, core in ((own_ref, tok), (other_ref, 1 - tok)):
            start = pl.multiple_of(((row ^ flip) * 2 + core) * held, held)
            out_ref[flip] = turned[pl.ds(start, held), :]


def packed_rows(lower, width):
    return -(-lower.shape[0] // (width // lower.shape[1]) // 16) * 16


def join_kernel(own_ref, given_ref, lower_ref, *refs):
    _, held, width = own_ref.shape
    rows, lanes = lower_ref.shape
    high = packed_rows(lower_ref, width)
    for flip, out_ref in enumerate(refs):
        out_ref[:held] = own_ref[flip]
        out_ref[held:2 * held] = given_ref[flip]
        if flip:
            out_ref[2 * held:] = jnp.zeros((high, width), out_ref.dtype)
            for number, start in enumerate(range(0, rows, high)):
                size = min(high, rows - start)
                out_ref[2 * held:2 * held + size, number * lanes:(number + 1) * lanes] = lower_ref[start:start + size]


def plane_kernel(lower_ref, *refs):
    out_ref = refs[-1]
    rows, lanes = lower_ref.shape
    out_ref[0] = lower_ref[...]
    for flip, found in enumerate(refs[:-1]):
        high = packed_rows(lower_ref, found.shape[1])
        base = found.shape[0] - high
        for number, start in enumerate(range(0, rows, high)):
            size = min(high, rows - start)
            out_ref[flip + 1, start:start + size] = found[base:base + size, number * lanes:(number + 1) * lanes]


def gather_kernel(*refs):
    out_ref, ordered = refs[-2:]
    row, tok = lax.axis_index("row"), lax.axis_index("tok")
    for flip, piece in zip(NEAR_FIRST, refs[:-2]):
        held = piece.shape[0]
        start = pl.multiple_of(((row ^ flip // 2) * 2 + (tok ^ flip % 2)) * held, held)
        ordered[pl.ds(start, held), :] = piece[...].astype(jnp.float32)
    for start in range(0, out_ref.shape[1], LANES):
        out_ref[:, start:start + LANES] = ordered[start:start + LANES, :].T


def body(hidden, gains, weights, lengths):
    rows = lax.axis_size("row")
    cols = lax.axis_size("col")
    toks = lax.axis_size("tok")
    slots, block = hidden.shape
    width = block * rows * cols
    models = toks * gains.shape[0]
    row_width, col_width = weights.shape[1:]
    columns = col_width // (rows * toks)
    sub_rows = row_width // toks
    features = hidden.T
    paired = toks == 2 and rows == 4
    any_space = pl.BlockSpec(memory_space=pl.ANY)
    small = pltpu.CompilerParams(vmem_limit_bytes=10 << 20)
    scalars = pl.BlockSpec(memory_space=pltpu.SMEM)
    in_vmem = pl.BlockSpec(memory_space=pltpu.VMEM)

    def swap(value, flip):
        pairs = [
            (t * rows + r, (t ^ flip % 2) * rows + (r ^ flip // 2)) for t in range(toks) for r in range(rows)
        ]
        return lax.ppermute(value, ("tok", "row"), pairs)

    if paired:
        half, quarter = slots // 2, slots // 4
        held = half + quarter
        given = swap(features[:, held:], 1)
        own, other = pl.pallas_call(
            send_kernel,
            out_shape=[jax.ShapeDtypeStruct((rows, columns, row_width), jnp.bfloat16)] * 2,
            in_specs=[in_vmem],
            out_specs=[in_vmem] * 2,
            scratch_shapes=[pltpu.VMEM((col_width, row_width), jnp.bfloat16)],
            compiler_params=small,
        )(weights[0])
        cut = block * 7 // 10
        upper, lower = pl.pallas_call(
            piece_kernel,
            out_shape=[
                jax.ShapeDtypeStruct((cut + 16, held), jnp.bfloat16),
                jax.ShapeDtypeStruct((block - cut, held), jnp.bfloat16),
            ],
            in_specs=[scalars, in_vmem, in_vmem, in_vmem],
            out_specs=[in_vmem] * 2,
            scratch_shapes=[pltpu.VMEM((16, held), jnp.float32)],
            compiler_params=small,
        )(lengths, features, given, gains)
        packed = packed_rows(lower, row_width)
        joined = pl.pallas_call(
            join_kernel,
            out_shape=[
                jax.ShapeDtypeStruct((toks * columns + (packed if flip else 0), row_width), jnp.bfloat16)
                for flip in range(rows)
            ],
            in_specs=[in_vmem] * 3,
            out_specs=[in_vmem] * rows,
            compiler_params=small,
        )(own, swap(other, 1), lower)
        value = lax.all_gather(upper, "col", axis=0, tiled=False)
        weight_pieces = [swap(value, 2 * flip) if flip else value for flip, value in enumerate(joined)]
        places = list(range(rows))
        value, weight_pieces = lax.optimization_barrier((value, weight_pieces))
        plane = pl.pallas_call(
            plane_kernel,
            out_shape=jax.ShapeDtypeStruct((rows,) + lower.shape, jnp.bfloat16),
            in_specs=[in_vmem] * rows,
            out_specs=in_vmem,
            compiler_params=small,
        )(lower, *weight_pieces[1:])
        by_near, by_far = swap(value, 2), swap(value, 4)
        middle = cut // 2
        crossed = [
            (0, 0, value), (1, 0, by_near), (2, 0, by_far),
            (3, 0, swap(by_far[:, :middle], 2)), (3, middle, swap(by_near[:, middle:], 4)),
        ]
        rounds = lax.all_gather(plane, "col", axis=0, tiled=False).reshape((cols * rows,) + lower.shape)
        pieces, copies = [], []
        for flip, first, found in crossed:
            high = min(first + found.shape[1], cut) - first
            for part, arrived in enumerate((found, swap(found, 1))):
                pieces.append(arrived)
                copies.append([(i, (flip, i), part, held, first, high) for i in range(cols)])
        for part, arrived in enumerate((rounds, swap(rounds, 1))):
            pieces.append(arrived)
            copies.append([
                (i, (i % rows, i // rows), part, held, cut, block - cut) for i in range(cols * rows)
            ])
        owners = (0, 0, -1, 1, 1, -1)
        small_inputs = []
    else:
        sent = weights[0].T.reshape(rows * toks, columns, row_width)
        own_weights = lax.all_to_all(sent, ("row", "tok"), 0, 0, tiled=True)
        own_weights = own_weights.reshape(rows, models * columns, row_width)
        weight_pieces = [own_weights.transpose(1, 0, 2).reshape(models * columns, width)]
        places = [(0, 0)]
        held = slots
        everything = lax.all_gather(features, ("row", "col"), axis=0, tiled=False)
        pieces = [lax.all_gather(everything, "tok", axis=0, tiled=True)]
        tiles = slots // LANES
        owners = tuple(m for m in range(models) for _ in range(tiles))
        copies = [[
            (m * rows * cols + b, b, m, slots, 0, block) for m in range(models) for b in range(rows * cols)
        ]]
        live = jnp.arange(slots, dtype=jnp.int32)[None, :] < lengths[:, None]
        floats = features.astype(jnp.float32)
        squares = lax.psum(jnp.sum(floats * floats, axis=0), ("row", "col"))
        every_gain = lax.all_gather(gains[0], ("row", "col"), axis=0, tiled=True)
        small_inputs = [
            live.reshape(1, -1).astype(jnp.float32),
            lax.all_gather(squares, "tok", axis=0, tiled=True)[None, :],
            lax.all_gather(every_gain, "tok", axis=0, tiled=False).T,
        ]
    slots_held = toks * held

    if paired:
        out_shape = [jax.ShapeDtypeStruct((columns, sub_rows), jnp.bfloat16)] * (rows * toks)
    else:
        out_shape = [jax.ShapeDtypeStruct((columns, width), jnp.bfloat16)]
    found = pl.pallas_call(
        functools.partial(solve_kernel, owners, models, block, copies, places),
        out_shape=out_shape,
        in_specs=[scalars] + [in_vmem] * len(small_inputs) + [any_space] * (len(pieces) + len(weight_pieces)),
        out_specs=[in_vmem] * len(out_shape),
        scratch_shapes=[
            pltpu.VMEM((width, slots_held), jnp.bfloat16),
            pltpu.VMEM((models * columns, width), jnp.bfloat16),
            pltpu.VMEM((models, width), jnp.float32),
            pltpu.VMEM((1, width), jnp.float32),
            pltpu.VMEM((columns, width), jnp.float32),
            pltpu.VMEM((columns, width), jnp.float32),
            pltpu.VMEM((columns, width), jnp.float32),
            pltpu.VMEM((2 * columns, width), jnp.bfloat16),
            pltpu.VMEM((max(models, 2) * columns, slots_held), jnp.float32),
            pltpu.VMEM((columns, slots_held), jnp.bfloat16),
            pltpu.VMEM((2 * columns, slots_held), jnp.bfloat16),
            pltpu.VMEM((models * rows * cols, 16, slots_held // models) if paired else (8, 16, LANES), jnp.bfloat16),
            pltpu.VMEM((width if paired else 8, LANES), jnp.float32),
            pltpu.SemaphoreType.DMA((3,)),
        ],
        compiler_params=pltpu.CompilerParams(vmem_limit_bytes=width * slots_held * 2 + (18 << 20)),
    )(
        lengths,
        *small_inputs,
        *pieces,
        *weight_pieces,
    )
    if paired:
        arrived = [found[0]] + [swap(x, flip) for x, flip in zip(found[1:], NEAR_FIRST[1:])]
        return pl.pallas_call(
            gather_kernel,
            out_shape=jax.ShapeDtypeStruct((sub_rows, col_width), jnp.float32),
            in_specs=[in_vmem] * len(arrived),
            out_specs=in_vmem,
            scratch_shapes=[pltpu.VMEM((col_width, sub_rows), jnp.float32)],
            compiler_params=small,
        )(*arrived)
    found = found[0].reshape(columns, rows * toks, sub_rows).transpose(1, 0, 2)
    back = lax.all_to_all(found, ("row", "tok"), 0, 0, tiled=True)
    return back.reshape(col_width, sub_rows).T.astype(jnp.float32)


def solution(mesh):
    return jax.shard_map(
        body,
        mesh=mesh,
        in_specs=(P("tok", ("row", "col")), P("tok", ("row", "col")), P("tok", "row", "col"), P()),
        out_specs=P(("row", "tok"), "col"),
        check_vma=False,
    )
```

```python
import functools

import jax
import jax.numpy as jnp
from jax import lax
from jax.experimental import pallas as pl
from jax.experimental.pallas import tpu as pltpu
from jax.sharding import PartitionSpec as P

ITERS = 4

MIXING = 0.9
EPSILON = 1e-06

LANES = 128
CHUNK = 1024
MOST_TOKENS = 1024
NEAR_FIRST = (0, 2, 4, 6, 3, 5, 7, 1)


def two_terms(value):
    high = value.astype(jnp.bfloat16).astype(jnp.float32)
    return jnp.concatenate([high, value - high], axis=0).astype(jnp.bfloat16)


def add_over_features(left, tokens, part, found):
    slots = tokens.shape[1]
    if slots <= MOST_TOKENS:
        found[...] += jnp.dot(left, tokens[part, :], preferred_element_type=jnp.float32)
        return

    def some(step, carry):
        lanes = pl.ds(pl.multiple_of(step * CHUNK, CHUNK), CHUNK)
        found[:, lanes] += jnp.dot(left, tokens[part, lanes], preferred_element_type=jnp.float32)
        return carry

    lax.fori_loop(0, slots // CHUNK, some, 0)


def over_features(left, tokens, found):
    slots = tokens.shape[1]
    if slots <= MOST_TOKENS:
        found[...] = jnp.dot(left[...], tokens[...], preferred_element_type=jnp.float32)
        return

    def some(step, carry):
        lanes = pl.ds(pl.multiple_of(step * CHUNK, CHUNK), CHUNK)
        found[:, lanes] = jnp.dot(left[...], tokens[:, lanes], preferred_element_type=jnp.float32)
        return carry

    lax.fori_loop(0, slots // CHUNK, some, 0)


def over_tokens(left, tokens, part):
    slots = tokens.shape[1]
    product = functools.partial(
        lax.dot_general, dimension_numbers=(((1,), (1,)), ((), ())), preferred_element_type=jnp.float32
    )
    if slots <= MOST_TOKENS:
        return product(left[...], tokens[part, :])

    def some(step, total):
        lanes = pl.ds(pl.multiple_of(step * CHUNK, CHUNK), CHUNK)
        return total + product(left[:, lanes], tokens[part, lanes])

    return lax.fori_loop(0, slots // CHUNK, some, jnp.zeros((left.shape[0], CHUNK), jnp.float32))


def in_pair_order(lengths_ref, width):
    half, quarter = width // 3, width // 6
    lane = lax.broadcasted_iota(jnp.int32, (1, width), 1)
    part = jnp.where(lane >= width // 2, 1, 0)
    spot = lane - part * (width // 2)
    place = spot - half + part * quarter
    late = spot >= half
    second = jnp.where(late, jnp.where(place >= lengths_ref[0] - half, 1, 0), part)
    position = jnp.where(late, jnp.where(second == 1, 2 * half - 1 - place, half + place), spot)
    length = jnp.where(second == 1, lengths_ref[1], lengths_ref[0])
    return jnp.where(position < length, 1.0, 0.0), second.astype(jnp.float32)


def solve_kernel(owners, models, block, copies, places, lengths_ref, *refs):
    riding = len(copies) > 1
    if not riding:
        live_ref, squares_ref, gains_ref, refs = refs[0], refs[1], refs[2], refs[3:]
    pieces = refs[:len(copies)]
    weight_pieces = refs[len(copies):len(copies) + len(places)]
    out_refs = refs[len(copies) + len(places):-14]
    (tokens, weights, squared, diagonal, residual, direction, merged, terms, values, outputs, seen, extras, gains_held,
     sems) = refs[-14:]
    width, slots = tokens.shape
    columns = residual.shape[0]
    blocks = width // block
    started = [[], [], []]

    def begin(source, target, kind):
        copy = pltpu.make_async_copy(source, target, sems.at[kind])
        copy.start()
        started[kind].append(copy)

    def finish(kind):
        for copy in started[kind]:
            copy.wait()

    if riding:
        row, col, tok = lax.axis_index("row"), lax.axis_index("col"), lax.axis_index("tok")
        cols = lax.axis_size("col")
    moves = []
    for piece, parts in zip(pieces, copies):
        for source, entry, part, lanes, first, held in parts:
            if riding:
                flip, back = entry
                entry = (row ^ flip) * cols + lax.rem(col - back + cols, cols)
                part = tok ^ part
            moves.append((piece, source, entry, part, lanes, first, held))
    for piece, source, entry, part, lanes, first, held in moves:
        if piece.shape[1] > held:
            begin(piece.at[source, pl.ds(held, 16)], extras.at[part * blocks + entry], 0)
    for piece, source, entry, part, lanes, first, held in moves:
        start = pl.multiple_of(entry * block + first, 16)
        lane = pl.multiple_of(part * lanes, LANES)
        begin(piece.at[source, pl.ds(0, held)], tokens.at[pl.ds(start, held), pl.ds(lane, lanes)], 1)
    for piece, place in zip(weight_pieces, places):
        if riding:
            row_width = piece.shape[1]
            lane = pl.multiple_of((row ^ place) * row_width, LANES)
            for part in range(2):
                high = pl.multiple_of((tok ^ part) * columns, columns)
                begin(
                    piece.at[pl.ds(part * columns, columns)],
                    weights.at[pl.ds(high, columns), pl.ds(lane, row_width)],
                    2,
                )
        else:
            begin(piece, weights, 2)
    finish(0)

    if riding:
        every = extras[...].astype(jnp.float32)
        sums = [jnp.sum(every[part * blocks:(part + 1) * blocks], axis=0) for part in range(models)]
        squares = jnp.concatenate([x[0:1] + x[1:2] + x[2:3] for x in sums], axis=1)
        turned = (every[:, 3] + every[:, 4] + every[:, 5]).T[:block]
        lane = lax.broadcasted_iota(jnp.int32, turned.shape, 1)
        side = lax.broadcasted_iota(jnp.int32, (block, LANES), 1)

        def hold_gains(step, carry):
            gain = [
                jnp.sum(jnp.where(lane == part * blocks + step, turned, 0.0), axis=1, keepdims=True)
                for part in range(models)
            ]
            gains_held[pl.ds(pl.multiple_of(step * block, block), block), :] = jnp.where(side == 0, gain[0], gain[1])
            return carry

        lax.fori_loop(0, blocks, hold_gains, 0)
        gains_ref = gains_held
        live, second = in_pair_order(lengths_ref, slots)
    else:
        squares, live = squares_ref[...], live_ref[...]
    inverse_rms = lax.rsqrt(squares / width + EPSILON) * live
    finish(1)

    def norm_rows(start):
        gains = gains_ref[pl.ds(start, LANES), :]
        sums = [jnp.zeros((LANES, LANES), jnp.float32) for _ in range(models)]
        for tile, owner in enumerate(owners):
            lanes = slice(tile * LANES, (tile + 1) * LANES)
            value = tokens[pl.ds(start, LANES), lanes].astype(jnp.float32)
            if owner < 0:
                gain = jnp.where(second[:, lanes] > 0, gains[:, 1:2], gains[:, 0:1])
            else:
                gain = gains[:, owner:owner + 1]
            normed = (value * inverse_rms[:, lanes] * gain).astype(jnp.bfloat16)
            tokens[pl.ds(start, LANES), lanes] = normed
            value = normed.astype(jnp.float32)
            value = value * value
            if owner < 0:
                theirs = value * second[:, lanes]
                sums[0] = sums[0] + (value - theirs)
                sums[1] = sums[1] + theirs
            else:
                sums[owner] = sums[owner] + value
        sums = [jnp.sum(part.T, axis=0, keepdims=True) for part in sums]
        for model in range(models):
            squared[model:model + 1, pl.ds(start, LANES)] = sums[model]
        diagonal[:, pl.ds(start, LANES)] = functools.reduce(jnp.add, sums)

    def norm_and_multiply(step, carry):
        start = pl.multiple_of(step * 2 * LANES, 2 * LANES)
        for half in range(2):
            norm_rows(pl.multiple_of(start + half * LANES, LANES))
        rows = pl.ds(start, 2 * LANES)
        add_over_features(weights[:, rows], tokens, rows, values.at[:models * columns])
        return carry

    finish(2)
    values[...] = jnp.zeros_like(values)

    lax.fori_loop(0, width // (2 * LANES), norm_and_multiply, 0, unroll=2 if riding else 1)

    picked = []
    for tile, owner in enumerate(owners):
        lanes = slice(tile * LANES, (tile + 1) * LANES)
        if owner < 0:
            picked.append(jnp.where(second[:, lanes] > 0, values[columns:2 * columns, lanes], values[:columns, lanes]))
        else:
            picked.append(values[owner * columns:(owner + 1) * columns, lanes])
    outputs[...] = jnp.concatenate(picked, axis=1).astype(jnp.bfloat16)

    norm_now = jnp.zeros((columns, 1), jnp.float32)
    for start in range(0, width, CHUNK):
        part = slice(start, start + CHUNK)
        weighted = jnp.zeros((columns, CHUNK), jnp.float32)
        for model in range(models):
            rows = weights[model * columns:(model + 1) * columns, part].astype(jnp.float32)
            weighted = weighted + squared[model:model + 1, part] * rows
        right = MIXING * over_tokens(outputs, tokens, part) + (1.0 - MIXING) * weighted
        residual[:, part] = right
        direction[:, part] = jnp.zeros_like(right)
        merged[:, part] = jnp.zeros_like(right)
        norm_now = norm_now + jnp.sum(right * right, axis=1, keepdims=True)

    def step_of(scale, norm_now):
        weighted = jnp.zeros((columns, 1), jnp.float32)
        for start in range(0, width, CHUNK):
            part = slice(start, start + CHUNK)
            value = residual[:, part] + scale * direction[:, part]
            direction[:, part] = value
            terms[:, part] = two_terms(value)
            weighted = weighted + jnp.sum(diagonal[:, part] * value * value, axis=1, keepdims=True)
        both = values.at[:2 * columns]
        over_features(terms, tokens, both)
        both = both[:columns] + both[columns:]
        seen[...] = two_terms(both)
        curvature = MIXING * jnp.sum(both * both, axis=1, keepdims=True) + (1.0 - MIXING) * weighted
        return norm_now / curvature

    def iterate(_, carry):
        scale, norm_now = carry
        step_size = step_of(scale, norm_now)
        norm_next = jnp.zeros((columns, 1), jnp.float32)
        for start in range(0, width, CHUNK):
            part = slice(start, start + CHUNK)
            both = over_tokens(seen, tokens, part)
            along = direction[:, part]
            image = MIXING * (both[:columns] + both[columns:]) + (1.0 - MIXING) * diagonal[:, part] * along
            merged[:, part] = merged[:, part] + step_size * along
            value = residual[:, part] - step_size * image
            residual[:, part] = value
            norm_next = norm_next + jnp.sum(value * value, axis=1, keepdims=True)
        return norm_next / norm_now, norm_next

    scale, norm_now = lax.fori_loop(0, ITERS - 1, iterate, (jnp.zeros((columns, 1), jnp.float32), norm_now))
    step_size = step_of(scale, norm_now)
    merged[...] = merged[...] + step_size * direction[...]
    for number, out_ref in enumerate(out_refs):
        sub_rows = out_ref.shape[1]
        if len(out_refs) > 1:
            flip = NEAR_FIRST[number]
            sub_block = (row ^ flip // 2) * 2 + (tok ^ flip % 2)
            start = pl.multiple_of(sub_block * sub_rows, LANES)
            out_ref[...] = merged[:, pl.ds(start, sub_rows)].astype(out_ref.dtype)
        else:
            out_ref[...] = merged[...].astype(out_ref.dtype)


def three_terms(value):
    high = value.astype(jnp.bfloat16).astype(jnp.float32)
    rest = value - high
    middle = rest.astype(jnp.bfloat16).astype(jnp.float32)
    return [high, middle, rest - middle]


def piece_kernel(lengths_ref, features_ref, given_ref, gains_ref, upper_ref, lower_ref, extra):
    block, slots = features_ref.shape
    half, quarter = slots // 2, slots // 4
    tok = lax.axis_index("tok")
    first = tok == 0
    lower = features_ref[:, half:half + quarter].astype(jnp.float32)
    given = given_ref[...].astype(jnp.float32)
    row = lax.broadcasted_iota(jnp.int32, (quarter, quarter), 0)
    lane = lax.broadcasted_iota(jnp.int32, (quarter, quarter), 1)
    mirror = jnp.where(row + lane == quarter - 1, 1.0, 0.0).astype(jnp.bfloat16)
    turned = jnp.dot(
        jnp.where(first, given, lower).astype(jnp.bfloat16), mirror, preferred_element_type=jnp.float32
    )
    place = lax.broadcasted_iota(jnp.int32, (block, quarter), 1) + tok * quarter
    mixed = jnp.where(place >= lengths_ref[0] - half, turned, jnp.where(first, lower, given))
    kept = features_ref[:, :half]
    cut = block - lower_ref.shape[0]
    upper_ref[:cut, :half] = kept[:cut]
    upper_ref[:cut, half:] = mixed[:cut].astype(jnp.bfloat16)
    lower_ref[:, :half] = kept[cut:]
    lower_ref[:, half:] = mixed[cut:].astype(jnp.bfloat16)
    kept = kept.astype(jnp.float32)
    extra[...] = jnp.zeros_like(extra)
    for number, value in enumerate(three_terms(jnp.sum(kept * kept, axis=0, keepdims=True))):
        extra[number:number + 1, :half] = value
    for number, value in enumerate(three_terms(jnp.sum(mixed * mixed, axis=0, keepdims=True))):
        extra[number:number + 1, half:] = value
    for number, value in enumerate(three_terms(gains_ref[...])):
        extra[3 + number:4 + number, :block] = value
    upper_ref[cut:, :] = extra[...].astype(jnp.bfloat16)


def send_kernel(weights_ref, own_ref, other_ref, turned):
    row, tok = lax.axis_index("row"), lax.axis_index("tok")
    for start in range(0, weights_ref.shape[1], LANES):
        value = weights_ref[:, start:start + LANES].astype(jnp.float32)
        turned[start:start + LANES, :] = value.T.astype(jnp.bfloat16)
    rows, held, _ = own_ref.shape
    for flip in range(rows):
        for out_ref, core in ((own_ref, tok), (other_ref, 1 - tok)):
            start = pl.multiple_of(((row ^ flip) * 2 + core) * held, held)
            out_ref[flip] = turned[pl.ds(start, held), :]


def packed_rows(lower, width):
    return -(-lower.shape[0] // (width // lower.shape[1]) // 16) * 16


def join_kernel(own_ref, given_ref, lower_ref, *refs):
    _, held, width = own_ref.shape
    rows, lanes = lower_ref.shape
    high = packed_rows(lower_ref, width)
    for flip, out_ref in enumerate(refs):
        out_ref[:held] = own_ref[flip]
        out_ref[held:2 * held] = given_ref[flip]
        if flip:
            out_ref[2 * held:] = jnp.zeros((high, width), out_ref.dtype)
            for number, start in enumerate(range(0, rows, high)):
                size = min(high, rows - start)
                out_ref[2 * held:2 * held + size, number * lanes:(number + 1) * lanes] = lower_ref[start:start + size]


def plane_kernel(lower_ref, *refs):
    out_ref = refs[-1]
    rows, lanes = lower_ref.shape
    out_ref[0] = lower_ref[...]
    for flip, found in enumerate(refs[:-1]):
        high = packed_rows(lower_ref, found.shape[1])
        base = found.shape[0] - high
        for number, start in enumerate(range(0, rows, high)):
            size = min(high, rows - start)
            out_ref[flip + 1, start:start + size] = found[base:base + size, number * lanes:(number + 1) * lanes]


def gather_kernel(*refs):
    out_ref, ordered = refs[-2:]
    row, tok = lax.axis_index("row"), lax.axis_index("tok")
    for flip, piece in zip(NEAR_FIRST, refs[:-2]):
        held = piece.shape[0]
        start = pl.multiple_of(((row ^ flip // 2) * 2 + (tok ^ flip % 2)) * held, held)
        ordered[pl.ds(start, held), :] = piece[...].astype(jnp.float32)
    for start in range(0, out_ref.shape[1], LANES):
        out_ref[:, start:start + LANES] = ordered[start:start + LANES, :].T


def body(hidden, gains, weights, lengths):
    rows = lax.axis_size("row")
    cols = lax.axis_size("col")
    toks = lax.axis_size("tok")
    slots, block = hidden.shape
    width = block * rows * cols
    models = toks * gains.shape[0]
    row_width, col_width = weights.shape[1:]
    columns = col_width // (rows * toks)
    sub_rows = row_width // toks
    features = hidden.T
    paired = toks == 2 and rows == 4
    any_space = pl.BlockSpec(memory_space=pl.ANY)
    small = pltpu.CompilerParams(vmem_limit_bytes=10 << 20)
    scalars = pl.BlockSpec(memory_space=pltpu.SMEM)
    in_vmem = pl.BlockSpec(memory_space=pltpu.VMEM)

    def swap(value, flip):
        pairs = [
            (t * rows + r, (t ^ flip % 2) * rows + (r ^ flip // 2)) for t in range(toks) for r in range(rows)
        ]
        return lax.ppermute(value, ("tok", "row"), pairs)

    if paired:
        half, quarter = slots // 2, slots // 4
        held = half + quarter
        given = swap(features[:, held:], 1)
        own, other = pl.pallas_call(
            send_kernel,
            out_shape=[jax.ShapeDtypeStruct((rows, columns, row_width), jnp.bfloat16)] * 2,
            in_specs=[in_vmem],
            out_specs=[in_vmem] * 2,
            scratch_shapes=[pltpu.VMEM((col_width, row_width), jnp.bfloat16)],
            compiler_params=small,
        )(weights[0])
        cut = block * 7 // 10
        upper, lower = pl.pallas_call(
            piece_kernel,
            out_shape=[
                jax.ShapeDtypeStruct((cut + 16, held), jnp.bfloat16),
                jax.ShapeDtypeStruct((block - cut, held), jnp.bfloat16),
            ],
            in_specs=[scalars, in_vmem, in_vmem, in_vmem],
            out_specs=[in_vmem] * 2,
            scratch_shapes=[pltpu.VMEM((16, held), jnp.float32)],
            compiler_params=small,
        )(lengths, features, given, gains)
        packed = packed_rows(lower, row_width)
        joined = pl.pallas_call(
            join_kernel,
            out_shape=[
                jax.ShapeDtypeStruct((toks * columns + (packed if flip else 0), row_width), jnp.bfloat16)
                for flip in range(rows)
            ],
            in_specs=[in_vmem] * 3,
            out_specs=[in_vmem] * rows,
            compiler_params=small,
        )(own, swap(other, 1), lower)
        line = [upper] + [
            lax.ppermute(upper, "col", [(i, (i + shift) % cols) for i in range(cols)]) for shift in range(1, cols)
        ]
        weight_pieces = [swap(value, 2 * flip) if flip else value for flip, value in enumerate(joined)]
        places = list(range(rows))
        line, weight_pieces = lax.optimization_barrier((line, weight_pieces))
        plane = pl.pallas_call(
            plane_kernel,
            out_shape=jax.ShapeDtypeStruct((rows,) + lower.shape, jnp.bfloat16),
            in_specs=[in_vmem] * rows,
            out_specs=in_vmem,
            compiler_params=small,
        )(lower, *weight_pieces[1:])
        up = [(i, (i + 1) % cols) for i in range(cols)]
        value = jnp.stack(line)
        by_near, by_far = swap(value, 2), swap(value, 4)
        middle = cut // 2
        crossed = [
            (0, 0, value), (1, 0, by_near), (2, 0, by_far),
            (3, 0, swap(by_far[:, :middle], 2)), (3, middle, swap(by_near[:, middle:], 4)),
        ]
        rounds = [plane]
        for _ in range(cols - 1):
            rounds.append(lax.ppermute(rounds[-1], "col", up))
        pieces, copies = [], []
        for flip, first, found in crossed:
            high = min(first + found.shape[1], cut) - first
            for part, arrived in enumerate((found, swap(found, 1))):
                pieces.append(arrived)
                copies.append([(i, (flip, i), part, held, first, high) for i in range(cols)])
        for back, found in enumerate(rounds):
            for part, arrived in enumerate((found, swap(found, 1))):
                pieces.append(arrived)
                copies.append([(flip, (flip, back), part, held, cut, block - cut) for flip in range(rows)])
        owners = (0, 0, -1, 1, 1, -1)
        small_inputs = []
    else:
        sent = weights[0].T.reshape(rows * toks, columns, row_width)
        own_weights = lax.all_to_all(sent, ("row", "tok"), 0, 0, tiled=True)
        own_weights = own_weights.reshape(rows, models * columns, row_width)
        weight_pieces = [own_weights.transpose(1, 0, 2).reshape(models * columns, width)]
        places = [(0, 0)]
        held = slots
        everything = lax.all_gather(features, ("row", "col"), axis=0, tiled=False)
        pieces = [lax.all_gather(everything, "tok", axis=0, tiled=True)]
        tiles = slots // LANES
        owners = tuple(m for m in range(models) for _ in range(tiles))
        copies = [[
            (m * rows * cols + b, b, m, slots, 0, block) for m in range(models) for b in range(rows * cols)
        ]]
        live = jnp.arange(slots, dtype=jnp.int32)[None, :] < lengths[:, None]
        floats = features.astype(jnp.float32)
        squares = lax.psum(jnp.sum(floats * floats, axis=0), ("row", "col"))
        every_gain = lax.all_gather(gains[0], ("row", "col"), axis=0, tiled=True)
        small_inputs = [
            live.reshape(1, -1).astype(jnp.float32),
            lax.all_gather(squares, "tok", axis=0, tiled=True)[None, :],
            lax.all_gather(every_gain, "tok", axis=0, tiled=False).T,
        ]
    slots_held = toks * held

    if paired:
        out_shape = [jax.ShapeDtypeStruct((columns, sub_rows), jnp.bfloat16)] * (rows * toks)
    else:
        out_shape = [jax.ShapeDtypeStruct((columns, width), jnp.bfloat16)]
    found = pl.pallas_call(
        functools.partial(solve_kernel, owners, models, block, copies, places),
        out_shape=out_shape,
        in_specs=[scalars] + [in_vmem] * len(small_inputs) + [any_space] * (len(pieces) + len(weight_pieces)),
        out_specs=[in_vmem] * len(out_shape),
        scratch_shapes=[
            pltpu.VMEM((width, slots_held), jnp.bfloat16),
            pltpu.VMEM((models * columns, width), jnp.bfloat16),
            pltpu.VMEM((models, width), jnp.float32),
            pltpu.VMEM((1, width), jnp.float32),
            pltpu.VMEM((columns, width), jnp.float32),
            pltpu.VMEM((columns, width), jnp.float32),
            pltpu.VMEM((columns, width), jnp.float32),
            pltpu.VMEM((2 * columns, width), jnp.bfloat16),
            pltpu.VMEM((max(models, 2) * columns, slots_held), jnp.float32),
            pltpu.VMEM((columns, slots_held), jnp.bfloat16),
            pltpu.VMEM((2 * columns, slots_held), jnp.bfloat16),
            pltpu.VMEM((models * rows * cols, 16, slots_held // models) if paired else (8, 16, LANES), jnp.bfloat16),
            pltpu.VMEM((width if paired else 8, LANES), jnp.float32),
            pltpu.SemaphoreType.DMA((3,)),
        ],
        compiler_params=pltpu.CompilerParams(vmem_limit_bytes=width * slots_held * 2 + (18 << 20)),
    )(
        lengths,
        *small_inputs,
        *pieces,
        *weight_pieces,
    )
    if paired:
        arrived = [found[0]] + [swap(x, flip) for x, flip in zip(found[1:], NEAR_FIRST[1:])]
        return pl.pallas_call(
            gather_kernel,
            out_shape=jax.ShapeDtypeStruct((sub_rows, col_width), jnp.float32),
            in_specs=[in_vmem] * len(arrived),
            out_specs=in_vmem,
            scratch_shapes=[pltpu.VMEM((col_width, sub_rows), jnp.float32)],
            compiler_params=small,
        )(*arrived)
    found = found[0].reshape(columns, rows * toks, sub_rows).transpose(1, 0, 2)
    back = lax.all_to_all(found, ("row", "tok"), 0, 0, tiled=True)
    return back.reshape(col_width, sub_rows).T.astype(jnp.float32)


def solution(mesh):
    return jax.shard_map(
        body,
        mesh=mesh,
        in_specs=(P("tok", ("row", "col")), P("tok", ("row", "col")), P("tok", "row", "col"), P()),
        out_specs=P(("row", "tok"), "col"),
        check_vma=False,
    )
```

```python
import functools

import jax
import jax.numpy as jnp
from jax import lax
from jax.experimental import pallas as pl
from jax.experimental.pallas import tpu as pltpu
from jax.sharding import PartitionSpec as P

ITERS = 4

MIXING = 0.9
EPSILON = 1e-06

LANES = 128
CHUNK = 1024
MOST_TOKENS = 1024
FLIPS = (0, 6, 2, 4, 7, 3, 5, 1)


def two_terms(value):
    high = value.astype(jnp.bfloat16).astype(jnp.float32)
    return jnp.concatenate([high, value - high], axis=0).astype(jnp.bfloat16)


def add_over_features(left, tokens, part, found):
    slots = tokens.shape[1]
    if slots <= MOST_TOKENS:
        found[...] += jnp.dot(left, tokens[part, :], preferred_element_type=jnp.float32)
        return

    def some(step, carry):
        lanes = pl.ds(pl.multiple_of(step * CHUNK, CHUNK), CHUNK)
        found[:, lanes] += jnp.dot(left, tokens[part, lanes], preferred_element_type=jnp.float32)
        return carry

    lax.fori_loop(0, slots // CHUNK, some, 0)


def over_features(left, tokens, found):
    slots = tokens.shape[1]
    if slots <= MOST_TOKENS:
        found[...] = jnp.dot(left[...], tokens[...], preferred_element_type=jnp.float32)
        return

    def some(step, carry):
        lanes = pl.ds(pl.multiple_of(step * CHUNK, CHUNK), CHUNK)
        found[:, lanes] = jnp.dot(left[...], tokens[:, lanes], preferred_element_type=jnp.float32)
        return carry

    lax.fori_loop(0, slots // CHUNK, some, 0)


def over_tokens(left, tokens, part):
    slots = tokens.shape[1]
    product = functools.partial(
        lax.dot_general, dimension_numbers=(((1,), (1,)), ((), ())), preferred_element_type=jnp.float32
    )
    if slots <= MOST_TOKENS:
        return product(left[...], tokens[part, :])

    def some(step, total):
        lanes = pl.ds(pl.multiple_of(step * CHUNK, CHUNK), CHUNK)
        return total + product(left[:, lanes], tokens[part, lanes])

    return lax.fori_loop(0, slots // CHUNK, some, jnp.zeros((left.shape[0], CHUNK), jnp.float32))


def in_pair_order(lengths_ref, width):
    half, quarter = width // 3, width // 6
    lane = lax.broadcasted_iota(jnp.int32, (1, width), 1)
    part = jnp.where(lane >= width // 2, 1, 0)
    spot = lane - part * (width // 2)
    place = spot - half + part * quarter
    late = spot >= half
    second = jnp.where(late, jnp.where(place >= lengths_ref[0] - half, 1, 0), part)
    position = jnp.where(late, jnp.where(second == 1, 2 * half - 1 - place, half + place), spot)
    length = jnp.where(second == 1, lengths_ref[1], lengths_ref[0])
    return jnp.where(position < length, 1.0, 0.0), second.astype(jnp.float32)


def solve_kernel(owners, models, block, copies, places, lengths_ref, *refs):
    riding = len(copies) > 1
    if not riding:
        live_ref, squares_ref, gains_ref, refs = refs[0], refs[1], refs[2], refs[3:]
    pieces = refs[:len(copies)]
    weight_pieces = refs[len(copies):len(copies) + len(places)]
    out_refs = refs[len(copies) + len(places):-14]
    (tokens, weights, squared, diagonal, residual, direction, merged, terms, values, outputs, seen, extras, gains_held,
     sems) = refs[-14:]
    width, slots = tokens.shape
    columns = residual.shape[0]
    blocks = width // block
    started = [[], [], []]

    def begin(source, target, kind):
        copy = pltpu.make_async_copy(source, target, sems.at[kind])
        copy.start()
        started[kind].append(copy)

    def finish(kind):
        for copy in started[kind]:
            copy.wait()

    if riding:
        row, col, tok = lax.axis_index("row"), lax.axis_index("col"), lax.axis_index("tok")
        cols = lax.axis_size("col")
    moves = []
    for piece, parts in zip(pieces, copies):
        for source, entry, part, lanes, first, held in parts:
            if riding:
                flip, back = entry
                entry = (row ^ flip) * cols + lax.rem(col - back + cols, cols)
                part = tok ^ part
            moves.append((piece, source, entry, part, lanes, first, held))
    for piece, source, entry, part, lanes, first, held in moves:
        if piece.shape[1] > held:
            begin(piece.at[source, pl.ds(held, 16)], extras.at[part * blocks + entry], 0)
    for piece, source, entry, part, lanes, first, held in moves:
        start = pl.multiple_of(entry * block + first, 16)
        lane = pl.multiple_of(part * lanes, LANES)
        begin(piece.at[source, pl.ds(0, held)], tokens.at[pl.ds(start, held), pl.ds(lane, lanes)], 1)
    for piece, place in zip(weight_pieces, places):
        if riding:
            row_width = piece.shape[1]
            lane = pl.multiple_of((row ^ place) * row_width, LANES)
            for part in range(2):
                high = pl.multiple_of((tok ^ part) * columns, columns)
                begin(
                    piece.at[pl.ds(part * columns, columns)],
                    weights.at[pl.ds(high, columns), pl.ds(lane, row_width)],
                    2,
                )
        else:
            begin(piece, weights, 2)
    finish(0)

    if riding:
        every = extras[...].astype(jnp.float32)
        sums = [jnp.sum(every[part * blocks:(part + 1) * blocks], axis=0) for part in range(models)]
        squares = jnp.concatenate([x[0:1] + x[1:2] + x[2:3] for x in sums], axis=1)
        turned = (every[:, 3] + every[:, 4] + every[:, 5]).T[:block]
        lane = lax.broadcasted_iota(jnp.int32, turned.shape, 1)
        side = lax.broadcasted_iota(jnp.int32, (block, LANES), 1)

        def hold_gains(step, carry):
            gain = [
                jnp.sum(jnp.where(lane == part * blocks + step, turned, 0.0), axis=1, keepdims=True)
                for part in range(models)
            ]
            gains_held[pl.ds(pl.multiple_of(step * block, block), block), :] = jnp.where(side == 0, gain[0], gain[1])
            return carry

        lax.fori_loop(0, blocks, hold_gains, 0)
        gains_ref = gains_held
        live, second = in_pair_order(lengths_ref, slots)
    else:
        squares, live = squares_ref[...], live_ref[...]
    inverse_rms = lax.rsqrt(squares / width + EPSILON) * live
    finish(1)

    def norm_rows(start):
        gains = gains_ref[pl.ds(start, LANES), :]
        sums = [jnp.zeros((LANES, LANES), jnp.float32) for _ in range(models)]
        for tile, owner in enumerate(owners):
            lanes = slice(tile * LANES, (tile + 1) * LANES)
            value = tokens[pl.ds(start, LANES), lanes].astype(jnp.float32)
            if owner < 0:
                gain = jnp.where(second[:, lanes] > 0, gains[:, 1:2], gains[:, 0:1])
            else:
                gain = gains[:, owner:owner + 1]
            normed = (value * inverse_rms[:, lanes] * gain).astype(jnp.bfloat16)
            tokens[pl.ds(start, LANES), lanes] = normed
            value = normed.astype(jnp.float32)
            value = value * value
            if owner < 0:
                theirs = value * second[:, lanes]
                sums[0] = sums[0] + (value - theirs)
                sums[1] = sums[1] + theirs
            else:
                sums[owner] = sums[owner] + value
        sums = [jnp.sum(part.T, axis=0, keepdims=True) for part in sums]
        for model in range(models):
            squared[model:model + 1, pl.ds(start, LANES)] = sums[model]
        diagonal[:, pl.ds(start, LANES)] = functools.reduce(jnp.add, sums)

    def norm_and_multiply(step, carry):
        start = pl.multiple_of(step * 2 * LANES, 2 * LANES)
        for half in range(2):
            norm_rows(pl.multiple_of(start + half * LANES, LANES))
        rows = pl.ds(start, 2 * LANES)
        add_over_features(weights[:, rows], tokens, rows, values.at[:models * columns])
        return carry

    finish(2)
    values[...] = jnp.zeros_like(values)

    lax.fori_loop(0, width // (2 * LANES), norm_and_multiply, 0, unroll=4 if riding else 1)

    picked = []
    for tile, owner in enumerate(owners):
        lanes = slice(tile * LANES, (tile + 1) * LANES)
        if owner < 0:
            picked.append(jnp.where(second[:, lanes] > 0, values[columns:2 * columns, lanes], values[:columns, lanes]))
        else:
            picked.append(values[owner * columns:(owner + 1) * columns, lanes])
    outputs[...] = jnp.concatenate(picked, axis=1).astype(jnp.bfloat16)

    norm_now = jnp.zeros((columns, 1), jnp.float32)
    for start in range(0, width, CHUNK):
        part = slice(start, start + CHUNK)
        weighted = jnp.zeros((columns, CHUNK), jnp.float32)
        for model in range(models):
            rows = weights[model * columns:(model + 1) * columns, part].astype(jnp.float32)
            weighted = weighted + squared[model:model + 1, part] * rows
        right = MIXING * over_tokens(outputs, tokens, part) + (1.0 - MIXING) * weighted
        residual[:, part] = right
        direction[:, part] = jnp.zeros_like(right)
        merged[:, part] = jnp.zeros_like(right)
        norm_now = norm_now + jnp.sum(right * right, axis=1, keepdims=True)

    def step_of(scale, norm_now):
        weighted = jnp.zeros((columns, 1), jnp.float32)
        for start in range(0, width, CHUNK):
            part = slice(start, start + CHUNK)
            value = residual[:, part] + scale * direction[:, part]
            direction[:, part] = value
            terms[:, part] = two_terms(value)
            weighted = weighted + jnp.sum(diagonal[:, part] * value * value, axis=1, keepdims=True)
        both = values.at[:2 * columns]
        over_features(terms, tokens, both)
        both = both[:columns] + both[columns:]
        seen[...] = two_terms(both)
        curvature = MIXING * jnp.sum(both * both, axis=1, keepdims=True) + (1.0 - MIXING) * weighted
        return norm_now / curvature

    def iterate(_, carry):
        scale, norm_now = carry
        step_size = step_of(scale, norm_now)
        norm_next = jnp.zeros((columns, 1), jnp.float32)
        for start in range(0, width, CHUNK):
            part = slice(start, start + CHUNK)
            both = over_tokens(seen, tokens, part)
            along = direction[:, part]
            image = MIXING * (both[:columns] + both[columns:]) + (1.0 - MIXING) * diagonal[:, part] * along
            merged[:, part] = merged[:, part] + step_size * along
            value = residual[:, part] - step_size * image
            residual[:, part] = value
            norm_next = norm_next + jnp.sum(value * value, axis=1, keepdims=True)
        return norm_next / norm_now, norm_next

    scale, norm_now = lax.fori_loop(0, ITERS - 1, iterate, (jnp.zeros((columns, 1), jnp.float32), norm_now))
    step_size = step_of(scale, norm_now)
    merged[...] = merged[...] + step_size * direction[...]
    for number, out_ref in enumerate(out_refs):
        sub_rows = out_ref.shape[1]
        if len(out_refs) > 1:
            flip = FLIPS[number]
            sub_block = (row ^ flip // 2) * 2 + (tok ^ flip % 2)
            start = pl.multiple_of(sub_block * sub_rows, LANES)
            out_ref[...] = merged[:, pl.ds(start, sub_rows)].astype(out_ref.dtype)
        else:
            out_ref[...] = merged[...].astype(out_ref.dtype)


def three_terms(value):
    high = value.astype(jnp.bfloat16).astype(jnp.float32)
    rest = value - high
    middle = rest.astype(jnp.bfloat16).astype(jnp.float32)
    return [high, middle, rest - middle]


def piece_kernel(lengths_ref, features_ref, given_ref, gains_ref, upper_ref, lower_ref, extra):
    block, slots = features_ref.shape
    half, quarter = slots // 2, slots // 4
    tok = lax.axis_index("tok")
    first = tok == 0
    lower = features_ref[:, half:half + quarter].astype(jnp.float32)
    given = given_ref[...].astype(jnp.float32)
    row = lax.broadcasted_iota(jnp.int32, (quarter, quarter), 0)
    lane = lax.broadcasted_iota(jnp.int32, (quarter, quarter), 1)
    mirror = jnp.where(row + lane == quarter - 1, 1.0, 0.0).astype(jnp.bfloat16)
    turned = jnp.dot(
        jnp.where(first, given, lower).astype(jnp.bfloat16), mirror, preferred_element_type=jnp.float32
    )
    place = lax.broadcasted_iota(jnp.int32, (block, quarter), 1) + tok * quarter
    mixed = jnp.where(place >= lengths_ref[0] - half, turned, jnp.where(first, lower, given))
    kept = features_ref[:, :half]
    cut = block - lower_ref.shape[0]
    upper_ref[:cut, :half] = kept[:cut]
    upper_ref[:cut, half:] = mixed[:cut].astype(jnp.bfloat16)
    lower_ref[:, :half] = kept[cut:]
    lower_ref[:, half:] = mixed[cut:].astype(jnp.bfloat16)
    kept = kept.astype(jnp.float32)
    extra[...] = jnp.zeros_like(extra)
    for number, value in enumerate(three_terms(jnp.sum(kept * kept, axis=0, keepdims=True))):
        extra[number:number + 1, :half] = value
    for number, value in enumerate(three_terms(jnp.sum(mixed * mixed, axis=0, keepdims=True))):
        extra[number:number + 1, half:] = value
    for number, value in enumerate(three_terms(gains_ref[...])):
        extra[3 + number:4 + number, :block] = value
    upper_ref[cut:, :] = extra[...].astype(jnp.bfloat16)


def send_kernel(weights_ref, own_ref, other_ref, turned):
    row, tok = lax.axis_index("row"), lax.axis_index("tok")
    for start in range(0, weights_ref.shape[1], LANES):
        value = weights_ref[:, start:start + LANES].astype(jnp.float32)
        turned[start:start + LANES, :] = value.T.astype(jnp.bfloat16)
    rows, held, _ = own_ref.shape
    for flip in range(rows):
        for out_ref, core in ((own_ref, tok), (other_ref, 1 - tok)):
            start = pl.multiple_of(((row ^ flip) * 2 + core) * held, held)
            out_ref[flip] = turned[pl.ds(start, held), :]


def packed_rows(lower, width):
    return -(-lower.shape[0] // (width // lower.shape[1]) // 16) * 16


def join_kernel(own_ref, given_ref, lower_ref, *refs):
    _, held, width = own_ref.shape
    rows, lanes = lower_ref.shape
    high = packed_rows(lower_ref, width)
    for flip, out_ref in enumerate(refs):
        out_ref[:held] = own_ref[flip]
        out_ref[held:2 * held] = given_ref[flip]
        if flip:
            out_ref[2 * held:] = jnp.zeros((high, width), out_ref.dtype)
            for number, start in enumerate(range(0, rows, high)):
                size = min(high, rows - start)
                out_ref[2 * held:2 * held + size, number * lanes:(number + 1) * lanes] = lower_ref[start:start + size]


def plane_kernel(lower_ref, *refs):
    out_ref = refs[-1]
    rows, lanes = lower_ref.shape
    out_ref[0] = lower_ref[...]
    for flip, found in enumerate(refs[:-1]):
        high = packed_rows(lower_ref, found.shape[1])
        base = found.shape[0] - high
        for number, start in enumerate(range(0, rows, high)):
            size = min(high, rows - start)
            out_ref[flip + 1, start:start + size] = found[base:base + size, number * lanes:(number + 1) * lanes]


def gather_kernel(*refs):
    out_ref, ordered = refs[-2:]
    row, tok = lax.axis_index("row"), lax.axis_index("tok")
    for flip, piece in zip(FLIPS, refs[:-2]):
        held = piece.shape[0]
        start = pl.multiple_of(((row ^ flip // 2) * 2 + (tok ^ flip % 2)) * held, held)
        ordered[pl.ds(start, held), :] = piece[...].astype(jnp.float32)
    for start in range(0, out_ref.shape[1], LANES):
        out_ref[:, start:start + LANES] = ordered[start:start + LANES, :].T


def body(hidden, gains, weights, lengths):
    rows = lax.axis_size("row")
    cols = lax.axis_size("col")
    toks = lax.axis_size("tok")
    slots, block = hidden.shape
    width = block * rows * cols
    models = toks * gains.shape[0]
    row_width, col_width = weights.shape[1:]
    columns = col_width // (rows * toks)
    sub_rows = row_width // toks
    features = hidden.T
    paired = toks == 2 and rows == 4
    any_space = pl.BlockSpec(memory_space=pl.ANY)
    small = pltpu.CompilerParams(vmem_limit_bytes=10 << 20)
    scalars = pl.BlockSpec(memory_space=pltpu.SMEM)
    in_vmem = pl.BlockSpec(memory_space=pltpu.VMEM)

    def swap(value, flip):
        pairs = [
            (t * rows + r, (t ^ flip % 2) * rows + (r ^ flip // 2)) for t in range(toks) for r in range(rows)
        ]
        return lax.ppermute(value, ("tok", "row"), pairs)

    if paired:
        half, quarter = slots // 2, slots // 4
        held = half + quarter
        given = swap(features[:, held:], 1)
        own, other = pl.pallas_call(
            send_kernel,
            out_shape=[jax.ShapeDtypeStruct((rows, columns, row_width), jnp.bfloat16)] * 2,
            in_specs=[in_vmem],
            out_specs=[in_vmem] * 2,
            scratch_shapes=[pltpu.VMEM((col_width, row_width), jnp.bfloat16)],
            compiler_params=small,
        )(weights[0])
        cut = block * 7 // 10
        upper, lower = pl.pallas_call(
            piece_kernel,
            out_shape=[
                jax.ShapeDtypeStruct((cut + 16, held), jnp.bfloat16),
                jax.ShapeDtypeStruct((block - cut, held), jnp.bfloat16),
            ],
            in_specs=[scalars, in_vmem, in_vmem, in_vmem],
            out_specs=[in_vmem] * 2,
            scratch_shapes=[pltpu.VMEM((16, held), jnp.float32)],
            compiler_params=small,
        )(lengths, features, given, gains)
        packed = packed_rows(lower, row_width)
        joined = pl.pallas_call(
            join_kernel,
            out_shape=[
                jax.ShapeDtypeStruct((toks * columns + (packed if flip else 0), row_width), jnp.bfloat16)
                for flip in range(rows)
            ],
            in_specs=[in_vmem] * 3,
            out_specs=[in_vmem] * rows,
            compiler_params=small,
        )(own, swap(other, 1), lower)
        line = [upper] + [
            lax.ppermute(upper, "col", [(i, (i + shift) % cols) for i in range(cols)]) for shift in range(1, cols)
        ]
        weight_pieces = [swap(value, 2 * flip) if flip else value for flip, value in enumerate(joined)]
        places = list(range(rows))
        line, weight_pieces = lax.optimization_barrier((line, weight_pieces))
        plane = pl.pallas_call(
            plane_kernel,
            out_shape=jax.ShapeDtypeStruct((rows,) + lower.shape, jnp.bfloat16),
            in_specs=[in_vmem] * rows,
            out_specs=in_vmem,
            compiler_params=small,
        )(lower, *weight_pieces[1:])
        up = [(i, (i + 1) % cols) for i in range(cols)]
        value = jnp.stack(line)
        by_near, by_far = swap(value, 2), swap(value, 4)
        middle = cut // 2
        crossed = [
            (0, 0, value), (1, 0, by_near), (2, 0, by_far),
            (3, 0, swap(by_far[:, :middle], 2)), (3, middle, swap(by_near[:, middle:], 4)),
        ]
        rounds = [plane]
        for _ in range(cols - 1):
            rounds.append(lax.ppermute(rounds[-1], "col", up))
        pieces, copies = [], []
        for flip, first, found in crossed:
            high = min(first + found.shape[1], cut) - first
            for part, arrived in enumerate((found, swap(found, 1))):
                pieces.append(arrived)
                copies.append([(i, (flip, i), part, held, first, high) for i in range(cols)])
        for back, found in enumerate(rounds):
            for part, arrived in enumerate((found, swap(found, 1))):
                pieces.append(arrived)
                copies.append([(flip, (flip, back), part, held, cut, block - cut) for flip in range(rows)])
        owners = (0, 0, -1, 1, 1, -1)
        small_inputs = []
    else:
        sent = weights[0].T.reshape(rows * toks, columns, row_width)
        own_weights = lax.all_to_all(sent, ("row", "tok"), 0, 0, tiled=True)
        own_weights = own_weights.reshape(rows, models * columns, row_width)
        weight_pieces = [own_weights.transpose(1, 0, 2).reshape(models * columns, width)]
        places = [(0, 0)]
        held = slots
        everything = lax.all_gather(features, ("row", "col"), axis=0, tiled=False)
        pieces = [lax.all_gather(everything, "tok", axis=0, tiled=True)]
        tiles = slots // LANES
        owners = tuple(m for m in range(models) for _ in range(tiles))
        copies = [[
            (m * rows * cols + b, b, m, slots, 0, block) for m in range(models) for b in range(rows * cols)
        ]]
        live = jnp.arange(slots, dtype=jnp.int32)[None, :] < lengths[:, None]
        floats = features.astype(jnp.float32)
        squares = lax.psum(jnp.sum(floats * floats, axis=0), ("row", "col"))
        every_gain = lax.all_gather(gains[0], ("row", "col"), axis=0, tiled=True)
        small_inputs = [
            live.reshape(1, -1).astype(jnp.float32),
            lax.all_gather(squares, "tok", axis=0, tiled=True)[None, :],
            lax.all_gather(every_gain, "tok", axis=0, tiled=False).T,
        ]
    slots_held = toks * held

    if paired:
        out_shape = [jax.ShapeDtypeStruct((columns, sub_rows), jnp.bfloat16)] * (rows * toks)
    else:
        out_shape = [jax.ShapeDtypeStruct((columns, width), jnp.bfloat16)]
    found = pl.pallas_call(
        functools.partial(solve_kernel, owners, models, block, copies, places),
        out_shape=out_shape,
        in_specs=[scalars] + [in_vmem] * len(small_inputs) + [any_space] * (len(pieces) + len(weight_pieces)),
        out_specs=[in_vmem] * len(out_shape),
        scratch_shapes=[
            pltpu.VMEM((width, slots_held), jnp.bfloat16),
            pltpu.VMEM((models * columns, width), jnp.bfloat16),
            pltpu.VMEM((models, width), jnp.float32),
            pltpu.VMEM((1, width), jnp.float32),
            pltpu.VMEM((columns, width), jnp.float32),
            pltpu.VMEM((columns, width), jnp.float32),
            pltpu.VMEM((columns, width), jnp.float32),
            pltpu.VMEM((2 * columns, width), jnp.bfloat16),
            pltpu.VMEM((max(models, 2) * columns, slots_held), jnp.float32),
            pltpu.VMEM((columns, slots_held), jnp.bfloat16),
            pltpu.VMEM((2 * columns, slots_held), jnp.bfloat16),
            pltpu.VMEM((models * rows * cols, 16, slots_held // models) if paired else (8, 16, LANES), jnp.bfloat16),
            pltpu.VMEM((width if paired else 8, LANES), jnp.float32),
            pltpu.SemaphoreType.DMA((3,)),
        ],
        compiler_params=pltpu.CompilerParams(vmem_limit_bytes=width * slots_held * 2 + (18 << 20)),
    )(
        lengths,
        *small_inputs,
        *pieces,
        *weight_pieces,
    )
    if paired:
        arrived = [found[0]] + [swap(x, flip) for x, flip in zip(found[1:], FLIPS[1:])]
        return pl.pallas_call(
            gather_kernel,
            out_shape=jax.ShapeDtypeStruct((sub_rows, col_width), jnp.float32),
            in_specs=[in_vmem] * len(arrived),
            out_specs=in_vmem,
            scratch_shapes=[pltpu.VMEM((col_width, sub_rows), jnp.float32)],
            compiler_params=small,
        )(*arrived)
    found = found[0].reshape(columns, rows * toks, sub_rows).transpose(1, 0, 2)
    back = lax.all_to_all(found, ("row", "tok"), 0, 0, tiled=True)
    return back.reshape(col_width, sub_rows).T.astype(jnp.float32)


def solution(mesh):
    return jax.shard_map(
        body,
        mesh=mesh,
        in_specs=(P("tok", ("row", "col")), P("tok", ("row", "col")), P("tok", "row", "col"), P()),
        out_specs=P(("row", "tok"), "col"),
        check_vma=False,
    )
```
